32 devices in a mesh: ctx: 8 (over y, x, core), wt: 4 (over z).
Axes of the slice: x: 2, y: 2, z: 4, core: 2. Of those that a mesh axis runs over, the one named last changes fastest.
Arguments:
- tokens: bfloat16 [2048, 576], P('ctx'), may hold values from -6 to 6
- w_query: bfloat16 [576, 576], replicated, may hold values from -0.25 to 0.25
- w_key: bfloat16 [576, 192], replicated, may hold values from -0.25 to 0.25
- w_value: bfloat16 [576, 192], replicated, may hold values from -0.25 to 0.25
- w_out: bfloat16 [576, 576], replicated, may hold values from -1.5 to 1.5
- norm_attn: bfloat16 [576], replicated, may hold values from 0.5 to 1.5
- norm_mlp: bfloat16 [576], replicated, may hold values from 0.5 to 1.5
- w_gate: bfloat16 [576, 1536], P(None, 'wt'), may hold values from -0.25 to 0.25
- w_up: bfloat16 [576, 1536], P(None, 'wt'), may hold values from -0.25 to 0.25
- w_down: bfloat16 [1536, 576], P('wt'), may hold values from -0.15625 to 0.15625
- stretch_order: int32 [1, 16], replicated, may hold values from 0 to 15, as said below
- cotangent: bfloat16 [2048, 576], P('ctx'), may hold values from -6 to 6
Outputs:
- output: bfloat16 [2048, 576], P('ctx')
- grad_tokens: float32 [2048, 576], P('ctx')
- grad_query: float32 [576, 576], replicated
- grad_key: float32 [576, 192], replicated
- grad_value: float32 [576, 192], replicated
- grad_out: float32 [576, 576], replicated
- grad_norm_attn: float32 [576], replicated
- grad_norm_mlp: float32 [576], replicated
- grad_gate: float32 [576, 1536], P(None, 'wt')
- grad_up: float32 [576, 1536], P(None, 'wt')
- grad_down: float32 [1536, 576], P('wt')
The draws below stay inside these ranges and needn't reach their ends.
Inputs may be any that keep to these rules, and one draw needn't show every extreme that they name: `stretch_order`: for every sequence, slots 2 j and 2 j + 1 hold stretches c and 15 - c with c < 8; every stretch stands once.
All inputs are finite; a program needn't handle non-finite values.
Results may differ from the reference program's by a relative error of at most 0.019.
Values may be sent and summed in bfloat16 or wider, within the bound.
No kernel may reach another device: no remote copies, remote signals or barrier semaphores. Data moves between devices by JAX's collectives and lax.ppermute only.
A program may use at most 128 MiB of HBM per device.

```python
import jax
import jax.numpy as jnp
from jax import lax

D = 576
Q_HEADS = 9
KV_HEADS = 3
HEAD = 64
FF = 1536
TOK_DEV = 256
TOKENS = 2048
SEQ_LEN = 2048
SEQS = 1
SLOTS = 16
STRETCH = 128
KVW = 192


def draw_stretch_order(key, part):
    key = jax.random.fold_in(key, 11)
    seq_keys = jax.random.split(key, SEQS)
    lowest_stretch = jax.vmap(lambda single_key: jax.random.permutation(single_key, SLOTS // 2))(seq_keys).astype(jnp.int32)
    return jnp.stack([lowest_stretch, SLOTS - 1 - lowest_stretch], axis=-1).reshape(SEQS, SLOTS)


def level_of(rng, extent, shards, low, largest):
    factor_of = 1.0
    for axis_at, parts in shards:
        draws = jax.random.uniform(jax.random.fold_in(jax.random.fold_in(rng, 6), axis_at), (parts,), jnp.float32, low / len(shards), largest / len(shards))
        factor_of = factor_of * jnp.repeat(jnp.exp(draws), extent[axis_at] // parts).reshape((-1,) + (1,) * (len(extent) - 1 - axis_at))
    return factor_of


def normal_values(own_key, shape, deviation, bound, cuts=(), kind=jnp.bfloat16):
    entries = jax.random.normal(own_key, shape, jnp.float32) * deviation
    if len(cuts) > 0:
        entries = level_of(own_key, shape, cuts, -0.22, 0.18) * entries
    return jnp.clip(entries, min=-bound, max=bound).astype(kind)


def setup_inputs(seed: int = 0) -> dict:
    keys = jax.random.split(jax.random.key(seed), 13)
    return {
        "tokens": normal_values(keys[0], (TOKENS, D), 1.0, 6.0, ((0, 8),)),
        "w_query": normal_values(keys[1], (D, D), D ** -0.5, 0.25),
        "w_key": normal_values(keys[2], (D, KVW), D ** -0.5, 0.25),
        "w_value": normal_values(keys[3], (D, KVW), D ** -0.5, 0.25),
        "w_out": normal_values(keys[4], (D, D), (max(1, D // 32)) ** -0.5, 1.5),
        "norm_attn": jnp.clip(1.0 + 0.1 * jax.random.normal(keys[5], (D,), jnp.float32), 0.5, 1.5).astype(jnp.bfloat16),
        "norm_mlp": jnp.clip(1.0 + 0.1 * jax.random.normal(keys[6], (D,), jnp.float32), 0.5, 1.5).astype(jnp.bfloat16),
        "w_gate": normal_values(keys[7], (D, FF), D ** -0.5, 0.25, ((1, 4),)),
        "w_up": normal_values(keys[8], (D, FF), D ** -0.5, 0.25, ((1, 4),)),
        "w_down": normal_values(keys[9], (FF, D), FF ** -0.5, 0.15625, ((0, 4),)),
        "stretch_order": draw_stretch_order(jax.random.fold_in(keys[12], 71), 0),
        "cotangent": normal_values(keys[11], (TOKENS, D), 1.0, 6.0, ((0, 8),)),
    }


EPSILON = 1e-05
THETA = 100000.0

@jax.custom_vjp
def low(v):
    return lax.optimization_barrier(v.astype(jnp.bfloat16)).astype(jnp.float32)

@jax.custom_vjp
def low_back(v):
    return v

def low_keep(v):
    return (low(v), None)

def low_pass(kept, grad):
    return (grad,)

def back_keep(v):
    return (v, None)

def back_low(kept, grad):
    return (low(grad),)
low.defvjp(low_keep, low_pass)
low_back.defvjp(back_keep, back_low)

def dense(left, right):
    return jnp.dot(left, right, precision=lax.Precision.HIGHEST, preferred_element_type=jnp.float32)

def rms_norm(values, gain):
    return values * lax.rsqrt(lax.optimization_barrier(jnp.mean(values * values, axis=-1, keepdims=True)) + EPSILON) * gain

def rotate(values, places):
    half = values.shape[-1] // 2
    rates = THETA ** (-jnp.arange(half, dtype=jnp.float32) / half)
    angle = places.astype(jnp.float32)[:, None] * rates[None, :]
    cosine = jnp.cos(angle)[:, None, :]
    sine = jnp.sin(angle)[:, None, :]
    first = values[..., :half]
    second = values[..., half:]
    return jnp.concatenate([first * cosine - second * sine, second * cosine + first * sine], axis=-1)

def attend_one(items):
    query, key, value = items
    length = query.shape[0]
    group = query.shape[1] // key.shape[1]
    key_rep = jnp.repeat(key, group, axis=1)
    value_rep = jnp.repeat(value, group, axis=1)
    block = min(512, length)
    scale = query.shape[2] ** (-0.5)
    places = jnp.arange(length, dtype=jnp.int32)

    def one_block(part):
        query_rows, first = part
        score = jnp.einsum('qhd,khd->hqk', query_rows, key_rep, precision=lax.Precision.HIGHEST) * scale
        score = low_back(score)
        seen = places[None, :] <= (first + jnp.arange(block, dtype=jnp.int32))[:, None]
        score = jnp.where(seen[None], score, -1e+30)
        weight = low(jax.nn.softmax(score, axis=-1))
        return jnp.einsum('hqk,khd->qhd', weight, value_rep, precision=lax.Precision.HIGHEST)
    blocks = query.reshape(length // block, block, query.shape[1], query.shape[2])
    firsts = jnp.arange(length // block, dtype=jnp.int32) * block
    result = lax.map(jax.checkpoint(one_block), (blocks, firsts))
    return result.reshape(length, query.shape[1], query.shape[2])

def layer(natural, w_query, w_key, w_value, w_out, norm_attn, norm_mlp, w_gate, w_up, w_down):
    seq_count, length, width = natural.shape
    places = jnp.arange(length, dtype=jnp.int32)
    normed = low(rms_norm(natural, norm_attn))
    query_pre = low_back(dense(normed, w_query))
    key_pre = low_back(dense(normed, w_key))
    value_flat = low(low_back(dense(normed, w_value)))
    query = low(rotate(query_pre.reshape(seq_count, length, Q_HEADS, HEAD), places))
    key = low(rotate(key_pre.reshape(seq_count, length, KV_HEADS, HEAD), places))
    value = value_flat.reshape(seq_count, length, KV_HEADS, HEAD)
    attended = lax.map(attend_one, (query, key, value)).reshape(seq_count, length, width)
    attended = low(low_back(attended))
    mixed = natural + low_back(dense(attended, w_out))
    normed_mlp = low(rms_norm(mixed, norm_mlp))
    gate = low_back(dense(normed_mlp, w_gate))
    up_proj = low_back(dense(normed_mlp, w_up))
    hidden = low(jax.nn.silu(gate) * up_proj)
    return mixed + dense(hidden, w_down)

def reference(tokens, w_query, w_key, w_value, w_out, norm_attn, norm_mlp, w_gate, w_up, w_down, stretch_order, cotangent):
    row_ids = jnp.arange(TOKENS, dtype=jnp.int32)
    device = row_ids // TOK_DEV
    inner = row_ids % TOK_DEV
    sequence = inner // (2 * STRETCH)
    slot_bit = inner // STRETCH % 2
    stretch_ids = stretch_order[sequence, 2 * device + slot_bit]
    place = sequence * SEQ_LEN + stretch_ids * STRETCH + inner % STRETCH
    order = jnp.argsort(place).astype(jnp.int32)
    inverse = jnp.argsort(order).astype(jnp.int32)
    natural = tokens.astype(jnp.float32)[order].reshape(SEQS, SEQ_LEN, D)
    params = tuple((weight.astype(jnp.float32) for weight in (w_query, w_key, w_value, w_out, norm_attn, norm_mlp, w_gate, w_up, w_down)))
    result, pullback = jax.vjp(layer, natural, *params)
    grads = pullback(cotangent.astype(jnp.float32)[order].reshape(SEQS, SEQ_LEN, D))
    output = result.reshape(TOKENS, D)[inverse].astype(jnp.bfloat16)
    grad_tokens = grads[0].reshape(TOKENS, D)[inverse]
    return (output, grad_tokens, grads[1], grads[2], grads[3], grads[4], grads[5], grads[6], grads[7], grads[8], grads[9])
```

```python
import functools

import jax
import jax.numpy as jnp
from jax import lax
from jax.experimental import pallas as pl
from jax.experimental.pallas import tpu as pltpu
from jax.sharding import PartitionSpec as P

Q_HEADS = 9
KV_HEADS = 3
GROUP = 3
HEAD = 64
PAIR = 2 * HEAD
EPSILON = 1e-05
THETA = 100000.0
NEGATIVE = -1e30
BF = jnp.bfloat16
F32 = jnp.float32
MIB = 1 << 20

VM = pl.BlockSpec(memory_space=pltpu.VMEM)
SM = pl.BlockSpec(memory_space=pltpu.SMEM)
HB = pl.BlockSpec(memory_space=pl.ANY)


def dot(left, right):
    return jnp.dot(left, right, preferred_element_type=F32)


def dot_nt(left, right):
    return lax.dot_general(left, right, (((1,), (1,)), ((), ())), preferred_element_type=F32)


def dot_tn(left, right):
    return lax.dot_general(left, right, (((0,), (0,)), ((), ())), preferred_element_type=F32)


def swap_lanes(x):
    half = x.shape[-1] // 2
    return jnp.concatenate([x[:, half:], x[:, :half]], axis=1)


def call(body, out_shape, in_specs, vmem, scratch=(), out_specs=None, flops=0, **kw):
    return pl.pallas_call(
        body,
        out_shape=out_shape,
        in_specs=in_specs,
        out_specs=out_specs if out_specs is not None else jax.tree.map(lambda _: VM, out_shape),
        scratch_shapes=list(scratch),
        compiler_params=pltpu.CompilerParams(vmem_limit_bytes=vmem * MIB),
        cost_estimate=pl.CostEstimate(flops=flops, bytes_accessed=4 * MIB, transcendentals=0),
        **kw,
    )


def shape(dims, dtype):
    return jax.ShapeDtypeStruct(dims, dtype)


def key_kernel(tok, gain, wk, wv, cos, sin, normed_out, kv_out):
    x = tok[...].astype(F32)
    r = lax.rsqrt(jnp.mean(x * x, axis=-1, keepdims=True) + EPSILON)
    normed = (x * r * gain[...].astype(F32)).astype(BF)
    normed_out[...] = normed
    k = dot(normed, wk[...])
    v = dot(normed, wv[...])
    for g in range(KV_HEADS):
        kg = k[:, g * HEAD : (g + 1) * HEAD]
        kr = kg * cos[...] + swap_lanes(kg) * sin[...]
        vg = v[:, g * HEAD : (g + 1) * HEAD]
        kv_out[:, g * PAIR : (g + 1) * PAIR] = jnp.concatenate([kr, vg], axis=1).astype(BF)


def query_kernel(normed, wq, cos, sin, q_out):
    rows = normed.shape[0]
    stretch = rows // 2
    q = dot(normed[...], wq[...])
    zero = jnp.zeros((rows, HEAD), F32)
    for h in range(Q_HEADS):
        qh = q[:, h * HEAD : (h + 1) * HEAD]
        qr = (qh * cos[...] + swap_lanes(qh) * sin[...]) * HEAD**-0.5
        wide = jnp.concatenate([qr, zero], axis=1).astype(BF)
        g, hh = h // GROUP, h % GROUP
        for sel in range(2):
            at = (sel * GROUP + hh) * stretch
            q_out[g, at : at + stretch, :] = wide[sel * stretch : (sel + 1) * stretch]


def parts_of(n):
    low_group = min(n, 8)
    unit_group = max(d for d in range(1, 14) if (n + 1) % d == 0)
    return low_group, n // low_group, unit_group, (n + 1) // unit_group


def loop(count, body):
    if count == 1:
        body(0)
    else:
        lax.fori_loop(0, count, lambda i, c: (body(i), c)[1], 0)


def unit(u, c, n):
    is_low = u <= c
    sel = jnp.where(is_low, 0, 1)
    stretch_id = jnp.where(is_low, u, n - 1 + u - c)
    diagonal = jnp.logical_or(u == c, u == n)
    return is_low, sel, stretch_id, diagonal


def seen_mask(stretch, diagonal):
    keys = lax.broadcasted_iota(jnp.int32, (stretch, GROUP * stretch), 0)
    cols = lax.broadcasted_iota(jnp.int32, (stretch, GROUP * stretch), 1)
    queries = lax.bitwise_and(cols, stretch - 1)
    return jnp.logical_or(keys <= queries, jnp.logical_not(diagonal))


def forward_kernel(n, wt, *refs):
    evens = refs[: n // 2]
    (meta, order, odds, q_ref, tok, cot, w_out, gain, w_gate, w_up, w_down) = refs[n // 2 : n // 2 + 11]
    outs = refs[n // 2 + 11 :]
    (kv_all, att_t, att_low_out, lse_out, mixed_out, n2_out, hid_out, gl_out, ul_out, po_out) = outs[:10]
    pin_outs = outs[10 : 10 + wt]
    kvn, m_s, l_s, o_s, pin_s, sems, out_sem = outs[10 + wt :]
    rows = tok.shape[0]
    stretch = rows // 2
    wide = GROUP * stretch
    me = meta[0]
    copies = []
    for k in range(n):
        low = order[0, 2 * lax.bitwise_xor(me, k)]
        src = evens[k // 2] if k % 2 == 0 else odds.at[k // 2]
        for half in range(2):
            to = low if half == 0 else 2 * n - 1 - low
            copies.append(
                pltpu.make_async_copy(
                    src.at[half * stretch : (half + 1) * stretch],
                    kvn.at[pl.ds(pl.multiple_of(to * stretch, stretch), stretch)],
                    sems.at[2 * k + half],
                )
            )
    for copy in copies:
        copy.start()
    for copy in copies:
        copy.wait()
    keep = pltpu.make_async_copy(kvn, kv_all, out_sem)
    keep.start()
    c = order[0, 2 * me]
    low_group, low_steps, unit_group, unit_steps = parts_of(n)

    for g in range(KV_HEADS):
        lanes = slice(g * PAIR, (g + 1) * PAIR)
        for sel in range(2):
            m_s[2 * g + sel] = jnp.full((1, wide), NEGATIVE, F32)
            l_s[2 * g + sel] = jnp.zeros((1, wide), F32)
            o_s[2 * g + sel] = jnp.zeros((PAIR, wide), F32)

        def low_step(i, g=g, lanes=lanes):
            size = low_group * stretch
            keys = kvn[pl.ds(i * size, size), lanes]
            s = dot_nt(keys, q_ref[g, wide : 2 * wide, :])
            at = 2 * g + 1
            top = jnp.maximum(m_s[at], jnp.max(s, axis=0, keepdims=True))
            fade = jnp.exp(m_s[at] - top)
            p = jnp.exp(s - top)
            l_s[at] = l_s[at] * fade + jnp.sum(p, axis=0, keepdims=True)
            o_s[at] = o_s[at] * fade + dot_tn(keys, p.astype(BF))
            m_s[at] = top

        loop(low_steps, low_step)

        def unit_step(i, g=g, lanes=lanes):
            scores = []
            tops = [m_s[2 * g], m_s[2 * g + 1]]
            for j in range(unit_group):
                u = i * unit_group + j
                is_low, sel, st, diagonal = unit(u, c, n)
                keys = kvn[pl.ds(pl.multiple_of(st * stretch, stretch), stretch), lanes]
                q = q_ref[g, pl.ds(pl.multiple_of(sel * wide, wide), wide), :]
                s = jnp.where(seen_mask(stretch, diagonal), dot_nt(keys, q), NEGATIVE)
                peak = jnp.max(s, axis=0, keepdims=True)
                tops[0] = jnp.where(is_low, jnp.maximum(tops[0], peak), tops[0])
                tops[1] = jnp.where(is_low, tops[1], jnp.maximum(tops[1], peak))
                scores.append((s, keys, is_low, sel))
            sums = []
            for sel in range(2):
                at = 2 * g + sel
                fade = jnp.exp(m_s[at] - tops[sel])
                sums.append(l_s[at] * fade)
                o_s[at] = o_s[at] * fade
                m_s[at] = tops[sel]
            for s, keys, is_low, sel in scores:
                p = jnp.exp(s - jnp.where(is_low, tops[0], tops[1]))
                part = jnp.sum(p, axis=0, keepdims=True)
                sums[0] = sums[0] + jnp.where(is_low, part, 0.0)
                sums[1] = sums[1] + jnp.where(is_low, 0.0, part)
                o_s[2 * g + sel] += dot_tn(keys, p.astype(BF))
            for sel in range(2):
                l_s[2 * g + sel] = sums[sel]

        loop(unit_steps, unit_step)
        for sel in range(2):
            at = 2 * g + sel
            total = l_s[at]
            lse_out[at : at + 1, :] = m_s[at] + jnp.log(total)
            result = o_s[at][HEAD:, :] / total
            for hh in range(GROUP):
                h = g * GROUP + hh
                att_t[h * HEAD : (h + 1) * HEAD, sel * stretch : (sel + 1) * stretch] = result[
                    :, hh * stretch : (hh + 1) * stretch
                ]
    att_low = att_t[...].T.astype(BF)
    att_low_out[...] = att_low
    mixed = tok[...].astype(F32) + dot(att_low, w_out[...])
    mixed_out[...] = mixed
    r = lax.rsqrt(jnp.mean(mixed * mixed, axis=-1, keepdims=True) + EPSILON)
    n2 = (mixed * r * gain[...].astype(F32)).astype(BF)
    n2_out[...] = n2
    gate = dot(n2, w_gate[...])
    up = dot(n2, w_up[...])
    sig = 1.0 / (1.0 + jnp.exp(-gate))
    silu = gate * sig
    hidden = (silu * up).astype(BF)
    hid_out[...] = hidden
    grad_hidden = dot_nt(cot[...], w_down[...])
    gl = (grad_hidden * up * (sig * (1.0 + gate * (1.0 - sig)))).astype(BF)
    ul = (grad_hidden * silu).astype(BF)
    gl_out[...] = gl
    ul_out[...] = ul
    pin_s[...] = dot_nt(gl, w_gate[...]) + dot_nt(ul, w_up[...])
    piece = rows // wt
    for k in range(wt):
        at = pl.multiple_of(lax.bitwise_xor(meta[1], k) * piece, piece)
        pin_outs[k][...] = pin_s[pl.ds(at, piece), :].astype(BF)
    po_out[...] = dot(hidden, w_down[...]).astype(BF)
    keep.wait()


def put_blocks(n, me, scratch, even, odd):
    size = scratch.shape[0] // n
    if n > 8:
        even[...] = scratch[...].astype(BF)
        odd[...] = jnp.zeros(odd.shape, BF)
        return
    for k in range(n):
        at = pl.multiple_of(lax.bitwise_xor(me, k) * size, size)
        to = even if k % 2 == 0 else odd
        to[k // 2] = scratch[pl.ds(at, size), :].astype(BF)


def mlp_grad_kernel(n, meta, n2, gl, ul, hidden, cot, even, odd, scratch):
    width = gl.shape[1]
    scratch[:, :width] = dot_tn(n2[...], gl[...])
    scratch[:, width : 2 * width] = dot_tn(n2[...], ul[...])
    scratch[:, 2 * width :] = dot_tn(cot[...], hidden[...])
    put_blocks(n, meta[0], scratch, even, odd)


def query_grad_kernel(n, meta, normed, dq_t, att_low, branch, wq, gn_out, even, odd, scratch):
    width = normed.shape[1]
    dq = dq_t[...].T.astype(BF)
    scratch[:, :width] = dot_tn(normed[...], dq)
    scratch[:, width:] = dot_tn(att_low[...], branch[...])
    gn_out[...] = dot_nt(dq, wq[...])
    put_blocks(n, meta[0], scratch, even, odd)


def key_grad_kernel(n, count, meta, *refs):
    kv_parts = refs[:count]
    (normed, gnq, wk, wv, cos, sin, tok, gain, gm, gnorm_mlp) = refs[count : count + 10]
    gt_out, even, odd, scratch, norm_s = refs[count + 10 :]
    total = kv_parts[0][...].astype(F32)
    for part in kv_parts[1:]:
        total = total + part[...].astype(F32)
    dk, dv = [], []
    for g in range(KV_HEADS):
        k = total[:, g * PAIR : g * PAIR + HEAD]
        dk.append(k * cos[...] - swap_lanes(k) * sin[...])
        dv.append(total[:, g * PAIR + HEAD : (g + 1) * PAIR])
    dk = jnp.concatenate(dk, axis=1).astype(BF)
    dv = jnp.concatenate(dv, axis=1).astype(BF)
    both = jnp.concatenate([dk, dv], axis=1)
    gn = gnq[...] + dot_nt(dk, wk[...]) + dot_nt(dv, wv[...])
    x = tok[...].astype(F32)
    r = lax.rsqrt(jnp.mean(x * x, axis=-1, keepdims=True) + EPSILON)
    xn = x * r
    e = gn * gain[...].astype(F32)
    gt_out[...] = gm[...] + r * (e - xn * jnp.mean(e * xn, axis=-1, keepdims=True))
    scratch[...] = dot_tn(normed[...], both)
    width = normed.shape[1]
    norm_s[...] = jnp.zeros(norm_s.shape, F32)
    norm_s[0:1, :width] = jnp.sum(gn * xn, axis=0, keepdims=True)
    norm_s[1:2, :width] = gnorm_mlp[...]
    if n > 8:
        even[...] = scratch[...].astype(BF)
        odd[...] = norm_s[...].astype(BF)
        return
    size = scratch.shape[0] // n
    for k in range(n):
        who = lax.bitwise_xor(meta[0], k)
        to = even if k % 2 == 0 else odd
        to[k // 2, :size, :] = scratch[pl.ds(pl.multiple_of(who * size, size), size), :].astype(BF)
        cut = norm_s[:, pl.ds(pl.multiple_of(who * 128, 128), 128)]
        tail = jnp.concatenate([cut, jnp.zeros((8, scratch.shape[1] - 128), F32)], axis=1)
        to[k // 2, size:, :] = tail.astype(BF)


def join_kernel(n, splits, turned, norms, meta, *refs):
    evens = refs[: n // 2]
    odds = refs[n // 2]
    outs = refs[n // 2 + 1 :]
    scratch = outs[-2] if norms else outs[-1]
    size = scratch.shape[0] // n
    if norms:
        norm_s = outs[-1]
        norm_s[...] = jnp.zeros(norm_s.shape, F32)
    for k in range(n):
        who = lax.bitwise_xor(meta[0], k)
        block = evens[k // 2][...] if k % 2 == 0 else odds[k // 2]
        block = block.astype(F32)
        scratch[pl.ds(pl.multiple_of(who * size, size), size), :] = block[:size]
        if norms:
            norm_s[:, pl.ds(pl.multiple_of(who * 128, 128), 128)] = block[size:, :128]
    at = 0
    for i, width in enumerate(splits):
        part = scratch[:, at : at + width]
        outs[i][...] = part.T if i in turned else part
        at += width
    if norms:
        for i in range(2):
            outs[len(splits) + i][...] = norm_s[i : i + 1, : scratch.shape[0]]


def backward_kernel(n, wt, *refs):
    quarters = refs[:wt]
    (meta, order, mixed, cot, gain, w_out, att_t, lse, kv, q_ref, cos_t, sin_t) = refs[wt : wt + 12]
    gm_out, branch_out, gnorm_out, dq_out, even, odd, gn_s, do_s, dl_s, dkv, dq_s = refs[wt + 12 :]
    rows = mixed.shape[0]
    stretch = rows // 2
    wide = GROUP * stretch
    me = meta[0]
    c = order[0, 2 * me]
    g = pl.program_id(0)
    low_group, low_steps, unit_group, unit_steps = parts_of(n)

    @pl.when(g == 0)
    def _():
        piece = rows // wt
        for k in range(wt):
            at = pl.multiple_of(lax.bitwise_xor(meta[1], k) * piece, piece)
            gn_s[pl.ds(at, piece), :] = quarters[k][...].astype(F32)
        x = mixed[...]
        gn = gn_s[...]
        r = lax.rsqrt(jnp.mean(x * x, axis=-1, keepdims=True) + EPSILON)
        xn = x * r
        e = gn * gain[...].astype(F32)
        gm = cot[...].astype(F32) + r * (e - xn * jnp.mean(e * xn, axis=-1, keepdims=True))
        gm_out[...] = gm
        gnorm_out[...] = jnp.sum(gn * xn, axis=0, keepdims=True)
        branch = gm.astype(BF)
        branch_out[...] = branch
        ga = dot_nt(branch, w_out[...]).astype(BF).astype(F32)
        prod = ga.T * att_t[...]
        zero = jnp.zeros((rows, HEAD), F32)
        for h in range(Q_HEADS):
            gg, hh = h // GROUP, h % GROUP
            delta = jnp.sum(prod[h * HEAD : (h + 1) * HEAD, :], axis=0, keepdims=True)
            do = jnp.concatenate([zero, ga[:, h * HEAD : (h + 1) * HEAD]], axis=1).astype(BF)
            for sel in range(2):
                at = (sel * GROUP + hh) * stretch
                half = slice(sel * stretch, (sel + 1) * stretch)
                dl_s[2 * gg + sel, :, hh * stretch : (hh + 1) * stretch] = delta[:, half]
                do_s[gg, at : at + stretch, :] = do[half]

    dkv[n * stretch :, :] = jnp.zeros((n * stretch, PAIR), F32)
    dq_s[...] = jnp.zeros(dq_s.shape, F32)

    def low_step(i):
        size = low_group * stretch
        at = pl.multiple_of(i * size, size)
        keys = kv[pl.ds(at, size), :]
        q = q_ref[0, wide : 2 * wide, :]
        do = do_s[g, wide : 2 * wide, :]
        p = jnp.exp(dot_nt(keys, q) - lse[2 * g + 1])
        ds = (p * (dot_nt(keys, do) - dl_s[2 * g + 1])).astype(BF)
        dkv[pl.ds(at, size), :] = dot(ds, q) + dot(p.astype(BF), do)
        dq_s[1] += dot_tn(keys, ds)

    loop(low_steps, low_step)

    def unit_step(i):
        for j in range(unit_group):
            u = i * unit_group + j
            _, sel, st, diagonal = unit(u, c, n)
            at = pl.ds(pl.multiple_of(st * stretch, stretch), stretch)
            keys = kv[at, :]
            span = pl.ds(pl.multiple_of(sel * wide, wide), wide)
            q = q_ref[0, span, :]
            do = do_s[g, span, :]
            p = jnp.exp(dot_nt(keys, q) - lse[2 * g + sel])
            p = jnp.where(seen_mask(stretch, diagonal), p, 0.0)
            ds = (p * (dot_nt(keys, do) - dl_s[2 * g + sel])).astype(BF)
            dkv[at, :] += dot(ds, q) + dot(p.astype(BF), do)
            dq_s[sel] += dot_tn(keys, ds)

    loop(unit_steps, unit_step)
    for k in range(n):
        low = order[0, 2 * lax.bitwise_xor(me, k)]
        to = even if k % 2 == 0 else odd
        for half in range(2):
            st = low if half == 0 else 2 * n - 1 - low
            part = dkv[pl.ds(pl.multiple_of(st * stretch, stretch), stretch), :]
            to[k // 2, half * stretch : (half + 1) * stretch, :] = part.astype(BF)
    for sel in range(2):
        half = slice(sel * stretch, (sel + 1) * stretch)
        for hh in range(GROUP):
            x = dq_s[sel, :HEAD, hh * stretch : (hh + 1) * stretch] * HEAD**-0.5
            turned = jnp.concatenate([x[HEAD // 2 :], x[: HEAD // 2]], axis=0)
            dq_out[hh * HEAD : (hh + 1) * HEAD, half] = x * cos_t[:, half] - turned * sin_t[:, half]


def hop(x, axis, size, k):
    return lax.ppermute(x, axis, [(i, i ^ k) for i in range(size)])


def gather_blocks(x, axis, size):
    evens = [x] + [hop(x, axis, size, k) for k in range(2, size, 2)]
    odds = hop(jnp.stack(evens), axis, size, 1)
    return evens, odds


def scatter_terms(even, odd, axis, size):
    got = hop(odd, axis, size, 1).astype(F32)
    terms = []
    for i in range(size // 2):
        pair = even[i].astype(F32) + got[i]
        terms.append(pair if i == 0 else hop(pair.astype(BF), axis, size, 2 * i))
    return terms


def summed(terms):
    total = terms[0].astype(F32)
    for term in terms[1:]:
        total = total + term.astype(F32)
    return total


def reduce_blocks(even, odd, axis, size):
    if size > 8:
        return lax.psum((even, odd), axis)
    return gather_blocks(summed(scatter_terms(even, odd, axis, size)).astype(BF), axis, size)


def local(
    n,
    wt,
    tokens,
    w_query,
    w_key,
    w_value,
    w_out,
    norm_attn,
    norm_mlp,
    w_gate,
    w_up,
    w_down,
    stretch_order,
    cotangent,
):
    rows, width = tokens.shape
    stretch = rows // 2
    wide = GROUP * stretch
    kv_width = KV_HEADS * PAIR
    hidden_width = w_gate.shape[1]
    me = lax.axis_index("ctx")
    lane = lax.axis_index("wt")
    meta = jnp.stack([me, lane]).astype(jnp.int32)
    gain_attn = norm_attn.reshape(1, width)
    gain_mlp = norm_mlp.reshape(1, width)
    big = 30 if n <= 8 else 60

    pair = lax.dynamic_slice_in_dim(stretch_order[0], 2 * me, 2, 0)
    places = (pair[:, None] * stretch + jnp.arange(stretch, dtype=jnp.int32)[None, :]).reshape(rows)
    half = HEAD // 2
    rates = THETA ** (-jnp.arange(half, dtype=F32) / half)
    angle = places.astype(F32)[:, None] * rates[None, :]
    cosine, sine = jnp.cos(angle), jnp.sin(angle)
    cos = jnp.concatenate([cosine, cosine], axis=1)
    sin = jnp.concatenate([-sine, sine], axis=1)
    cos_t, sin_t = cos.T, sin.T

    normed, kv = call(
        key_kernel, (shape((rows, width), BF), shape((rows, kv_width), BF)), [VM] * 6, 16
    )(tokens, gain_attn, w_key, w_value, cos, sin)
    evens, odds = gather_blocks(kv, "ctx", n)
    q = call(query_kernel, shape((KV_HEADS, 2 * wide, PAIR), BF), [VM] * 4, 16)(
        normed, w_query, cos, sin
    )

    piece = rows // wt
    forward = call(
        functools.partial(forward_kernel, n, wt),
        (
            shape((n * rows, kv_width), BF),
            shape((width, rows), F32),
            shape((rows, width), BF),
            shape((2 * KV_HEADS, wide), F32),
            shape((rows, width), F32),
            shape((rows, width), BF),
            shape((rows, hidden_width), BF),
            shape((rows, hidden_width), BF),
            shape((rows, hidden_width), BF),
            shape((rows, width), BF),
        )
        + (shape((piece, width), BF),) * wt,
        [HB] * (n // 2) + [SM, SM, HB] + [VM] * 8,
        big,
        scratch=[
            pltpu.VMEM((n * rows, kv_width), BF),
            pltpu.VMEM((2 * KV_HEADS, 1, wide), F32),
            pltpu.VMEM((2 * KV_HEADS, 1, wide), F32),
            pltpu.VMEM((2 * KV_HEADS, PAIR, wide), F32),
            pltpu.VMEM((rows, width), F32),
            pltpu.SemaphoreType.DMA((2 * n,)),
            pltpu.SemaphoreType.DMA,
        ],
        out_specs=(HB,) + (VM,) * (9 + wt),
    )(*evens, meta, stretch_order, odds, q, tokens, cotangent, w_out, gain_mlp, w_gate, w_up, w_down)
    kv_all, att_t, att_low, lse, mixed, n2, hidden, gl, ul, part_out = forward[:10]
    part_in = forward[10:]

    terms = [part_in[0]] + [hop(part_in[k], "wt", wt, k) for k in range(1, wt)]
    quarter = summed(terms).astype(BF)
    quarters = [quarter] + [hop(quarter, "wt", wt, k) for k in range(1, wt)]

    mlp_total = lax.psum(part_out, "wt").astype(F32)
    output = (mixed + mlp_total).astype(BF)

    def block_shapes(columns, extra=0):
        if n > 8:
            return shape((width, columns), BF), shape((8, 128 * n), BF)
        size = width // n
        one = shape((n // 2, size + extra, columns), BF)
        return one, one

    def join(blocks, columns, splits, turned=(), norms=False):
        evens, odds = blocks
        if n > 8:
            cuts = [sum(splits[:i]) for i in range(len(splits) + 1)]
            parts = [evens[:, a:b].astype(F32) for a, b in zip(cuts, cuts[1:])]
            parts = [part.T if i in turned else part for i, part in enumerate(parts)]
            return parts + [odds[i : i + 1, :width].astype(F32) for i in range(2 * norms)]
        outs = tuple(
            shape((w, width) if i in turned else (width, w), F32) for i, w in enumerate(splits)
        )
        scratch = [pltpu.VMEM((width, columns), F32)]
        if norms:
            outs = outs + (shape((1, width), F32),) * 2
            scratch.append(pltpu.VMEM((8, 128 * n), F32))
        return call(
            functools.partial(join_kernel, n, splits, turned, norms),
            outs,
            [SM] + [VM] * (n // 2 + 1),
            24,
            scratch=scratch,
        )(meta, *evens, odds)

    mlp_columns = 3 * hidden_width
    even, odd = call(
        functools.partial(mlp_grad_kernel, n),
        block_shapes(mlp_columns),
        [SM] + [VM] * 5,
        24,
        scratch=[pltpu.VMEM((width, mlp_columns), F32)],
    )(meta, n2, gl, ul, hidden, cotangent)
    mlp_blocks = reduce_blocks(even, odd, "ctx", n)

    full = lambda *dims: pl.BlockSpec(dims, lambda g: (0,) * len(dims))
    gm, branch, gnorm_mlp, dq_t, even, odd = call(
        functools.partial(backward_kernel, n, wt),
        (
            shape((rows, width), F32),
            shape((rows, width), BF),
            shape((1, width), F32),
            shape((width, rows), F32),
            shape((n // 2, rows, kv_width), BF),
            shape((n // 2, rows, kv_width), BF),
        ),
        [VM] * wt
        + [SM, SM]
        + [VM] * 6
        + [
            pl.BlockSpec((n * rows, PAIR), lambda g: (0, g)),
            pl.BlockSpec((1, 2 * wide, PAIR), lambda g: (g, 0, 0)),
            VM,
            VM,
        ],
        big,
        scratch=[
            pltpu.VMEM((rows, width), F32),
            pltpu.VMEM((KV_HEADS, 2 * wide, PAIR), BF),
            pltpu.VMEM((2 * KV_HEADS, 1, wide), F32),
            pltpu.VMEM((n * rows, PAIR), F32),
            pltpu.VMEM((2, PAIR, wide), F32),
        ],
        out_specs=(
            full(rows, width),
            full(rows, width),
            full(1, width),
            pl.BlockSpec((GROUP * HEAD, rows), lambda g: (g, 0)),
            pl.BlockSpec((n // 2, rows, PAIR), lambda g: (0, 0, g)),
            pl.BlockSpec((n // 2, rows, PAIR), lambda g: (0, 0, g)),
        ),
        grid=(KV_HEADS,),
    )(
        *quarters,
        meta,
        stretch_order,
        mixed,
        cotangent,
        gain_mlp,
        w_out,
        att_t,
        lse.reshape(2 * KV_HEADS, 1, wide),
        kv_all,
        q,
        cos_t,
        sin_t,
    )
    kv_terms = scatter_terms(even, odd, "ctx", n)

    gn_query, even, odd = call(
        functools.partial(query_grad_kernel, n),
        (shape((rows, width), F32),) + block_shapes(2 * width),
        [SM] + [VM] * 5,
        24,
        scratch=[pltpu.VMEM((width, 2 * width), F32)],
    )(meta, normed, dq_t, att_low, branch, w_query)
    query_blocks = reduce_blocks(even, odd, "ctx", n)

    grad_tokens, even, odd = call(
        functools.partial(key_grad_kernel, n, len(kv_terms)),
        (shape((rows, width), F32),) + block_shapes(kv_width, 8),
        [SM] + [VM] * (len(kv_terms) + 10),
        24,
        scratch=[pltpu.VMEM((width, kv_width), F32), pltpu.VMEM((8, 128 * n), F32)],
    )(meta, *kv_terms, normed, gn_query, w_key, w_value, cos, sin, tokens, gain_attn, gm, gnorm_mlp)
    key_blocks = reduce_blocks(even, odd, "ctx", n)

    grad_gate, grad_up, grad_down = join(mlp_blocks, mlp_columns, (hidden_width,) * 3, (2,))
    grad_query, grad_out = join(query_blocks, 2 * width, (width, width))
    grad_key, grad_value, grad_norm_attn, grad_norm_mlp = join(
        key_blocks, kv_width, (kv_width // 2,) * 2, norms=True
    )
    return (
        output,
        grad_tokens,
        grad_query,
        grad_key,
        grad_value,
        grad_out,
        grad_norm_attn.reshape(width),
        grad_norm_mlp.reshape(width),
        grad_gate,
        grad_up,
        grad_down,
    )


def solution(mesh):
    return jax.shard_map(
        functools.partial(local, mesh.shape["ctx"], mesh.shape["wt"]),
        mesh=mesh,
        in_specs=(
            P("ctx", None),
            P(),
            P(),
            P(),
            P(),
            P(),
            P(),
            P(None, "wt"),
            P(None, "wt"),
            P("wt", None),
            P(),
            P("ctx", None),
        ),
        out_specs=(
            P("ctx", None),
            P("ctx", None),
            P(),
            P(),
            P(),
            P(),
            P(),
            P(),
            P(None, "wt"),
            P(None, "wt"),
            P("wt", None),
        ),
        check_vma=False,
    )
```

```python
import functools

import jax
import jax.numpy as jnp
import numpy as np
from jax import lax
from jax.experimental import pallas as pl
from jax.experimental.pallas import tpu as pltpu
from jax.sharding import PartitionSpec as P

Q_HEADS = 9
KV_HEADS = 3
GROUP = 3
HEAD = 64
HALF = 32
PAIR = 2 * HEAD
EPSILON = 1e-05
THETA = 100000.0
NEGATIVE = -1e30
BF = jnp.bfloat16
F32 = jnp.float32
MIB = 1 << 20


def dot(left, right):
    return jnp.dot(left, right, preferred_element_type=F32)


def dot_nt(left, right):
    return lax.dot_general(left, right, (((1,), (1,)), ((), ())), preferred_element_type=F32)


def dot_tn(left, right):
    return lax.dot_general(left, right, (((0,), (0,)), ((), ())), preferred_element_type=F32)


def shape(dims, dtype):
    return jax.ShapeDtypeStruct(dims, dtype)


SPEC = {
    "v": pl.BlockSpec(memory_space=pltpu.VMEM),
    "s": pl.BlockSpec(memory_space=pltpu.SMEM),
    "h": pl.BlockSpec(memory_space=pltpu.HBM),
    "c": pl.BlockSpec(memory_space=pltpu.HBM),
}


class Fetched:
    def __init__(self, copy, ref):
        self.copy, self.ref, self.waited = copy, ref, False

    def get(self):
        if not self.waited:
            self.copy.wait()
            self.waited = True
        return self.ref


class Stored:
    def __init__(self, copy, ref):
        self.copy, self.ref, self.sent = copy, ref, False

    def send(self):
        self.copy.start()
        self.sent = True


def call(body, ins, in_kinds, outs, out_kinds, scratch=(), vmem=60, flops=0):
    real = [(a, kind) for a, kind in zip(ins, in_kinds) if kind != "m"]
    staged = [a for a, kind in real if kind == "c"]
    staged_out = [o for o, kind in zip(outs, out_kinds) if kind == "c"]
    count = len(staged) + len(staged_out)
    buffers = [pltpu.VMEM(a.shape, a.dtype) for a in staged + staged_out]
    if count:
        buffers.append(pltpu.SemaphoreType.DMA((count,)))

    def kernel(*refs):
        in_refs = iter(refs[: len(real)])
        out_refs = refs[len(real) : len(real) + len(outs)]
        own = refs[len(real) + len(outs) : len(refs) - len(buffers)]
        extra = refs[len(refs) - len(buffers) :]
        at = 0
        given, results = [], []
        for kind in in_kinds:
            ref = (lax.axis_index("ctx"), lax.axis_index("wt")) if kind == "m" else next(in_refs)
            if kind == "c":
                copy = pltpu.make_async_copy(ref, extra[at], extra[-1].at[at])
                copy.start()
                ref = Fetched(copy, extra[at])
                at += 1
            given.append(ref)
        for ref, kind in zip(out_refs, out_kinds):
            if kind == "c":
                ref = Stored(pltpu.make_async_copy(extra[at], ref, extra[-1].at[at]), extra[at])
                at += 1
            results.append(ref)
        body(given, results, own)
        for item in given:
            if isinstance(item, Fetched):
                item.get()
        for item in results:
            if isinstance(item, Stored):
                if not item.sent:
                    item.send()
                item.copy.wait()

    return pl.pallas_call(
        kernel,
        out_shape=tuple(outs),
        in_specs=[SPEC[k] for _, k in real],
        out_specs=tuple(SPEC[k] for k in out_kinds),
        scratch_shapes=list(scratch) + buffers,
        compiler_params=pltpu.CompilerParams(vmem_limit_bytes=vmem * MIB),
        cost_estimate=pl.CostEstimate(flops=flops, bytes_accessed=4 * MIB, transcendentals=0),
    )(*[a for a, _ in real])


def angle_tables(n, stretch):
    rates = THETA ** (-np.arange(HALF, dtype=np.float64) / HALF)
    places = np.arange(2 * n * stretch, dtype=np.float64).reshape(2 * n, 1, stretch)
    angle = places * rates[None, :, None]
    turned = np.concatenate([np.cos(angle), np.sin(angle)], axis=1).astype(np.float32)
    sign = np.concatenate([np.ones(HALF), -np.ones(HALF)])
    lanes = np.concatenate([rates, rates])
    start = np.arange(2 * n)[:, None] * stretch * lanes[None, :]
    offset = np.arange(stretch)[:, None] * lanes[None, :]

    def widen(table, fill):
        return np.concatenate([table, np.full(table.shape, fill)], axis=1).astype(np.float32)

    first = np.stack([widen(np.cos(start), 1.0), widen(np.sin(start) * sign, 0.0)], axis=1)
    inner = np.stack([widen(np.cos(offset), 1.0), widen(np.sin(offset) * sign, 0.0)])
    return turned, first, inner


def row_of(ref):
    return ref[...].astype(F32).reshape(1, ref.shape[0])


def norm_scale(x, axis):
    return lax.rsqrt(jnp.mean(x * x, axis=axis, keepdims=True) + EPSILON)


def key_body(ins, outs, scratch):
    meta, order, gain, tok, wk, wv, turned = ins
    normed_out, kv_out, angle_out, normed_q = outs
    (normed_s,) = scratch
    me = meta[0]
    low, high = order[0, 2 * me], order[0, 2 * me + 1]
    x = tok[...].astype(F32)
    gain = jnp.broadcast_to(row_of(gain), (8, x.shape[0])).T[:, 0:1]
    normed = (x * norm_scale(x, 0) * gain).astype(BF)
    normed_out[...] = normed
    normed_s[...] = normed.astype(F32)
    normed_q[...] = normed_s[span(meta[1], normed_q.shape[0]), :].astype(BF)
    turned = turned.get()
    angle = jnp.concatenate([turned[low], turned[high]], axis=1)
    angle_out[...] = angle
    cos, sin = angle[:HALF], angle[HALF:]
    k = dot(wk.get()[...], normed)
    v = dot(wv.get()[...], normed)
    parts = []
    for g in range(KV_HEADS):
        a, b = k[g * HEAD : g * HEAD + HALF], k[g * HEAD + HALF : (g + 1) * HEAD]
        parts += [a * cos - b * sin, b * cos + a * sin, v[g * HEAD : (g + 1) * HEAD]]
    kv_out[...] = jnp.concatenate(parts, axis=0).T.astype(BF)


def query_body(ins, outs, scratch):
    normed, wq, angle = ins
    q_out = outs[0].ref
    rows = normed.shape[1]
    stretch = rows // 2
    q = dot(normed[...].astype(F32).T.astype(BF), wq.get()[...])
    table = angle[...].T
    cos = jnp.concatenate([table[:, :HALF]] * 2, axis=1)
    sin = jnp.concatenate([-table[:, HALF:], table[:, HALF:]], axis=1)
    zero = jnp.zeros((rows, HEAD), F32)
    for h in range(Q_HEADS):
        qh = q[:, h * HEAD : (h + 1) * HEAD]
        swapped = jnp.concatenate([qh[:, HALF:], qh[:, :HALF]], axis=1)
        qr = (qh * cos + swapped * sin) * HEAD**-0.5
        wide = jnp.concatenate([qr, zero], axis=1).astype(BF)
        g, hh = h // GROUP, h % GROUP
        for sel in range(2):
            at = (sel * GROUP + hh) * stretch
            q_out[g, at : at + stretch, :] = wide[sel * stretch : (sel + 1) * stretch]


def parts_of(n):
    low_group = min(n, 8)
    unit_group = max(d for d in range(1, 14) if (n + 1) % d == 0)
    return low_group, n // low_group, unit_group, (n + 1) // unit_group


def loop(count, body):
    if count == 1:
        body(0)
    else:
        lax.fori_loop(0, count, lambda i, c: (body(i), c)[1], 0)


def unit(u, c, n):
    is_low = u <= c
    sel = jnp.where(is_low, 0, 1)
    stretch_id = jnp.where(is_low, u, n - 1 + u - c)
    diagonal = jnp.logical_or(u == c, u == n)
    return is_low, sel, stretch_id, diagonal


def seen_mask(stretch, diagonal):
    keys = lax.broadcasted_iota(jnp.int32, (stretch, GROUP * stretch), 0)
    cols = lax.broadcasted_iota(jnp.int32, (stretch, GROUP * stretch), 1)
    queries = lax.bitwise_and(cols, stretch - 1)
    return jnp.logical_or(keys <= queries, jnp.logical_not(diagonal))


def span(index, size):
    return pl.ds(pl.multiple_of(index * size, size), size)


def forward_body(n, wt, ins, outs, scratch):
    evens = ins[: n // 2]
    odds, meta, order, q_in, tok, w_out, gain, w_gate, w_up, cot, w_down = ins[n // 2 :]
    kv_all, att_t_out, lse_out, mixed_out, even, odd = outs[:6]
    pin_outs, out_parts = outs[6 : 6 + wt], outs[6 + wt :]
    kvn, m_s, l_s, o_s, part, grads, sems = scratch
    rows = tok.ref.shape[1]
    stretch = rows // 2
    wide = GROUP * stretch
    me = meta[0]
    copies = []
    for k in range(n):
        low = order[0, 2 * lax.bitwise_xor(me, k)]
        src = evens[k // 2] if k % 2 == 0 else odds.at[k // 2]
        for half in range(2):
            to = low if half == 0 else 2 * n - 1 - low
            copies.append(
                pltpu.make_async_copy(
                    src.at[half * stretch : (half + 1) * stretch],
                    kvn.at[span(to, stretch)],
                    sems.at[2 * k + half],
                )
            )
    for copy in copies:
        copy.start()
    for copy in copies:
        copy.wait()
    keep = pltpu.make_async_copy(kvn, kv_all, sems.at[2 * n])
    keep.start()
    c = order[0, 2 * me]
    low_group, low_steps, unit_group, unit_steps = parts_of(n)
    q_ref = q_in.get()
    att_t = att_t_out.ref

    def one_head(g):
        lanes = span(g, PAIR)
        for sel in range(2):
            m_s[2 * g + sel] = jnp.full((1, wide), NEGATIVE, F32)
            l_s[2 * g + sel] = jnp.zeros((1, wide), F32)
            o_s[2 * g + sel] = jnp.zeros((PAIR, wide), F32)

        def low_step(i):
            keys = kvn[span(i, low_group * stretch), lanes]
            s = dot_nt(keys, q_ref[g, wide : 2 * wide, :])
            at = 2 * g + 1
            top = jnp.maximum(m_s[at], jnp.max(s, axis=0, keepdims=True))
            fade = jnp.exp(m_s[at] - top)
            p = jnp.exp(s - top)
            l_s[at] = l_s[at] * fade + jnp.sum(p, axis=0, keepdims=True)
            o_s[at] = o_s[at] * fade + dot_tn(keys, p.astype(BF))
            m_s[at] = top

        loop(low_steps, low_step)

        def unit_step(i):
            scores = []
            tops = [m_s[2 * g], m_s[2 * g + 1]]
            for j in range(unit_group):
                u = i * unit_group + j
                is_low, sel, st, diagonal = unit(u, c, n)
                keys = kvn[span(st, stretch), lanes]
                s = dot_nt(keys, q_ref[g, span(sel, wide), :])
                s = jnp.where(seen_mask(stretch, diagonal), s, NEGATIVE)
                peak = jnp.max(s, axis=0, keepdims=True)
                tops[0] = jnp.where(is_low, jnp.maximum(tops[0], peak), tops[0])
                tops[1] = jnp.where(is_low, tops[1], jnp.maximum(tops[1], peak))
                scores.append((s, keys, is_low, sel))
            sums = []
            for sel in range(2):
                at = 2 * g + sel
                fade = jnp.exp(m_s[at] - tops[sel])
                sums.append(l_s[at] * fade)
                o_s[at] = o_s[at] * fade
                m_s[at] = tops[sel]
            for s, keys, is_low, sel in scores:
                p = jnp.exp(s - jnp.where(is_low, tops[0], tops[1]))
                part = jnp.sum(p, axis=0, keepdims=True)
                sums[0] = sums[0] + jnp.where(is_low, part, 0.0)
                sums[1] = sums[1] + jnp.where(is_low, 0.0, part)
                o_s[2 * g + sel] += dot_tn(keys, p.astype(BF))
            for sel in range(2):
                l_s[2 * g + sel] = sums[sel]

        loop(unit_steps, unit_step)
        for sel in range(2):
            at = 2 * g + sel
            total = l_s[at]
            lse_out.ref[at] = m_s[at] + jnp.log(total)
            result = o_s[at][HEAD:, :] / total
            for hh in range(GROUP):
                att_t[span(g * GROUP + hh, HEAD), sel * stretch : (sel + 1) * stretch] = result[
                    :, hh * stretch : (hh + 1) * stretch
                ]

    loop(KV_HEADS, one_head)
    lse_out.send()
    att_t_out.send()
    att_low = att_t[...].T.astype(BF)
    mixed = tok.get()[...].astype(F32).T + dot(att_low, w_out.get()[...])
    mixed_out.ref[...] = mixed
    mixed_out.send()
    n2 = (mixed * norm_scale(mixed, -1) * row_of(gain)).astype(BF)
    gate = dot(n2, w_gate.get()[...])
    up = dot(n2, w_up.get()[...])
    sig = 1.0 / (1.0 + jnp.exp(-gate))
    silu = gate * sig
    hidden = (silu * up).astype(BF)
    grad_hidden = dot_tn(cot.get()[...], w_down.get()[...])
    gl = (grad_hidden * up * (sig * (1.0 + gate * (1.0 - sig)))).astype(BF)
    ul = (grad_hidden * silu).astype(BF)
    piece = rows // wt
    part[...] = dot_nt(gl, w_gate.get()[...]) + dot_nt(ul, w_up.get()[...])
    for k in range(wt):
        pin_outs[k][...] = part[span(lax.bitwise_xor(meta[1], k), piece), :].astype(BF)
    part[...] = dot_nt(hidden, w_down.get()[...])
    for k in range(wt):
        out_parts[k][...] = part[span(lax.bitwise_xor(meta[1], k), piece), :].astype(BF)
    width = gl.shape[1]
    grads[:, :width] = dot_tn(n2, gl)
    grads[:, width : 2 * width] = dot_tn(n2, ul)
    grads[:, 2 * width :] = dot(cot.get()[...], hidden)
    if n > 8:
        even[...] = grads[...].astype(BF)
        odd[...] = jnp.zeros(odd.shape, BF)
    else:
        size = grads.shape[0] // n
        for k in range(n):
            to = even if k % 2 == 0 else odd
            to[k // 2] = grads[span(lax.bitwise_xor(me, k), size), :].astype(BF)
    keep.wait()


def backward_body(n, wt, ins, outs, scratch):
    quarters = ins[:wt]
    (meta, order, gain, mixed, cot, w_out, att_t, lse, kv, q_in, angle) = ins[wt : wt + 11]
    (first, inner, normed, wq, wk, wv, strip_odds) = ins[wt + 11 : wt + 18]
    strips = ins[wt + 18 :]
    gm_out, dq_out, even, odd = outs[:4]
    gn_s, do_s, dl_s, dkv, dq_s, dq_t, grads, norm_s, all_s, w_s, sems = scratch
    rows = mixed.ref.shape[0]
    width = mixed.ref.shape[1]
    stretch = rows // 2
    wide = GROUP * stretch
    me = meta[0]
    c = order[0, 2 * me]
    low_group, low_steps, unit_group, unit_steps = parts_of(n)
    copies = []
    for k in range(n):
        low = order[0, 2 * lax.bitwise_xor(me, k)]
        src = strips[k // 2] if k % 2 == 0 else strip_odds.at[k // 2]
        for half in range(2):
            to = low if half == 0 else 2 * n - 1 - low
            copies.append(
                pltpu.make_async_copy(
                    src.at[:, half * stretch : (half + 1) * stretch],
                    all_s.at[:, span(to, stretch)],
                    sems.at[2 * k + half],
                )
            )
    for copy in copies:
        copy.start()

    piece = rows // wt
    for k in range(wt):
        gn_s[span(lax.bitwise_xor(meta[1], k), piece), :] = quarters[k][...].astype(F32)
    x = mixed.get()[...]
    gn = gn_s[...]
    r = norm_scale(x, -1)
    xn = x * r
    e = gn * row_of(gain)
    gm = cot.get()[...].astype(F32).T + r * (e - xn * jnp.mean(e * xn, axis=-1, keepdims=True))
    gm_out.ref[...] = gm
    gm_out.send()
    norm_s[...] = jnp.zeros(norm_s.shape, F32)
    norm_s[1:2, :width] = jnp.sum(gn * xn, axis=0, keepdims=True)
    branch = gm.astype(BF)
    ga = dot_nt(branch, w_out.get()[...]).astype(BF).astype(F32)
    prod = ga.T * att_t.get()[...]
    zero = jnp.zeros((rows, HEAD), F32)
    for h in range(Q_HEADS):
        g, hh = h // GROUP, h % GROUP
        delta = jnp.sum(prod[h * HEAD : (h + 1) * HEAD, :], axis=0, keepdims=True)
        do = jnp.concatenate([zero, ga[:, h * HEAD : (h + 1) * HEAD]], axis=1).astype(BF)
        for sel in range(2):
            at = (sel * GROUP + hh) * stretch
            half = slice(sel * stretch, (sel + 1) * stretch)
            dl_s[2 * g + sel, :, hh * stretch : (hh + 1) * stretch] = delta[:, half]
            do_s[g, at : at + stretch, :] = do[half]
    strip = grads.shape[0]
    mine = span(meta[1], strip)
    grads[:, width : 2 * width] = dot(att_t.get()[mine, :].astype(BF), branch)
    lse, kv, q_ref, angle = lse.get(), kv.get(), q_in.get(), angle.get()
    first, inner = first.get(), inner.get()
    pre = kv
    lane_ids = lax.broadcasted_iota(jnp.int32, (stretch, PAIR), 1)

    def one_head(g):
        lanes = span(g, PAIR)
        dkv[n * stretch :, :] = jnp.zeros((n * stretch, PAIR), F32)
        dq_s[...] = jnp.zeros(dq_s.shape, F32)

        def low_step(i):
            at = span(i, low_group * stretch)
            keys = kv[at, lanes]
            q = q_ref[g, wide : 2 * wide, :]
            do = do_s[g, wide : 2 * wide, :]
            p = jnp.exp(dot_nt(keys, q) - lse[2 * g + 1])
            ds = (p * (dot_nt(keys, do) - dl_s[2 * g + 1])).astype(BF)
            dkv[at, :] = dot(ds, q) + dot(p.astype(BF), do)
            dq_s[1] += dot_tn(keys, ds)

        loop(low_steps, low_step)

        def unit_step(i):
            for j in range(unit_group):
                _, sel, st, diagonal = unit(i * unit_group + j, c, n)
                at = span(st, stretch)
                keys = kv[at, lanes]
                q = q_ref[g, span(sel, wide), :]
                do = do_s[g, span(sel, wide), :]
                p = jnp.exp(dot_nt(keys, q) - lse[2 * g + sel])
                p = jnp.where(seen_mask(stretch, diagonal), p, 0.0)
                ds = (p * (dot_nt(keys, do) - dl_s[2 * g + sel])).astype(BF)
                dkv[at, :] += dot(ds, q) + dot(p.astype(BF), do)
                dq_s[sel] += dot_tn(keys, ds)

        loop(unit_steps, unit_step)

        def turn(i):
            ct, st = inner[0], inner[1]
            cs, ss = first[i, 0:1, :], first[i, 1:2, :]
            part = dkv[span(i, stretch), :]
            back = pltpu.roll(part, PAIR - HALF, 1)
            ahead = pltpu.roll(part, HALF, 1)
            swapped = jnp.where(lane_ids < HALF, back, ahead)
            result = part * (ct * cs - st * ss) + swapped * (st * cs + ct * ss)
            pre[span(i, stretch), lanes] = result.astype(BF)

        if n <= 8:
            for i in range(2 * n):
                turn(i)
        else:
            loop(2 * n, turn)
        for sel in range(2):
            half = slice(sel * stretch, (sel + 1) * stretch)
            cos, sin = angle[:HALF, half], angle[HALF:, half]
            for hh in range(GROUP):
                dq = dq_s[sel, :HEAD, hh * stretch : (hh + 1) * stretch] * HEAD**-0.5
                a, b = dq[:HALF], dq[HALF:]
                turned = jnp.concatenate([a * cos + b * sin, b * cos - a * sin], axis=0)
                dq_t[span(g * GROUP + hh, HEAD), half] = turned

    loop(KV_HEADS, one_head)
    dq = dq_t[...].T.astype(BF)
    dq_out.ref[...] = dq
    dq_out.send()
    grads[:, :width] = dot(normed.get()[...], dq)
    for copy in copies:
        copy.wait()
    grads[:, 2 * width :] = dot(all_s[...], pre[...])
    wk, wv = wk.get()[...].astype(F32), wv.get()[...].astype(F32)
    chunks = []
    for g in range(KV_HEADS):
        chunks += [wk[g * HEAD : (g + 1) * HEAD], wv[g * HEAD : (g + 1) * HEAD]]
    w_s[...] = jnp.concatenate(chunks, axis=0).T
    sums = jnp.sum(grads[:, :width] * wq.get()[mine, :].astype(F32), axis=1, keepdims=True)
    sums = sums + jnp.sum(grads[:, 2 * width :] * w_s[mine, :], axis=1, keepdims=True)
    norm_s[0:1, :strip] = jnp.broadcast_to(sums, (strip, 128)).T[0:1, :]
    quarter = meta[1] * piece
    upper = quarter >= stretch
    inside = jnp.where(upper, quarter - stretch, quarter)

    def rows_for(who):
        low = order[0, 2 * who]
        st = jnp.where(upper, 2 * n - 1 - low, low)
        return pre[pl.ds(pl.multiple_of(st * stretch + inside, piece), piece), :]

    if n > 8:
        even[...] = grads[...].astype(BF)
        odd[...] = norm_s[...].astype(BF)
        for k in range(n):
            outs[4][k] = rows_for(k)
        return
    for k in range(n):
        who = lax.bitwise_xor(me, k)
        to = even if k % 2 == 0 else odd
        to[k // 2, :piece, :] = rows_for(who)
        block = grads[block_rows(strip, who), block_lanes(who)]
        cut = norm_s[:, span(who, 128)]
        tail = jnp.concatenate([cut, jnp.zeros((8, block.shape[1] - 128), F32)], axis=1)
        to[k // 2, piece:, :] = jnp.concatenate([block, tail], axis=0).astype(BF)


def block_rows(strip, who):
    size = strip // 2
    return pl.ds(pl.multiple_of(lax.shift_right_logical(who, 2) * size, size), size)


def block_lanes(who):
    return span(lax.bitwise_and(who, 3), KV_HEADS * PAIR)


def finish_body(wt, count, ins, outs, scratch):
    terms = ins[:count]
    out_terms = ins[count : count + wt]
    meta, gain, tok, mixed, gm, dq, wq, wk, wv = ins[count + wt :]
    (both_out,) = outs
    (x_s,) = scratch
    piece = both_out.shape[0]
    width = gain.shape[0]
    total = terms[0][:piece, :].astype(F32)
    for term in terms[1:]:
        total = total + term[:piece, :].astype(F32)
    mine = span(meta[1], piece)
    out = out_terms[0][...].astype(F32)
    for term in out_terms[1:]:
        out = out + term[...].astype(F32)
    both_out[:, 640:] = (mixed.get()[mine, :] + out).astype(BF)
    x_s[...] = tok.get()[...].astype(F32).T
    x = x_s[mine, :]
    dk, dv = [], []
    for g in range(KV_HEADS):
        dk.append(total[:, g * PAIR : g * PAIR + HEAD])
        dv.append(total[:, g * PAIR + HEAD : (g + 1) * PAIR])
    dk = jnp.concatenate(dk, axis=1).astype(BF)
    dv = jnp.concatenate(dv, axis=1).astype(BF)
    gn = dot_nt(dq.get()[mine, :], wq.get()[...])
    gn = gn + dot(dk, wk.get()[...]) + dot(dv, wv.get()[...])
    r = norm_scale(x, -1)
    xn = x * r
    e = gn * row_of(gain)
    result = gm.get()[mine, :] + r * (e - xn * jnp.mean(e * xn, axis=-1, keepdims=True))
    both_out[:, :width] = result.astype(BF)
    both_out[:, width:640] = jnp.zeros((piece, 640 - width), BF)


def mlp_join_body(n, wt, ins, outs, scratch):
    meta = ins[0]
    quarters = ins[1 : 1 + wt]
    blocks = ins[1 + wt :]
    grads, rows_s, out_s = scratch
    piece, width = quarters[0].shape[0], rows_s.shape[1]
    for k in range(wt):
        at = span(lax.bitwise_xor(meta[1], k), piece)
        rows_s[at, :] = quarters[k][:, :width].astype(F32)
        out_s[at, :] = quarters[k][:, 640:].astype(F32)
    outs[0][...] = rows_s[...].T
    outs[1][...] = out_s[...].T.astype(BF)
    if n > 8:
        grads[...] = blocks[0][...].astype(F32)
    else:
        size = grads.shape[0] // n
        for k in range(n):
            block = blocks[k // 2][...] if k % 2 == 0 else blocks[-1][k // 2]
            grads[span(lax.bitwise_xor(meta[0], k), size), :] = block.astype(F32)
    width = outs[2].shape[1]
    for i in range(3):
        outs[2 + i][...] = grads[:, i * width : (i + 1) * width]


def join_body(n, wt, ins, outs, scratch):
    meta, gain = ins[:2]
    blocks = ins[2:]
    gq, go, gk, gv, norm_attn, norm_mlp = outs
    grads, norm_s = scratch
    width = gq.shape[0]
    strip = width // wt
    norm_s[...] = jnp.zeros(norm_s.shape, F32)
    if n > 8:
        grads[...] = blocks[0][...].astype(F32)
        norm_s[...] = blocks[1][...].astype(F32)
    else:
        size = strip // 2
        for k in range(n):
            who = lax.bitwise_xor(meta[0], k)
            for kz in range(wt):
                lane = lax.bitwise_xor(meta[1], kz)
                block = blocks[k // 2][kz] if k % 2 == 0 else blocks[-1][k // 2, kz]
                block = block.astype(F32)
                at = lane * strip + lax.shift_right_logical(who, 2) * size
                grads[pl.ds(pl.multiple_of(at, size), size), block_lanes(who)] = block[:size]
                norm_s[lane, :, span(who, 128)] = block[size:, :128]
    gq[...] = grads[:, :width]
    go[...] = grads[:, width : 2 * width]
    both = grads[:, 2 * width :].T
    for g in range(KV_HEADS):
        gk[g * HEAD : (g + 1) * HEAD, :] = both[g * PAIR : g * PAIR + HEAD]
        gv[g * HEAD : (g + 1) * HEAD, :] = both[g * PAIR + HEAD : (g + 1) * PAIR]
    attn = jnp.concatenate([norm_s[lane, 0:1, :strip] for lane in range(wt)], axis=1)
    norm_attn[...] = (attn / row_of(gain)).reshape(width)
    norm_mlp[...] = norm_s[0, 1:2, :width].reshape(width)


def hop(x, axis, size, k):
    return lax.ppermute(x, axis, [(i, i ^ k) for i in range(size)])


def gather_blocks(x, axis, size):
    evens = [x] + [hop(x, axis, size, k) for k in range(2, size, 2)]
    odds = hop(jnp.stack(evens), axis, size, 1)
    return evens, odds


def pair_terms(even, odd, axis, size):
    got = hop(odd, axis, size, 1).astype(F32)
    pairs = [even[i].astype(F32) + got[i] for i in range(size // 2)]
    return pairs[:1] + [pair.astype(BF) for pair in pairs[1:]]


def scatter_terms(pairs, axis, size):
    return pairs[:1] + [hop(pairs[i], axis, size, 2 * i) for i in range(1, size // 2)]


def summed(terms):
    total = terms[0].astype(F32)
    for term in terms[1:]:
        total = total + term.astype(F32)
    return total


def after(dep, *arrays):
    held = lax.optimization_barrier((dep,) + arrays)
    return held[1:] if len(arrays) > 1 else held[1]


def local(
    n,
    wt,
    tokens,
    w_query,
    w_key,
    w_value,
    w_out,
    norm_attn,
    norm_mlp,
    w_gate,
    w_up,
    w_down,
    stretch_order,
    cotangent,
):
    rows, width = tokens.shape
    stretch = rows // 2
    wide = GROUP * stretch
    kv_width = KV_HEADS * PAIR
    hidden_width = w_gate.shape[1]
    piece = rows // wt
    size = width // n
    strip = width // wt
    small = n <= 8
    turned, first, inner = (jnp.asarray(t) for t in angle_tables(n, stretch))
    tok, cot, wk, wv, w_down = tokens.T, cotangent.T, w_key.T, w_value.T, w_down.T

    normed, kv, angle, normed_q = call(
        key_body,
        [None, stretch_order, norm_attn, tok, wk, wv, turned],
        "msvvccc",
        [shape((width, rows), BF), shape((rows, kv_width), BF), shape((HEAD, rows), F32)]
        + [shape((strip, rows), BF)],
        "vvvv",
        scratch=[pltpu.VMEM((width, rows), F32)],
    )
    (q,) = call(
        query_body,
        [normed, w_query, angle],
        "vcv",
        [shape((KV_HEADS, 2 * wide, PAIR), BF)],
        "c",
    )
    evens = [kv] + [hop(kv, "ctx", n, k) for k in range(2, n, 2)]
    odds = hop(jnp.stack(after(q, *evens)), "ctx", n, 1)

    mlp_columns = 3 * hidden_width
    if small:
        block_shapes = [shape((n // 2, size, mlp_columns), BF)] * 2
    else:
        block_shapes = [shape((width, mlp_columns), BF), shape((8, 128), BF)]
    kv_all, att_t, lse, mixed, even, odd, *pieces = call(
        functools.partial(forward_body, n, wt),
        [*evens, odds, None, stretch_order, q, tok, w_out, norm_mlp, w_gate, w_up, cot, w_down],
        "h" * (n // 2 + 1) + "msccc" + "v" + "cccc",
        [
            shape((n * rows, kv_width), BF),
            shape((width, rows), F32),
            shape((2 * KV_HEADS, 1, wide), F32),
            shape((rows, width), F32),
        ]
        + block_shapes
        + [shape((piece, width), BF)] * (2 * wt),
        "hccc" + "vv" + "v" * (2 * wt),
        scratch=[
            pltpu.VMEM((n * rows, kv_width), BF),
            pltpu.VMEM((2 * KV_HEADS, 1, wide), F32),
            pltpu.VMEM((2 * KV_HEADS, 1, wide), F32),
            pltpu.VMEM((2 * KV_HEADS, PAIR, wide), F32),
            pltpu.VMEM((rows, width), F32),
            pltpu.VMEM((width, mlp_columns), F32),
            pltpu.SemaphoreType.DMA((2 * n + 1,)),
        ],
    )
    part_in, out_parts = pieces[:wt], pieces[wt:]

    terms = [part_in[0]] + [hop(part_in[k], "wt", wt, k) for k in range(1, wt)]
    quarter = summed(terms).astype(BF)
    quarters = [quarter] + [hop(quarter, "wt", wt, k) for k in range(1, wt)]

    strips, strip_odds = gather_blocks(after(part_in[0], normed_q), "ctx", n)
    if small:
        mlp_own = summed(scatter_terms(pair_terms(even, odd, "ctx", n), "ctx", n)).astype(BF)
        quarters = after(mlp_own, *quarters)
        mlp_evens, mlp_odds = gather_blocks(mlp_own, "ctx", n)
        mlp_blocks = [*mlp_evens, mlp_odds]
    else:
        mlp_blocks = [lax.psum(even, "ctx")]

    columns = 2 * width + kv_width
    if small:
        out_blocks = [shape((n // 2, piece + strip // 2 + 8, kv_width), BF)] * 2
    else:
        out_blocks = [
            shape((strip, columns), BF),
            shape((8, 128 * n), BF),
            shape((n, piece, kv_width), BF),
        ]
    gm, dq, *message = call(
        functools.partial(backward_body, n, wt),
        [*quarters, None, stretch_order, norm_mlp, mixed, cot, w_out, att_t, lse, kv_all, q, angle]
        + [first, inner, normed_q, w_query, wk, wv, strip_odds, *strips],
        "v" * wt + "msv" + "c" * 8 + "c" * 6 + "h" * (1 + n // 2),
        [shape((rows, width), F32), shape((rows, width), BF)] + out_blocks,
        "cc" + "v" * len(out_blocks),
        scratch=[
            pltpu.VMEM((rows, width), F32),
            pltpu.VMEM((KV_HEADS, 2 * wide, PAIR), BF),
            pltpu.VMEM((2 * KV_HEADS, 1, wide), F32),
            pltpu.VMEM((n * rows, PAIR), F32),
            pltpu.VMEM((2, PAIR, wide), F32),
            pltpu.VMEM((width, rows), F32),
            pltpu.VMEM((strip, columns), F32),
            pltpu.VMEM((8, max(128 * n, 640)), F32),
            pltpu.VMEM((strip, n * rows), BF),
            pltpu.VMEM((width, kv_width), F32),
            pltpu.SemaphoreType.DMA((2 * n,)),
        ],
    )
    if small:
        message[1] = after(mlp_evens[-1], message[1])
        parts = scatter_terms(pair_terms(message[0], message[1], "ctx", n), "ctx", n)
        own = summed([part[piece:] for part in parts]).astype(BF)
        owns = [own] + [hop(own, "wt", wt, k) for k in range(1, wt)]
    else:
        parts = [lax.psum_scatter(message[2].astype(F32), "ctx", scatter_dimension=0)]
        last_blocks = list(lax.psum((message[0], message[1]), "ctx"))
        last_blocks = [lax.all_gather(b, "wt", axis=0, tiled=i == 0) for i, b in enumerate(last_blocks)]
    held = after(dq, *out_parts)
    out_parts = [held[0]] + [hop(held[k], "wt", wt, k) for k in range(1, wt)]
    (both,) = call(
        functools.partial(finish_body, wt, len(parts)),
        [*parts, *out_parts, None, norm_attn, tok, mixed, gm, dq, w_query, wk, wv],
        "v" * (len(parts) + wt) + "mv" + "c" * 7,
        [shape((piece, 640 + width), BF)],
        "v",
        scratch=[pltpu.VMEM((rows, width), F32)],
        vmem=16,
    )
    if small:
        own = jnp.stack(after(both, *owns))
        last_evens = [own] + [hop(own, "ctx", n, k) for k in range(2, n, 2)]
    boths = [both] + [hop(both, "wt", wt, k) for k in range(1, wt)]

    grad_tokens, output, grad_gate, grad_up, grad_down = call(
        functools.partial(mlp_join_body, n, wt),
        [None, *boths, *mlp_blocks],
        "m" + "v" * (wt + len(mlp_blocks)),
        [shape((width, rows), F32), shape((width, rows), BF)]
        + [shape((width, hidden_width), F32)] * 3,
        "vvvvv",
        scratch=[
            pltpu.VMEM((width, mlp_columns), F32),
            pltpu.VMEM((rows, width), F32),
            pltpu.VMEM((rows, width), F32),
        ],
        vmem=24,
    )
    if small:
        last_blocks = [*last_evens, hop(after(grad_gate, jnp.stack(last_evens)), "ctx", n, 1)]
    grad_query, grad_out, grad_key, grad_value, grad_norm_attn, grad_norm_mlp = call(
        functools.partial(join_body, n, wt),
        [None, norm_attn, *last_blocks],
        "mv" + "v" * len(last_blocks),
        [shape((width, width), F32)] * 2
        + [shape((kv_width // 2, width), F32)] * 2
        + [shape((width,), F32)] * 2,
        "vvvvvv",
        scratch=[
            pltpu.VMEM((width, columns), F32),
            pltpu.VMEM((wt, 8, max(128 * n, 640)), F32),
        ],
        vmem=24,
    )
    return (
        output.T,
        grad_tokens.T,
        grad_query,
        grad_key.T,
        grad_value.T,
        grad_out,
        grad_norm_attn,
        grad_norm_mlp,
        grad_gate,
        grad_up,
        grad_down.T,
    )


def solution(mesh):
    return jax.shard_map(
        functools.partial(local, mesh.shape["ctx"], mesh.shape["wt"]),
        mesh=mesh,
        in_specs=(
            P("ctx", None),
            P(),
            P(),
            P(),
            P(),
            P(),
            P(),
            P(None, "wt"),
            P(None, "wt"),
            P("wt", None),
            P(),
            P("ctx", None),
        ),
        out_specs=(
            P("ctx", None),
            P("ctx", None),
            P(),
            P(),
            P(),
            P(),
            P(),
            P(),
            P(None, "wt"),
            P(None, "wt"),
            P("wt", None),
        ),
        check_vma=False,
    )
```

```python
import functools

import jax
import jax.numpy as jnp
import numpy as np
from jax import lax
from jax.experimental import pallas as pl
from jax.experimental.pallas import tpu as pltpu
from jax.sharding import PartitionSpec as P

Q_HEADS = 9
KV_HEADS = 3
GROUP = 3
HEAD = 64
HALF = 32
PAIR = 2 * HEAD
EPSILON = 1e-05
THETA = 100000.0
NEGATIVE = -1e30
BF = jnp.bfloat16
F32 = jnp.float32
MIB = 1 << 20


def dot(left, right):
    return jnp.dot(left, right, preferred_element_type=F32)


def dot_nt(left, right):
    return lax.dot_general(left, right, (((1,), (1,)), ((), ())), preferred_element_type=F32)


def dot_tn(left, right):
    return lax.dot_general(left, right, (((0,), (0,)), ((), ())), preferred_element_type=F32)


def shape(dims, dtype):
    return jax.ShapeDtypeStruct(dims, dtype)


SPEC = {
    "v": pl.BlockSpec(memory_space=pltpu.VMEM),
    "s": pl.BlockSpec(memory_space=pltpu.SMEM),
    "h": pl.BlockSpec(memory_space=pltpu.HBM),
    "c": pl.BlockSpec(memory_space=pltpu.HBM),
}


class Fetched:
    def __init__(self, copy, ref):
        self.copy, self.ref, self.waited = copy, ref, False

    def get(self):
        if not self.waited:
            self.copy.wait()
            self.waited = True
        return self.ref


class Stored:
    def __init__(self, copy, ref):
        self.copy, self.ref, self.sent = copy, ref, False

    def send(self):
        self.copy.start()
        self.sent = True


def call(body, ins, in_kinds, outs, out_kinds, scratch=(), vmem=60, early=None, early_at=0, micros=3):
    real = [(a, kind) for a, kind in zip(ins, in_kinds) if kind != "m"]
    staged = [a for a, kind in real if kind == "c"]
    staged_out = [o for o, kind in zip(outs, out_kinds) if kind == "c"]
    count = len(staged) + len(staged_out)
    buffers = [pltpu.VMEM(a.shape, a.dtype) for a in staged + staged_out]
    if count:
        buffers.append(pltpu.SemaphoreType.DMA((count,)))

    def kernel(*refs):
        in_refs = iter(refs[: len(real)])
        out_refs = refs[len(real) : len(real) + len(outs)]
        own = refs[len(real) + len(outs) : len(refs) - len(buffers)]
        extra = refs[len(refs) - len(buffers) :]
        at = 0
        given, results = [], []
        for kind in in_kinds:
            place = (lax.axis_index("ctx"), lax.axis_index("wt")) if kind == "m" else next(in_refs)
            given.append(place)
        state = ()
        for i, kind in enumerate(in_kinds):
            if early is not None and i == early_at:
                state = (early(given, own),)
            if kind == "c":
                ref = given[i]
                copy = pltpu.make_async_copy(ref, extra[at], extra[-1].at[at])
                copy.start()
                given[i] = Fetched(copy, extra[at])
                at += 1
        for ref, kind in zip(out_refs, out_kinds):
            if kind == "c":
                ref = Stored(pltpu.make_async_copy(extra[at], ref, extra[-1].at[at]), extra[at])
                at += 1
            results.append(ref)
        body(given, results, own, *state)
        for item in given:
            if isinstance(item, Fetched):
                item.get()
        for item in results:
            if isinstance(item, Stored):
                if not item.sent:
                    item.send()
                item.copy.wait()

    return pl.pallas_call(
        kernel,
        out_shape=tuple(outs),
        in_specs=[SPEC[k] for _, k in real],
        out_specs=tuple(SPEC[k] for k in out_kinds),
        scratch_shapes=list(scratch) + buffers,
        compiler_params=pltpu.CompilerParams(vmem_limit_bytes=vmem * MIB),
        cost_estimate=pl.CostEstimate(flops=micros * 1_150_000_000, bytes_accessed=MIB, transcendentals=0),
    )(*[a for a, _ in real])


def angle_tables(n, stretch):
    rates = THETA ** (-np.arange(HALF, dtype=np.float64) / HALF)
    places = np.arange(2 * n * stretch, dtype=np.float64).reshape(2 * n, 1, stretch)
    angle = places * rates[None, :, None]
    turned = np.concatenate([np.cos(angle), np.sin(angle)], axis=1).astype(np.float32)
    sign = np.concatenate([np.ones(HALF), -np.ones(HALF)])
    lanes = np.concatenate([rates, rates])
    start = np.arange(2 * n)[:, None] * stretch * lanes[None, :]
    offset = np.arange(stretch)[:, None] * lanes[None, :]

    def widen(table, fill):
        return np.concatenate([table, np.full(table.shape, fill)], axis=1).astype(np.float32)

    first = np.stack([widen(np.cos(start), 1.0), widen(np.sin(start) * sign, 0.0)], axis=1)
    inner = np.stack([widen(np.cos(offset), 1.0), widen(np.sin(offset) * sign, 0.0)])
    return turned, first, inner


def row_of(ref):
    return ref[...].astype(F32).reshape(1, ref.shape[0])


def norm_scale(x, axis):
    return lax.rsqrt(jnp.mean(x * x, axis=axis, keepdims=True) + EPSILON)


def key_early(ins, scratch):
    meta, order, turned = ins[0], ins[1], ins[-1]
    copies = []
    for half in range(2):
        src = turned.at[order[0, 2 * meta[0] + half]]
        copies.append(pltpu.make_async_copy(src, scratch[1].at[half], scratch[2].at[half]))
        copies[-1].start()
    return copies


def key_body(ins, outs, scratch, copies):
    meta, order, gain, tok, wk, wv, turned = ins
    normed_out, kv_out, angle_out, normed_q = outs
    normed_s, angle_s, sems = scratch
    x = tok.get()[...].astype(F32)
    gain = jnp.broadcast_to(row_of(gain.get()), (8, x.shape[0])).T[:, 0:1]
    normed = (x * norm_scale(x, 0) * gain).astype(BF)
    normed_out[...] = normed
    normed_s[...] = normed.astype(F32)
    normed_q[...] = normed_s[span(meta[1], normed_q.shape[0]), :].astype(BF)
    for copy in copies:
        copy.wait()
    angle = jnp.concatenate([angle_s[0], angle_s[1]], axis=1)
    angle_out[...] = angle
    cos, sin = angle[:HALF], angle[HALF:]
    k = dot(wk.get()[...], normed)
    v = dot(wv.get()[...], normed)
    parts = []
    for g in range(KV_HEADS):
        a, b = k[g * HEAD : g * HEAD + HALF], k[g * HEAD + HALF : (g + 1) * HEAD]
        parts += [a * cos - b * sin, b * cos + a * sin, v[g * HEAD : (g + 1) * HEAD]]
    kv_out[...] = jnp.concatenate(parts, axis=0).T.astype(BF)


def query_body(ins, outs, scratch):
    normed, wq, angle = ins
    q_out = outs[0].ref
    rows = normed.shape[1]
    stretch = rows // 2
    q = dot(normed[...].astype(F32).T.astype(BF), wq.get()[...])
    table = angle[...].T
    cos = jnp.concatenate([table[:, :HALF]] * 2, axis=1)
    sin = jnp.concatenate([-table[:, HALF:], table[:, HALF:]], axis=1)
    zero = jnp.zeros((rows, HEAD), F32)
    for h in range(Q_HEADS):
        qh = q[:, h * HEAD : (h + 1) * HEAD]
        swapped = jnp.concatenate([qh[:, HALF:], qh[:, :HALF]], axis=1)
        qr = (qh * cos + swapped * sin) * HEAD**-0.5
        wide = jnp.concatenate([qr, zero], axis=1).astype(BF)
        g, hh = h // GROUP, h % GROUP
        for sel in range(2):
            at = (sel * GROUP + hh) * stretch
            q_out[g, at : at + stretch, :] = wide[sel * stretch : (sel + 1) * stretch]


def parts_of(n):
    low_group = min(n, 8)
    unit_group = max(d for d in range(1, 14) if (n + 1) % d == 0)
    return low_group, n // low_group, unit_group, (n + 1) // unit_group


def loop(count, body):
    if count == 1:
        body(0)
    else:
        lax.fori_loop(0, count, lambda i, c: (body(i), c)[1], 0)


def unit(u, c, n):
    is_low = u <= c
    sel = jnp.where(is_low, 0, 1)
    stretch_id = jnp.where(is_low, u, n - 1 + u - c)
    diagonal = jnp.logical_or(u == c, u == n)
    return is_low, sel, stretch_id, diagonal


def seen_mask(stretch, diagonal):
    keys = lax.broadcasted_iota(jnp.int32, (stretch, GROUP * stretch), 0)
    cols = lax.broadcasted_iota(jnp.int32, (stretch, GROUP * stretch), 1)
    queries = lax.bitwise_and(cols, stretch - 1)
    return jnp.logical_or(keys <= queries, jnp.logical_not(diagonal))


def span(index, size):
    return pl.ds(pl.multiple_of(index * size, size), size)


def natural_copies(n, me, order, evens, odds, to, sems, stretch, lanes=False):
    copies = []
    for k in range(n):
        low = order[0, 2 * lax.bitwise_xor(me, k)]
        src = evens[k // 2] if k % 2 == 0 else odds.at[k // 2]
        for half in range(2):
            at = span(low if half == 0 else 2 * n - 1 - low, stretch)
            cut = slice(half * stretch, (half + 1) * stretch)
            src_cut, to_cut = (src.at[:, cut], to.at[:, at]) if lanes else (src.at[cut], to.at[at])
            copies.append(pltpu.make_async_copy(src_cut, to_cut, sems.at[2 * k + half]))
    for copy in copies:
        copy.start()
    return copies


def forward_early(n, ins, scratch):
    evens, (odds, meta, order) = ins[: n // 2], ins[n // 2 : n // 2 + 3]
    return natural_copies(n, meta[0], order, evens, odds, scratch[0], scratch[-1], evens[0].shape[0] // 2)


def forward_body(n, wt, ins, outs, scratch, copies):
    odds, meta, order, q_in, tok, w_out, gain, w_gate, w_up, cot, w_down = ins[n // 2 :]
    att_t_out, lse_out, mixed_out, even, odd, mixed_q = outs[:6]
    pin_outs, out_parts = outs[6 : 6 + wt], outs[6 + wt :]
    kvn, m_s, l_s, o_s, part, grads, sems = scratch
    rows = tok.ref.shape[1]
    stretch = rows // 2
    wide = GROUP * stretch
    me = meta[0]
    for copy in copies:
        copy.wait()
    c = order[0, 2 * me]
    low_group, low_steps, unit_group, unit_steps = parts_of(n)
    q_ref = q_in.get()
    att_t = att_t_out.ref

    def one_head(g):
        lanes = span(g, PAIR)
        for sel in range(2):
            m_s[2 * g + sel] = jnp.full((1, wide), NEGATIVE, F32)
            l_s[2 * g + sel] = jnp.zeros((1, wide), F32)
            o_s[2 * g + sel] = jnp.zeros((PAIR, wide), F32)

        def low_step(i):
            keys = kvn[span(i, low_group * stretch), lanes]
            s = dot_nt(keys, q_ref[g, wide : 2 * wide, :])
            at = 2 * g + 1
            top = jnp.maximum(m_s[at], jnp.max(s, axis=0, keepdims=True))
            fade = jnp.exp(m_s[at] - top)
            p = jnp.exp(s - top)
            l_s[at] = l_s[at] * fade + jnp.sum(p, axis=0, keepdims=True)
            o_s[at] = o_s[at] * fade + dot_tn(keys, p.astype(BF))
            m_s[at] = top

        loop(low_steps, low_step)

        def unit_step(i):
            scores = []
            tops = [m_s[2 * g], m_s[2 * g + 1]]
            for j in range(unit_group):
                u = i * unit_group + j
                is_low, sel, st, diagonal = unit(u, c, n)
                keys = kvn[span(st, stretch), lanes]
                s = dot_nt(keys, q_ref[g, span(sel, wide), :])
                s = jnp.where(seen_mask(stretch, diagonal), s, NEGATIVE)
                peak = jnp.max(s, axis=0, keepdims=True)
                tops[0] = jnp.where(is_low, jnp.maximum(tops[0], peak), tops[0])
                tops[1] = jnp.where(is_low, tops[1], jnp.maximum(tops[1], peak))
                scores.append((s, keys, is_low, sel))
            sums = []
            for sel in range(2):
                at = 2 * g + sel
                fade = jnp.exp(m_s[at] - tops[sel])
                sums.append(l_s[at] * fade)
                o_s[at] = o_s[at] * fade
                m_s[at] = tops[sel]
            for s, keys, is_low, sel in scores:
                p = jnp.exp(s - jnp.where(is_low, tops[0], tops[1]))
                part = jnp.sum(p, axis=0, keepdims=True)
                sums[0] = sums[0] + jnp.where(is_low, part, 0.0)
                sums[1] = sums[1] + jnp.where(is_low, 0.0, part)
                o_s[2 * g + sel] += dot_tn(keys, p.astype(BF))
            for sel in range(2):
                l_s[2 * g + sel] = sums[sel]

        loop(unit_steps, unit_step)
        for sel in range(2):
            at = 2 * g + sel
            total = l_s[at]
            lse_out.ref[at] = m_s[at] + jnp.log(total)
            result = o_s[at][HEAD:, :] / total
            for hh in range(GROUP):
                att_t[span(g * GROUP + hh, HEAD), sel * stretch : (sel + 1) * stretch] = result[
                    :, hh * stretch : (hh + 1) * stretch
                ]

    loop(KV_HEADS, one_head)
    lse_out.send()
    att_t_out.send()
    att_low = att_t[...].T.astype(BF)
    mixed = tok.get()[...].astype(F32).T + dot(att_low, w_out.get()[...])
    width = mixed.shape[1]
    part[...] = jnp.zeros(part.shape, F32)
    part[:, :width] = mixed
    mixed_out.ref[...] = part[...]
    mixed_out.send()
    n2 = (mixed * norm_scale(mixed, -1) * row_of(gain.get())).astype(BF)
    gate = dot(n2, w_gate.get()[...])
    up = dot(n2, w_up.get()[...])
    sig = 1.0 / (1.0 + jnp.exp(-gate))
    silu = gate * sig
    hidden = (silu * up).astype(BF)
    grad_hidden = dot_tn(cot.get()[...], w_down.get()[...])
    gl = (grad_hidden * up * (sig * (1.0 + gate * (1.0 - sig)))).astype(BF)
    ul = (grad_hidden * silu).astype(BF)
    piece = rows // wt
    mixed_q.ref[...] = part[span(meta[1], piece), :]
    mixed_q.send()
    part[:, :width] = dot_nt(gl, w_gate.get()[...]) + dot_nt(ul, w_up.get()[...])
    for k in range(wt):
        pin_outs[k].ref[...] = part[span(lax.bitwise_xor(meta[1], k), piece), :].astype(BF)
        pin_outs[k].send()
    part[:, :width] = dot_nt(hidden, w_down.get()[...])
    for k in range(wt):
        out_parts[k].ref[...] = part[span(lax.bitwise_xor(meta[1], k), piece), :].astype(BF)
        out_parts[k].send()
    units = gl.shape[1]
    grads[:, :units] = dot_tn(n2, gl)
    grads[:, units : 2 * units] = dot_tn(n2, ul)
    grads[:, 2 * units :] = dot(cot.get()[...], hidden)
    if n > 8:
        even.ref[...] = grads[...].astype(BF)
        odd.ref[...] = jnp.zeros(odd.ref.shape, BF)
    else:
        size = grads.shape[0] // n
        for k in range(n):
            to = even.ref if k % 2 == 0 else odd.ref
            to[k // 2] = grads[span(lax.bitwise_xor(me, k), size), :].astype(BF)


def backward_early(n, wt, ins, scratch):
    meta, order = ins[wt], ins[wt + 1]
    blocks = ins[wt + 16 :]
    count = n // 2 + 1
    evens, odds = blocks[: count - 1], blocks[count - 1]
    strips, strip_odds = blocks[count : 2 * count - 1], blocks[2 * count - 1]
    stretch = evens[0].shape[0] // 2
    all_s, kv, sems, strip_sems = scratch[8], scratch[10], scratch[11], scratch[12]
    kv_copies = natural_copies(n, meta[0], order, evens, odds, kv, sems, stretch)
    return kv_copies, natural_copies(
        n, meta[0], order, strips, strip_odds, all_s, strip_sems, stretch, True
    )


def backward_body(n, wt, ins, outs, scratch, copies):
    kv_copies, strip_copies = copies
    quarters = ins[:wt]
    (meta, order, gain, mixed, cot, w_out, att_t, lse, q_in, angle) = ins[wt : wt + 10]
    (first, inner, normed, wq, wk, wv) = ins[wt + 10 : wt + 16]
    gm_out, dq_out, even, odd = outs[:4]
    gn_s, do_s, dl_s, dkv, dq_s, dq_t, grads, norm_s, all_s, w_s, kv = scratch[:11]
    rows = mixed.ref.shape[0]
    width = gain.ref.shape[0]
    stretch = rows // 2
    wide = GROUP * stretch
    me = meta[0]
    c = order[0, 2 * me]
    low_group, low_steps, unit_group, unit_steps = parts_of(n)
    piece = rows // wt
    for k in range(wt):
        gn_s[span(lax.bitwise_xor(meta[1], k), piece), :] = quarters[k].get()[...].astype(F32)
    x = mixed.get()[:, :width]
    gn = gn_s[:, :width]
    r = norm_scale(x, -1)
    xn = x * r
    e = gn * row_of(gain.get())
    gm = cot.get()[...].astype(F32).T + r * (e - xn * jnp.mean(e * xn, axis=-1, keepdims=True))
    gn_s[:, :width] = gm
    gm_out.ref[...] = gn_s[span(meta[1], piece), :]
    gm_out.send()
    norm_s[...] = jnp.zeros(norm_s.shape, F32)
    norm_s[1:2, :width] = jnp.sum(gn * xn, axis=0, keepdims=True)
    branch = gm.astype(BF)
    ga = dot_nt(branch, w_out.get()[...]).astype(BF).astype(F32)
    prod = ga.T * att_t.get()[...]
    zero = jnp.zeros((rows, HEAD), F32)
    for h in range(Q_HEADS):
        g, hh = h // GROUP, h % GROUP
        delta = jnp.sum(prod[h * HEAD : (h + 1) * HEAD, :], axis=0, keepdims=True)
        do = jnp.concatenate([zero, ga[:, h * HEAD : (h + 1) * HEAD]], axis=1).astype(BF)
        for sel in range(2):
            at = (sel * GROUP + hh) * stretch
            half = slice(sel * stretch, (sel + 1) * stretch)
            dl_s[2 * g + sel, :, hh * stretch : (hh + 1) * stretch] = delta[:, half]
            do_s[g, at : at + stretch, :] = do[half]
    strip = grads.shape[0]
    mine = span(meta[1], strip)
    grads[:, width : 2 * width] = dot(att_t.get()[mine, :].astype(BF), branch)
    lse, q_ref, angle = lse.get(), q_in.get(), angle.get()
    for copy in kv_copies:
        copy.wait()
    first, inner = first.get(), inner.get()
    chunk = 4
    low_chunks = lax.shift_right_logical(c, 2)
    key_ids = lax.broadcasted_iota(jnp.int32, (chunk * stretch, wide), 0)
    query_ids = lax.broadcasted_iota(jnp.int32, (chunk * stretch, wide), 1)
    query_ids = lax.bitwise_and(query_ids, stretch - 1)
    pre = kv
    lane_ids = lax.broadcasted_iota(jnp.int32, (stretch, PAIR), 1)

    def one_head(g):
        lanes = span(g, PAIR)
        dkv[n * stretch :, :] = jnp.zeros((n * stretch, PAIR), F32)
        dq_s[...] = jnp.zeros(dq_s.shape, F32)

        def low_step(i):
            at = span(i, low_group * stretch)
            keys = kv[at, lanes]
            q = q_ref[g, wide : 2 * wide, :]
            do = do_s[g, wide : 2 * wide, :]
            p = jnp.exp(dot_nt(keys, q) - lse[2 * g + 1])
            ds = (p * (dot_nt(keys, do) - dl_s[2 * g + 1])).astype(BF)
            dkv[at, :] = dot(ds, q) + dot(p.astype(BF), do)
            dq_s[1] += dot_tn(keys, ds)

        loop(low_steps, low_step)

        def unit_step(u):
            is_low = u <= low_chunks
            sel = jnp.where(is_low, 0, 1)
            low_key = jnp.where(is_low, u, u - low_chunks - 1 + n // chunk) * (chunk * stretch)
            at = pl.ds(pl.multiple_of(low_key, chunk * stretch), chunk * stretch)
            keys = kv[at, lanes]
            q = q_ref[g, span(sel, wide), :]
            do = do_s[g, span(sel, wide), :]
            p = jnp.exp(dot_nt(keys, q) - lse[2 * g + sel])
            ahead = low_key - jnp.where(is_low, c, 2 * n - 1 - c) * stretch
            p = jnp.where(key_ids + ahead <= query_ids, p, 0.0)
            ds = (p * (dot_nt(keys, do) - dl_s[2 * g + sel])).astype(BF)
            dkv[at, :] += dot(ds, q) + dot(p.astype(BF), do)
            dq_s[sel] += dot_tn(keys, ds)

        if n <= 8:
            for u in range(n // chunk + 1):
                unit_step(u)
        else:
            loop(n // chunk + 1, unit_step)

        def turn(i):
            ct, st = inner[0], inner[1]
            cs, ss = first[i, 0:1, :], first[i, 1:2, :]
            part = dkv[span(i, stretch), :]
            back = pltpu.roll(part, PAIR - HALF, 1)
            ahead = pltpu.roll(part, HALF, 1)
            swapped = jnp.where(lane_ids < HALF, back, ahead)
            result = part * (ct * cs - st * ss) + swapped * (st * cs + ct * ss)
            pre[span(i, stretch), lanes] = result.astype(BF)

        if n <= 8:
            for i in range(2 * n):
                turn(i)
        else:
            loop(2 * n, turn)
        for sel in range(2):
            half = slice(sel * stretch, (sel + 1) * stretch)
            cos, sin = angle[:HALF, half], angle[HALF:, half]
            for hh in range(GROUP):
                dq = dq_s[sel, :HEAD, hh * stretch : (hh + 1) * stretch] * HEAD**-0.5
                a, b = dq[:HALF], dq[HALF:]
                turned = jnp.concatenate([a * cos + b * sin, b * cos - a * sin], axis=0)
                dq_t[span(g * GROUP + hh, HEAD), half] = turned

    loop(KV_HEADS, one_head)
    dq = dq_t[...].T.astype(BF)
    gn_s[:, :width] = dq.astype(F32)
    dq_out.ref[...] = gn_s[span(meta[1], piece), :].astype(BF)
    dq_out.send()
    grads[:, :width] = dot(normed.get()[...], dq)
    for copy in strip_copies:
        copy.wait()
    grads[:, 2 * width :] = dot(all_s[...], pre[...])
    wk, wv = wk.get()[...].astype(F32), wv.get()[...].astype(F32)
    chunks = []
    for g in range(KV_HEADS):
        chunks += [wk[g * HEAD : (g + 1) * HEAD], wv[g * HEAD : (g + 1) * HEAD]]
    w_s[...] = jnp.concatenate(chunks, axis=0).T
    sums = jnp.sum(grads[:, :width] * wq.get()[mine, :].astype(F32), axis=1, keepdims=True)
    sums = sums + jnp.sum(grads[:, 2 * width :] * w_s[mine, :], axis=1, keepdims=True)
    norm_s[0:1, :strip] = jnp.broadcast_to(sums, (strip, 128)).T[0:1, :]
    quarter = meta[1] * piece
    upper = quarter >= stretch
    inside = jnp.where(upper, quarter - stretch, quarter)

    def rows_for(who):
        low = order[0, 2 * who]
        st = jnp.where(upper, 2 * n - 1 - low, low)
        return pre[pl.ds(pl.multiple_of(st * stretch + inside, piece), piece), :]

    if n > 8:
        even[...] = grads[...].astype(BF)
        odd[...] = norm_s[...].astype(BF)
        for k in range(n):
            outs[4][k] = rows_for(k)
        return
    for k in range(n):
        who = lax.bitwise_xor(me, k)
        to = even if k % 2 == 0 else odd
        to[k // 2, :piece, :] = rows_for(who)
        block = grads[block_rows(strip, who), block_lanes(who)]
        cut = norm_s[:, span(who, 128)]
        tail = jnp.concatenate([cut, jnp.zeros((8, block.shape[1] - 128), F32)], axis=1)
        to[k // 2, piece:, :] = jnp.concatenate([block, tail], axis=0).astype(BF)


def block_rows(strip, who):
    size = strip // 2
    return pl.ds(pl.multiple_of(lax.shift_right_logical(who, 2) * size, size), size)


def block_lanes(who):
    return span(lax.bitwise_and(who, 3), KV_HEADS * PAIR)


def finish_body(count, ins, outs, scratch):
    terms = ins[:count]
    meta, gain, tok, gm, dq, wq, wk, wv = ins[count:]
    (gt_out,) = outs
    (x_s,) = scratch
    piece = gt_out.shape[0]
    total = terms[0][:piece, :].astype(F32)
    for term in terms[1:]:
        total = total + term[:piece, :].astype(F32)
    mine = span(meta[1], piece)
    x_s[...] = tok.get()[...].astype(F32).T
    x = x_s[mine, :]
    dk, dv = [], []
    for g in range(KV_HEADS):
        dk.append(total[:, g * PAIR : g * PAIR + HEAD])
        dv.append(total[:, g * PAIR + HEAD : (g + 1) * PAIR])
    dk = jnp.concatenate(dk, axis=1).astype(BF)
    dv = jnp.concatenate(dv, axis=1).astype(BF)
    width = gain.shape[0]
    gn = dot_nt(dq[:, :width], wq.get()[...])
    gn = gn + dot(dk, wk.get()[...]) + dot(dv, wv.get()[...])
    r = norm_scale(x, -1)
    xn = x * r
    e = gn * row_of(gain)
    result = gm[:, :width] + r * (e - xn * jnp.mean(e * xn, axis=-1, keepdims=True))
    gt_out[:, :width] = result.astype(BF)
    gt_out[:, width:] = jnp.zeros((piece, gt_out.shape[1] - width), BF)


def token_join_body(wt, ins, outs, scratch):
    meta = ins[0]
    (rows_s,) = scratch
    for i in range(2):
        quarters = ins[1 + i * wt : 1 + (i + 1) * wt]
        for k in range(wt):
            at = span(lax.bitwise_xor(meta[1], k), quarters[0].shape[0])
            rows_s[at, :] = quarters[k][:, : rows_s.shape[1]].astype(F32)
        outs[i][...] = rows_s[...].T.astype(outs[i].dtype)


def mlp_join_body(n, ins, outs, scratch):
    meta, blocks = ins[0], ins[1:]
    (grads,) = scratch
    if n > 8:
        grads[...] = blocks[0][...].astype(F32)
    else:
        size = grads.shape[0] // n
        for k in range(n):
            block = blocks[k // 2][...] if k % 2 == 0 else blocks[-1][k // 2]
            grads[span(lax.bitwise_xor(meta[0], k), size), :] = block.astype(F32)
    width = outs[0].shape[1]
    for i in range(3):
        outs[i][...] = grads[:, i * width : (i + 1) * width]


def join_body(n, wt, ins, outs, scratch):
    meta, gain = ins[:2]
    blocks = ins[2:]
    gq, go, gk, gv, norm_attn, norm_mlp = outs
    grads, norm_s = scratch
    width = gq.shape[0]
    strip = width // wt
    norm_s[...] = jnp.zeros(norm_s.shape, F32)
    if n > 8:
        grads[...] = blocks[0][...].astype(F32)
        norm_s[...] = blocks[1][...].astype(F32)
    else:
        size = strip // 2
        for k in range(n):
            who = lax.bitwise_xor(meta[0], k)
            for kz in range(wt):
                lane = lax.bitwise_xor(meta[1], kz)
                block = blocks[k // 2][kz] if k % 2 == 0 else blocks[-1][k // 2, kz]
                block = block.astype(F32)
                at = lane * strip + lax.shift_right_logical(who, 2) * size
                grads[pl.ds(pl.multiple_of(at, size), size), block_lanes(who)] = block[:size]
                norm_s[lane, :, span(who, 128)] = block[size:, :128]
    gq[...] = grads[:, :width]
    go[...] = grads[:, width : 2 * width]
    both = grads[:, 2 * width :].T
    for g in range(KV_HEADS):
        gk[g * HEAD : (g + 1) * HEAD, :] = both[g * PAIR : g * PAIR + HEAD]
        gv[g * HEAD : (g + 1) * HEAD, :] = both[g * PAIR + HEAD : (g + 1) * PAIR]
    attn = jnp.concatenate([norm_s[lane, 0:1, :strip] for lane in range(wt)], axis=1)
    norm_attn[...] = (attn / row_of(gain)).reshape(width)
    norm_mlp[...] = norm_s[0, 1:2, :width].reshape(width)


def hop(x, axis, size, k):
    return lax.ppermute(x, axis, [(i, i ^ k) for i in range(size)])


def gather_blocks(x, axis, size):
    evens = [x] + [hop(x, axis, size, k) for k in range(2, size, 2)]
    odds = hop(jnp.stack(evens), axis, size, 1)
    return evens, odds


def pair_terms(even, odd, axis, size):
    got = hop(odd, axis, size, 1).astype(F32)
    pairs = [even[i].astype(F32) + got[i] for i in range(size // 2)]
    return pairs[:1] + [pair.astype(BF) for pair in pairs[1:]]


def scatter_terms(pairs, axis, size):
    return pairs[:1] + [hop(pairs[i], axis, size, 2 * i) for i in range(1, size // 2)]


def summed(terms):
    total = terms[0].astype(F32)
    for term in terms[1:]:
        total = total + term.astype(F32)
    return total


def after(dep, *arrays):
    held = lax.optimization_barrier((dep,) + arrays)
    return list(held[1:]) if len(arrays) > 1 else held[1]


def local(
    n,
    wt,
    tokens,
    w_query,
    w_key,
    w_value,
    w_out,
    norm_attn,
    norm_mlp,
    w_gate,
    w_up,
    w_down,
    stretch_order,
    cotangent,
):
    rows, width = tokens.shape
    stretch = rows // 2
    wide = GROUP * stretch
    kv_width = KV_HEADS * PAIR
    hidden_width = w_gate.shape[1]
    piece = rows // wt
    size = width // n
    strip = width // wt
    small = n <= 8
    padded = -(-width // 128) * 128
    turned, first, inner = (jnp.asarray(t) for t in angle_tables(n, stretch))
    tok, cot, wk, wv, w_down = tokens.T, cotangent.T, w_key.T, w_value.T, w_down.T

    normed, kv, angle, normed_q = call(
        key_body,
        [None, stretch_order, norm_attn, tok, wk, wv, turned],
        "mscccch",
        [shape((width, rows), BF), shape((rows, kv_width), BF), shape((HEAD, rows), F32)]
        + [shape((strip, rows), BF)],
        "vvvv",
        scratch=[
            pltpu.VMEM((width, rows), F32),
            pltpu.VMEM((2, HEAD, stretch), F32),
            pltpu.SemaphoreType.DMA((2,)),
        ],
        early=key_early,
    )
    (q,) = call(
        query_body,
        [normed, w_query, angle],
        "vcv",
        [shape((KV_HEADS, 2 * wide, PAIR), BF)],
        "c",
    )
    evens = [kv] + [hop(kv, "ctx", n, k) for k in range(2, n, 2)]
    strips = [normed_q] + [hop(normed_q, "ctx", n, k) for k in range(2, n, 2)]
    odds = hop(jnp.stack(after((q, strips), *evens)), "ctx", n, 1)
    strip_odds = hop(jnp.stack(strips), "ctx", n, 1)

    mlp_columns = 3 * hidden_width
    if small:
        block_shapes = [shape((n // 2, size, mlp_columns), BF)] * 2
    else:
        block_shapes = [shape((width, mlp_columns), BF), shape((8, 128), BF)]
    att_t, lse, mixed, even, odd, mixed_q, *pieces = call(
        functools.partial(forward_body, n, wt),
        [*evens, odds, None, stretch_order, q, tok, w_out, norm_mlp, w_gate, w_up, cot, w_down],
        "h" * (n // 2 + 1) + "msccc" + "c" + "cccc",
        [
            shape((width, rows), F32),
            shape((2 * KV_HEADS, 1, wide), F32),
            shape((rows, padded), F32),
        ]
        + block_shapes
        + [shape((piece, padded), F32)]
        + [shape((piece, padded), BF)] * (2 * wt),
        "ccc" + "ccc" + "c" * (2 * wt),
        scratch=[
            pltpu.VMEM((n * rows, kv_width), BF),
            pltpu.VMEM((2 * KV_HEADS, 1, wide), F32),
            pltpu.VMEM((2 * KV_HEADS, 1, wide), F32),
            pltpu.VMEM((2 * KV_HEADS, PAIR, wide), F32),
            pltpu.VMEM((rows, padded), F32),
            pltpu.VMEM((width, mlp_columns), F32),
            pltpu.SemaphoreType.DMA((2 * n,)),
        ],
        early=functools.partial(forward_early, n),
        micros=14,
    )
    part_in, out_parts = pieces[:wt], pieces[wt:]

    terms = [part_in[0]] + [hop(part_in[k], "wt", wt, k) for k in range(1, wt)]
    quarter = summed(terms).astype(BF)
    quarters = [quarter] + [hop(quarter, "wt", wt, k) for k in range(1, wt)]

    if small:
        pairs = pair_terms(even, odd, "ctx", n)
        quarters = after(pairs[0], *quarters)
        mlp_own = summed(scatter_terms(pairs, "ctx", n)).astype(BF)
    else:
        mlp_blocks = [lax.psum(even, "ctx")]

    columns = 2 * width + kv_width
    if small:
        out_blocks = [shape((n // 2, piece + strip // 2 + 8, kv_width), BF)] * 2
    else:
        out_blocks = [
            shape((strip, columns), BF),
            shape((8, 128 * n), BF),
            shape((n, piece, kv_width), BF),
        ]
    gm_q, dq_q, *message = call(
        functools.partial(backward_body, n, wt),
        [*quarters, None, stretch_order, norm_mlp, mixed, cot, w_out, att_t, lse, q, angle]
        + [first, inner, normed_q, w_query, wk, wv, *evens, odds, *strips, strip_odds],
        "c" * wt + "msc" + "c" * 7 + "c" * 6 + "h" * (n + 2),
        [shape((piece, padded), F32), shape((piece, padded), BF)] + out_blocks,
        "cc" + "v" * len(out_blocks),
        scratch=[
            pltpu.VMEM((rows, padded), F32),
            pltpu.VMEM((KV_HEADS, 2 * wide, PAIR), BF),
            pltpu.VMEM((2 * KV_HEADS, 1, wide), F32),
            pltpu.VMEM((n * rows, PAIR), F32),
            pltpu.VMEM((2, PAIR, wide), F32),
            pltpu.VMEM((width, rows), F32),
            pltpu.VMEM((strip, columns), F32),
            pltpu.VMEM((8, max(128 * n, 640)), F32),
            pltpu.VMEM((strip, n * rows), BF),
            pltpu.VMEM((width, kv_width), F32),
            pltpu.VMEM((n * rows, kv_width), BF),
            pltpu.SemaphoreType.DMA((2 * n,)),
            pltpu.SemaphoreType.DMA((2 * n,)),
        ],
        early=functools.partial(backward_early, n, wt),
        early_at=wt + 10,
        micros=17,
    )
    out_terms = [out_parts[0]] + [hop(out_parts[k], "wt", wt, k) for k in range(1, wt)]
    out_q = (mixed_q + summed(out_terms)).astype(BF)
    out_qs = [out_q] + [hop(out_q, "wt", wt, k) for k in range(1, wt)]
    if small:
        mlp_evens, mlp_odds = gather_blocks(mlp_own, "ctx", n)
        mlp_blocks = [*mlp_evens, mlp_odds]
        message[1] = after((mlp_evens, out_terms), message[1])
        parts = scatter_terms(pair_terms(message[0], message[1], "ctx", n), "ctx", n)
        parts = after(out_qs, *parts)
        own = summed([part[piece:] for part in parts]).astype(BF)
        owns = [own] + [hop(own, "wt", wt, k) for k in range(1, wt)]
    else:
        parts = [lax.psum_scatter(message[2].astype(F32), "ctx", scatter_dimension=0)]
        last_blocks = list(lax.psum((message[0], message[1]), "ctx"))
        last_blocks = [lax.all_gather(b, "wt", axis=0, tiled=i == 0) for i, b in enumerate(last_blocks)]
    (gt,) = call(
        functools.partial(finish_body, len(parts)),
        [*parts, None, norm_attn, tok, gm_q, dq_q, w_query, wk, wv],
        "v" * len(parts) + "mvcvvccc",
        [shape((piece, padded), BF)],
        "v",
        scratch=[pltpu.VMEM((rows, width), F32)],
        vmem=16,
        micros=2,
    )
    gts = [gt] + [hop(gt, "wt", wt, k) for k in range(1, wt)]
    grad_gate, grad_up, grad_down = call(
        functools.partial(mlp_join_body, n),
        [None, *mlp_blocks],
        "m" + "v" * len(mlp_blocks),
        [shape((width, hidden_width), F32)] * 3,
        "vvv",
        scratch=[pltpu.VMEM((width, mlp_columns), F32)],
        vmem=24,
        micros=2,
    )
    grad_tokens, output = call(
        functools.partial(token_join_body, wt),
        [None, *gts, *out_qs],
        "m" + "v" * (2 * wt),
        [shape((width, rows), F32), shape((width, rows), BF)],
        "vv",
        scratch=[pltpu.VMEM((rows, width), F32)],
        vmem=24,
        micros=2,
    )
    if small:
        last = jnp.stack(after(gt, *owns))
        last_evens = [last] + [hop(last, "ctx", n, k) for k in range(2, n, 2)]
        last = hop(after((grad_gate, gts), jnp.stack(last_evens)), "ctx", n, 1)
        last_blocks = [*last_evens, after(grad_tokens, last)]
    grad_query, grad_out, grad_key, grad_value, grad_norm_attn, grad_norm_mlp = call(
        functools.partial(join_body, n, wt),
        [None, norm_attn, *last_blocks],
        "mv" + "v" * len(last_blocks),
        [shape((width, width), F32)] * 2
        + [shape((kv_width // 2, width), F32)] * 2
        + [shape((width,), F32)] * 2,
        "vvvvvv",
        scratch=[
            pltpu.VMEM((width, columns), F32),
            pltpu.VMEM((wt, 8, max(128 * n, 640)), F32),
        ],
        vmem=24,
    )
    return (
        output.T,
        grad_tokens.T,
        grad_query,
        grad_key.T,
        grad_value.T,
        grad_out,
        grad_norm_attn,
        grad_norm_mlp,
        grad_gate,
        grad_up,
        grad_down.T,
    )


def solution(mesh):
    return jax.shard_map(
        functools.partial(local, mesh.shape["ctx"], mesh.shape["wt"]),
        mesh=mesh,
        in_specs=(
            P("ctx", None),
            P(),
            P(),
            P(),
            P(),
            P(),
            P(),
            P(None, "wt"),
            P(None, "wt"),
            P("wt", None),
            P(),
            P("ctx", None),
        ),
        out_specs=(
            P("ctx", None),
            P("ctx", None),
            P(),
            P(),
            P(),
            P(),
            P(),
            P(),
            P(None, "wt"),
            P(None, "wt"),
            P("wt", None),
        ),
        check_vma=False,
    )
```

```python
import functools

import jax
import jax.numpy as jnp
import numpy as np
from jax import lax
from jax.experimental import pallas as pl
from jax.experimental.pallas import tpu as pltpu
from jax.sharding import PartitionSpec as P

Q_HEADS = 9
KV_HEADS = 3
GROUP = 3
HEAD = 64
HALF = 32
PAIR = 2 * HEAD
EPSILON = 1e-05
THETA = 100000.0
NEGATIVE = -1e30
BF = jnp.bfloat16
F32 = jnp.float32
MIB = 1 << 20


def dot(left, right):
    return jnp.dot(left, right, preferred_element_type=F32)


def dot_nt(left, right):
    return lax.dot_general(left, right, (((1,), (1,)), ((), ())), preferred_element_type=F32)


def dot_tn(left, right):
    return lax.dot_general(left, right, (((0,), (0,)), ((), ())), preferred_element_type=F32)


def shape(dims, dtype):
    return jax.ShapeDtypeStruct(dims, dtype)


SPEC = {
    "v": pl.BlockSpec(memory_space=pltpu.VMEM),
    "s": pl.BlockSpec(memory_space=pltpu.SMEM),
    "h": pl.BlockSpec(memory_space=pltpu.HBM),
    "c": pl.BlockSpec(memory_space=pltpu.HBM),
}


class Fetched:
    def __init__(self, copy, ref):
        self.copy, self.ref, self.waited = copy, ref, False

    def get(self):
        if not self.waited:
            self.copy.wait()
            self.waited = True
        return self.ref


class Stored:
    def __init__(self, copy, ref):
        self.copy, self.ref, self.sent = copy, ref, False

    def send(self):
        self.copy.start()
        self.sent = True


def call(body, ins, in_kinds, outs, out_kinds, scratch=(), vmem=60, early=None, early_at=0, micros=3):
    real = [(a, kind) for a, kind in zip(ins, in_kinds) if kind != "m"]
    staged = [a for a, kind in real if kind == "c"]
    staged_out = [o for o, kind in zip(outs, out_kinds) if kind == "c"]
    count = len(staged) + len(staged_out)
    buffers = [pltpu.VMEM(a.shape, a.dtype) for a in staged + staged_out]
    if count:
        buffers.append(pltpu.SemaphoreType.DMA((count,)))

    def kernel(*refs):
        in_refs = iter(refs[: len(real)])
        out_refs = refs[len(real) : len(real) + len(outs)]
        own = refs[len(real) + len(outs) : len(refs) - len(buffers)]
        extra = refs[len(refs) - len(buffers) :]
        at = 0
        given, results = [], []
        for kind in in_kinds:
            place = (lax.axis_index("ctx"), lax.axis_index("wt")) if kind == "m" else next(in_refs)
            given.append(place)
        state = ()
        for i, kind in enumerate(in_kinds):
            if early is not None and i == early_at:
                state = (early(given, own),)
            if kind == "c":
                ref = given[i]
                copy = pltpu.make_async_copy(ref, extra[at], extra[-1].at[at])
                copy.start()
                given[i] = Fetched(copy, extra[at])
                at += 1
        for ref, kind in zip(out_refs, out_kinds):
            if kind == "c":
                ref = Stored(pltpu.make_async_copy(extra[at], ref, extra[-1].at[at]), extra[at])
                at += 1
            results.append(ref)
        body(given, results, own, *state)
        for item in given:
            if isinstance(item, Fetched):
                item.get()
        stored = [item for item in results if isinstance(item, Stored)]
        for item in stored:
            if not item.sent:
                item.send()
        for item in stored:
            item.copy.wait()

    return pl.pallas_call(
        kernel,
        out_shape=tuple(outs),
        in_specs=[SPEC[k] for _, k in real],
        out_specs=tuple(SPEC[k] for k in out_kinds),
        scratch_shapes=list(scratch) + buffers,
        compiler_params=pltpu.CompilerParams(vmem_limit_bytes=vmem * MIB),
        cost_estimate=pl.CostEstimate(flops=micros * 1_150_000_000, bytes_accessed=MIB, transcendentals=0),
    )(*[a for a, _ in real])


def angle_tables(n, stretch):
    rates = THETA ** (-np.arange(HALF, dtype=np.float64) / HALF)
    places = np.arange(2 * n * stretch, dtype=np.float64).reshape(2 * n, 1, stretch)
    angle = places * rates[None, :, None]
    turned = np.concatenate([np.cos(angle), np.sin(angle)], axis=1).astype(np.float32)
    sign = np.concatenate([np.ones(HALF), -np.ones(HALF)])
    lanes = np.concatenate([rates, rates])
    start = np.arange(2 * n)[:, None] * stretch * lanes[None, :]
    offset = np.arange(stretch)[:, None] * lanes[None, :]

    def widen(table, fill):
        return np.concatenate([table, np.full(table.shape, fill)], axis=1).astype(np.float32)

    first = np.stack([widen(np.cos(start), 1.0), widen(np.sin(start) * sign, 0.0)], axis=1)
    inner = np.stack([widen(np.cos(offset), 1.0), widen(np.sin(offset) * sign, 0.0)])
    return turned, first, inner


def row_of(ref):
    return ref[...].astype(F32).reshape(1, ref.shape[0])


def norm_scale(x, axis):
    return lax.rsqrt(jnp.mean(x * x, axis=axis, keepdims=True) + EPSILON)


def key_early(ins, scratch):
    meta, order, turned = ins[0], ins[1], ins[-1]
    copies = []
    for half in range(2):
        src = turned.at[order[0, 2 * meta[0] + half]]
        copies.append(pltpu.make_async_copy(src, scratch[1].at[half], scratch[2].at[half]))
        copies[-1].start()
    return copies


def key_body(ins, outs, scratch, copies):
    meta, order, gain, tok, wk, wv, turned = ins
    normed_out, kv_out, angle_out, normed_q = outs
    normed_s, angle_s, sems = scratch
    x = tok.get()[...].astype(F32)
    gain = jnp.broadcast_to(row_of(gain.get()), (8, x.shape[0])).T[:, 0:1]
    normed = (x * norm_scale(x, 0) * gain).astype(BF)
    normed_out[...] = normed
    normed_s[...] = normed.astype(F32)
    normed_q[...] = normed_s[span(meta[1], normed_q.shape[0]), :].astype(BF)
    for copy in copies:
        copy.wait()
    angle = jnp.concatenate([angle_s[0], angle_s[1]], axis=1)
    angle_out[...] = angle
    cos, sin = angle[:HALF], angle[HALF:]
    k = dot(wk.get()[...], normed)
    v = dot(wv.get()[...], normed)
    parts = []
    for g in range(KV_HEADS):
        a, b = k[g * HEAD : g * HEAD + HALF], k[g * HEAD + HALF : (g + 1) * HEAD]
        parts += [a * cos - b * sin, b * cos + a * sin, v[g * HEAD : (g + 1) * HEAD]]
    kv_out[...] = jnp.concatenate(parts, axis=0).T.astype(BF)


def query_body(ins, outs, scratch):
    normed, wq, angle = ins
    q_out = outs[0].ref
    rows = normed.shape[1]
    stretch = rows // 2
    q = dot(normed[...].astype(F32).T.astype(BF), wq.get()[...])
    table = angle[...].T
    cos = jnp.concatenate([table[:, :HALF]] * 2, axis=1)
    sin = jnp.concatenate([-table[:, HALF:], table[:, HALF:]], axis=1)
    zero = jnp.zeros((rows, HEAD), F32)
    for h in range(Q_HEADS):
        qh = q[:, h * HEAD : (h + 1) * HEAD]
        swapped = jnp.concatenate([qh[:, HALF:], qh[:, :HALF]], axis=1)
        qr = (qh * cos + swapped * sin) * HEAD**-0.5
        wide = jnp.concatenate([qr, zero], axis=1).astype(BF)
        g, hh = h // GROUP, h % GROUP
        for sel in range(2):
            at = (sel * GROUP + hh) * stretch
            q_out[g, at : at + stretch, :] = wide[sel * stretch : (sel + 1) * stretch]


def parts_of(n):
    low_group = min(n, 8)
    unit_group = max(d for d in range(1, 14) if (n + 1) % d == 0)
    return low_group, n // low_group, unit_group, (n + 1) // unit_group


def loop(count, body):
    if count == 1:
        body(0)
    else:
        lax.fori_loop(0, count, lambda i, c: (body(i), c)[1], 0)


def unit(u, c, n):
    is_low = u <= c
    sel = jnp.where(is_low, 0, 1)
    stretch_id = jnp.where(is_low, u, n - 1 + u - c)
    diagonal = jnp.logical_or(u == c, u == n)
    return is_low, sel, stretch_id, diagonal


def seen_mask(stretch, diagonal):
    keys = lax.broadcasted_iota(jnp.int32, (stretch, GROUP * stretch), 0)
    cols = lax.broadcasted_iota(jnp.int32, (stretch, GROUP * stretch), 1)
    queries = lax.bitwise_and(cols, stretch - 1)
    return jnp.logical_or(keys <= queries, jnp.logical_not(diagonal))


def span(index, size):
    return pl.ds(pl.multiple_of(index * size, size), size)


def natural_copies(n, me, order, evens, odds, to, sems, stretch, lanes=False):
    copies = []
    for k in range(n):
        low = order[0, 2 * lax.bitwise_xor(me, k)]
        src = evens[k // 2] if k % 2 == 0 else odds.at[k // 2]
        for half in range(2):
            at = span(low if half == 0 else 2 * n - 1 - low, stretch)
            cut = slice(half * stretch, (half + 1) * stretch)
            src_cut, to_cut = (src.at[:, cut], to.at[:, at]) if lanes else (src.at[cut], to.at[at])
            copies.append(pltpu.make_async_copy(src_cut, to_cut, sems.at[2 * k + half]))
    for copy in copies:
        copy.start()
    return copies


def forward_early(n, ins, scratch):
    evens, (odds, meta, order) = ins[: n // 2], ins[n // 2 : n // 2 + 3]
    return natural_copies(n, meta[0], order, evens, odds, scratch[0], scratch[-1], evens[0].shape[0] // 2)


def forward_body(n, wt, ins, outs, scratch, copies):
    odds, meta, order, q_in, tok, w_out, gain, w_gate, w_up, cot, w_down = ins[n // 2 :]
    att_t_out, lse_out, mixed_out, even, odd, mixed_q = outs[:6]
    pin_outs, out_parts = outs[6 : 6 + wt], outs[6 + wt :]
    kvn, m_s, l_s, o_s, part, grads, sems = scratch
    rows = tok.ref.shape[1]
    stretch = rows // 2
    wide = GROUP * stretch
    me = meta[0]
    for copy in copies:
        copy.wait()
    c = order[0, 2 * me]
    low_group, low_steps, unit_group, unit_steps = parts_of(n)
    q_ref = q_in.get()
    att_t = att_t_out.ref

    def one_head(g):
        lanes = span(g, PAIR)
        for sel in range(2):
            m_s[2 * g + sel] = jnp.full((1, wide), NEGATIVE, F32)
            l_s[2 * g + sel] = jnp.zeros((1, wide), F32)
            o_s[2 * g + sel] = jnp.zeros((PAIR, wide), F32)

        def low_step(i):
            keys = kvn[span(i, low_group * stretch), lanes]
            s = dot_nt(keys, q_ref[g, wide : 2 * wide, :])
            at = 2 * g + 1
            top = jnp.maximum(m_s[at], jnp.max(s, axis=0, keepdims=True))
            fade = jnp.exp(m_s[at] - top)
            p = jnp.exp(s - top)
            l_s[at] = l_s[at] * fade + jnp.sum(p, axis=0, keepdims=True)
            o_s[at] = o_s[at] * fade + dot_tn(keys, p.astype(BF))
            m_s[at] = top

        loop(low_steps, low_step)

        def unit_step(i):
            scores = []
            tops = [m_s[2 * g], m_s[2 * g + 1]]
            for j in range(unit_group):
                u = i * unit_group + j
                is_low, sel, st, diagonal = unit(u, c, n)
                keys = kvn[span(st, stretch), lanes]
                s = dot_nt(keys, q_ref[g, span(sel, wide), :])
                s = jnp.where(seen_mask(stretch, diagonal), s, NEGATIVE)
                peak = jnp.max(s, axis=0, keepdims=True)
                tops[0] = jnp.where(is_low, jnp.maximum(tops[0], peak), tops[0])
                tops[1] = jnp.where(is_low, tops[1], jnp.maximum(tops[1], peak))
                scores.append((s, keys, is_low, sel))
            sums = []
            for sel in range(2):
                at = 2 * g + sel
                fade = jnp.exp(m_s[at] - tops[sel])
                sums.append(l_s[at] * fade)
                o_s[at] = o_s[at] * fade
                m_s[at] = tops[sel]
            for s, keys, is_low, sel in scores:
                p = jnp.exp(s - jnp.where(is_low, tops[0], tops[1]))
                part = jnp.sum(p, axis=0, keepdims=True)
                sums[0] = sums[0] + jnp.where(is_low, part, 0.0)
                sums[1] = sums[1] + jnp.where(is_low, 0.0, part)
                o_s[2 * g + sel] += dot_tn(keys, p.astype(BF))
            for sel in range(2):
                l_s[2 * g + sel] = sums[sel]

        loop(unit_steps, unit_step)
        for sel in range(2):
            at = 2 * g + sel
            total = l_s[at]
            lse_out.ref[at] = m_s[at] + jnp.log(total)
            result = o_s[at][HEAD:, :] / total
            for hh in range(GROUP):
                att_t[span(g * GROUP + hh, HEAD), sel * stretch : (sel + 1) * stretch] = result[
                    :, hh * stretch : (hh + 1) * stretch
                ]

    loop(KV_HEADS, one_head)
    lse_out.send()
    att_t_out.send()
    att_low = att_t[...].T.astype(BF)
    mixed = tok.get()[...].astype(F32).T + dot(att_low, w_out.get()[...])
    width = mixed.shape[1]
    part[...] = jnp.zeros(part.shape, F32)
    part[:, :width] = mixed
    mixed_out.ref[...] = part[...]
    mixed_out.send()
    n2 = (mixed * norm_scale(mixed, -1) * row_of(gain.get())).astype(BF)
    gate = dot(n2, w_gate.get()[...])
    up = dot(n2, w_up.get()[...])
    sig = 1.0 / (1.0 + jnp.exp(-gate))
    silu = gate * sig
    hidden = (silu * up).astype(BF)
    grad_hidden = dot_tn(cot.get()[...], w_down.get()[...])
    gl = (grad_hidden * up * (sig * (1.0 + gate * (1.0 - sig)))).astype(BF)
    ul = (grad_hidden * silu).astype(BF)
    piece = rows // wt
    mixed_q.ref[...] = part[span(meta[1], piece), :]
    mixed_q.send()
    part[:, :width] = dot_nt(gl, w_gate.get()[...]) + dot_nt(ul, w_up.get()[...])
    for k in range(wt):
        pin_outs[k].ref[...] = part[span(lax.bitwise_xor(meta[1], k), piece), :].astype(BF)
        pin_outs[k].send()
    part[:, :width] = dot_nt(hidden, w_down.get()[...])
    for k in range(wt):
        out_parts[k].ref[...] = part[span(lax.bitwise_xor(meta[1], k), piece), :].astype(BF)
        out_parts[k].send()
    units = gl.shape[1]
    grads[:, :units] = dot_tn(n2, gl)
    grads[:, units : 2 * units] = dot_tn(n2, ul)
    grads[:, 2 * units :] = dot(cot.get()[...], hidden)
    if n > 8:
        even.ref[...] = grads[...].astype(BF)
        odd.ref[...] = jnp.zeros(odd.ref.shape, BF)
    else:
        size = grads.shape[0] // n
        for k in range(n):
            to = even.ref if k % 2 == 0 else odd.ref
            to[k // 2] = grads[span(lax.bitwise_xor(me, k), size), :].astype(BF)


def backward_early(n, wt, ins, scratch):
    meta, order = ins[wt], ins[wt + 1]
    blocks = ins[wt + 16 :]
    count = n // 2 + 1
    evens, odds = blocks[: count - 1], blocks[count - 1]
    strips, strip_odds = blocks[count : 2 * count - 1], blocks[2 * count - 1]
    stretch = evens[0].shape[0] // 2
    all_s, kv, sems, strip_sems = scratch[8], scratch[10], scratch[11], scratch[12]
    kv_copies = natural_copies(n, meta[0], order, evens, odds, kv, sems, stretch)
    return kv_copies, natural_copies(
        n, meta[0], order, strips, strip_odds, all_s, strip_sems, stretch, True
    )


def backward_body(n, wt, ins, outs, scratch, copies):
    kv_copies, strip_copies = copies
    quarters = ins[:wt]
    (meta, order, gain, mixed, cot, w_out, att_t, lse, q_in, angle) = ins[wt : wt + 10]
    (first, inner, normed, wq, wk, wv) = ins[wt + 10 : wt + 16]
    gm_out, dq_out, even, odd = outs[:4]
    gn_s, do_s, dl_s, dkv, dq_s, dq_t, grads, norm_s, all_s, w_s, kv = scratch[:11]
    rows = mixed.ref.shape[0]
    width = gain.ref.shape[0]
    stretch = rows // 2
    wide = GROUP * stretch
    me = meta[0]
    c = order[0, 2 * me]
    low_group, low_steps, unit_group, unit_steps = parts_of(n)
    piece = rows // wt
    for k in range(wt):
        gn_s[span(lax.bitwise_xor(meta[1], k), piece), :] = quarters[k].get()[...].astype(F32)
    x = mixed.get()[:, :width]
    gn = gn_s[:, :width]
    r = norm_scale(x, -1)
    xn = x * r
    e = gn * row_of(gain.get())
    gm = cot.get()[...].astype(F32).T + r * (e - xn * jnp.mean(e * xn, axis=-1, keepdims=True))
    gn_s[:, :width] = gm
    gm_out.ref[...] = gn_s[span(meta[1], piece), :]
    gm_out.send()
    norm_s[...] = jnp.zeros(norm_s.shape, F32)
    norm_s[1:2, :width] = jnp.sum(gn * xn, axis=0, keepdims=True)
    branch = gm.astype(BF)
    ga = dot_nt(branch, w_out.get()[...]).astype(BF).astype(F32)
    prod = ga.T * att_t.get()[...]
    zero = jnp.zeros((rows, HEAD), F32)
    for h in range(Q_HEADS):
        g, hh = h // GROUP, h % GROUP
        delta = jnp.sum(prod[h * HEAD : (h + 1) * HEAD, :], axis=0, keepdims=True)
        do = jnp.concatenate([zero, ga[:, h * HEAD : (h + 1) * HEAD]], axis=1).astype(BF)
        for sel in range(2):
            at = (sel * GROUP + hh) * stretch
            half = slice(sel * stretch, (sel + 1) * stretch)
            dl_s[2 * g + sel, :, hh * stretch : (hh + 1) * stretch] = delta[:, half]
            do_s[g, at : at + stretch, :] = do[half]
    strip = grads.shape[0]
    mine = span(meta[1], strip)
    grads[:, width : 2 * width] = dot(att_t.get()[mine, :].astype(BF), branch)
    lse, q_ref, angle = lse.get(), q_in.get(), angle.get()
    for copy in kv_copies:
        copy.wait()
    first, inner = first.get(), inner.get()
    chunk = 4
    low_chunks = lax.shift_right_logical(c, 2)
    key_ids = lax.broadcasted_iota(jnp.int32, (chunk * stretch, wide), 0)
    query_ids = lax.broadcasted_iota(jnp.int32, (chunk * stretch, wide), 1)
    query_ids = lax.bitwise_and(query_ids, stretch - 1)
    pre = kv
    lane_ids = lax.broadcasted_iota(jnp.int32, (stretch, PAIR), 1)

    def one_head(g):
        lanes = span(g, PAIR)
        dkv[n * stretch :, :] = jnp.zeros((n * stretch, PAIR), F32)
        dq_s[...] = jnp.zeros(dq_s.shape, F32)

        def low_step(i):
            at = span(i, low_group * stretch)
            keys = kv[at, lanes]
            q = q_ref[g, wide : 2 * wide, :]
            do = do_s[g, wide : 2 * wide, :]
            p = jnp.exp(dot_nt(keys, q) - lse[2 * g + 1])
            ds = (p * (dot_nt(keys, do) - dl_s[2 * g + 1])).astype(BF)
            dkv[at, :] = dot(ds, q) + dot(p.astype(BF), do)
            dq_s[1] += dot_tn(keys, ds)

        loop(low_steps, low_step)

        def unit_step(u):
            is_low = u <= low_chunks
            sel = jnp.where(is_low, 0, 1)
            low_key = jnp.where(is_low, u, u - low_chunks - 1 + n // chunk) * (chunk * stretch)
            at = pl.ds(pl.multiple_of(low_key, chunk * stretch), chunk * stretch)
            keys = kv[at, lanes]
            q = q_ref[g, span(sel, wide), :]
            do = do_s[g, span(sel, wide), :]
            p = jnp.exp(dot_nt(keys, q) - lse[2 * g + sel])
            ahead = low_key - jnp.where(is_low, c, 2 * n - 1 - c) * stretch
            p = jnp.where(key_ids + ahead <= query_ids, p, 0.0)
            ds = (p * (dot_nt(keys, do) - dl_s[2 * g + sel])).astype(BF)
            dkv[at, :] += dot(ds, q) + dot(p.astype(BF), do)
            dq_s[sel] += dot_tn(keys, ds)

        if n <= 8:
            for u in range(n // chunk + 1):
                unit_step(u)
        else:
            loop(n // chunk + 1, unit_step)

        def turn(i):
            ct, st = inner[0], inner[1]
            cs, ss = first[i, 0:1, :], first[i, 1:2, :]
            part = dkv[span(i, stretch), :]
            back = pltpu.roll(part, PAIR - HALF, 1)
            ahead = pltpu.roll(part, HALF, 1)
            swapped = jnp.where(lane_ids < HALF, back, ahead)
            result = part * (ct * cs - st * ss) + swapped * (st * cs + ct * ss)
            pre[span(i, stretch), lanes] = result.astype(BF)

        if n <= 8:
            for i in range(2 * n):
                turn(i)
        else:
            loop(2 * n, turn)
        for sel in range(2):
            half = slice(sel * stretch, (sel + 1) * stretch)
            cos, sin = angle[:HALF, half], angle[HALF:, half]
            for hh in range(GROUP):
                dq = dq_s[sel, :HEAD, hh * stretch : (hh + 1) * stretch] * HEAD**-0.5
                a, b = dq[:HALF], dq[HALF:]
                turned = jnp.concatenate([a * cos + b * sin, b * cos - a * sin], axis=0)
                dq_t[span(g * GROUP + hh, HEAD), half] = turned

    loop(KV_HEADS, one_head)
    dq = dq_t[...].T.astype(BF)
    gn_s[:, :width] = dq.astype(F32)
    dq_out.ref[...] = gn_s[span(meta[1], piece), :].astype(BF)
    dq_out.send()
    grads[:, :width] = dot(normed.get()[...], dq)
    for copy in strip_copies:
        copy.wait()
    grads[:, 2 * width :] = dot(all_s[...], pre[...])
    wk, wv = wk.get()[...].astype(F32), wv.get()[...].astype(F32)
    chunks = []
    for g in range(KV_HEADS):
        chunks += [wk[g * HEAD : (g + 1) * HEAD], wv[g * HEAD : (g + 1) * HEAD]]
    w_s[...] = jnp.concatenate(chunks, axis=0).T
    sums = jnp.sum(grads[:, :width] * wq.get()[mine, :].astype(F32), axis=1, keepdims=True)
    sums = sums + jnp.sum(grads[:, 2 * width :] * w_s[mine, :], axis=1, keepdims=True)
    norm_s[0:1, :strip] = jnp.broadcast_to(sums, (strip, 128)).T[0:1, :]
    quarter = meta[1] * piece
    upper = quarter >= stretch
    inside = jnp.where(upper, quarter - stretch, quarter)

    def rows_for(who):
        low = order[0, 2 * who]
        st = jnp.where(upper, 2 * n - 1 - low, low)
        return pre[pl.ds(pl.multiple_of(st * stretch + inside, piece), piece), :]

    if n > 8:
        even[...] = grads[...].astype(BF)
        odd[...] = norm_s[...].astype(BF)
        for k in range(n):
            outs[4][k] = rows_for(k)
        return
    for k in range(n):
        who = lax.bitwise_xor(me, k)
        to = even if k % 2 == 0 else odd
        to[k // 2, :piece, :] = rows_for(who)
        block = grads[block_rows(strip, who), block_lanes(who)]
        cut = norm_s[:, span(who, 128)]
        tail = jnp.concatenate([cut, jnp.zeros((8, block.shape[1] - 128), F32)], axis=1)
        to[k // 2, piece:, :] = jnp.concatenate([block, tail], axis=0).astype(BF)


def block_rows(strip, who):
    size = strip // 2
    return pl.ds(pl.multiple_of(lax.shift_right_logical(who, 2) * size, size), size)


def block_lanes(who):
    return span(lax.bitwise_and(who, 3), KV_HEADS * PAIR)


def finish_body(count, ins, outs, scratch):
    terms = ins[:count]
    meta, gain, tok, gm, dq, wq, wk, wv = ins[count:]
    (gt_out,) = outs
    (x_s,) = scratch
    piece = gt_out.shape[0]
    total = terms[0][:piece, :].astype(F32)
    for term in terms[1:]:
        total = total + term[:piece, :].astype(F32)
    mine = span(meta[1], piece)
    x_s[...] = tok.get()[...].astype(F32).T
    x = x_s[mine, :]
    dk, dv = [], []
    for g in range(KV_HEADS):
        dk.append(total[:, g * PAIR : g * PAIR + HEAD])
        dv.append(total[:, g * PAIR + HEAD : (g + 1) * PAIR])
    dk = jnp.concatenate(dk, axis=1).astype(BF)
    dv = jnp.concatenate(dv, axis=1).astype(BF)
    width = gain.shape[0]
    gn = dot_nt(dq[:, :width], wq.get()[...])
    gn = gn + dot(dk, wk.get()[...]) + dot(dv, wv.get()[...])
    r = norm_scale(x, -1)
    xn = x * r
    e = gn * row_of(gain)
    result = gm[:, :width] + r * (e - xn * jnp.mean(e * xn, axis=-1, keepdims=True))
    gt_out[:, :width] = result.astype(BF)
    gt_out[:, width:] = jnp.zeros((piece, gt_out.shape[1] - width), BF)


def token_join_body(wt, ins, outs, scratch):
    meta = ins[0]
    (rows_s,) = scratch
    for i in range(2):
        quarters = ins[1 + i * wt : 1 + (i + 1) * wt]
        for k in range(wt):
            at = span(lax.bitwise_xor(meta[1], k), quarters[0].shape[0])
            rows_s[at, :] = quarters[k][:, : rows_s.shape[1]].astype(F32)
        outs[i][...] = rows_s[...].T.astype(outs[i].dtype)


def mlp_join_body(n, ins, outs, scratch):
    meta, blocks = ins[0], ins[1:]
    (grads,) = scratch
    if n > 8:
        grads[...] = blocks[0][...].astype(F32)
    else:
        size = grads.shape[0] // n
        for k in range(n):
            block = blocks[k // 2][...] if k % 2 == 0 else blocks[-1][k // 2]
            grads[span(lax.bitwise_xor(meta[0], k), size), :] = block.astype(F32)
    width = outs[0].shape[1]
    for i in range(3):
        outs[i][...] = grads[:, i * width : (i + 1) * width]


def join_body(n, wt, ins, outs, scratch):
    meta, gain = ins[:2]
    blocks = ins[2:]
    gq, go, gk, gv, norm_attn, norm_mlp = outs
    grads, norm_s = scratch
    width = gq.shape[0]
    strip = width // wt
    norm_s[...] = jnp.zeros(norm_s.shape, F32)
    if n > 8:
        grads[...] = blocks[0][...].astype(F32)
        norm_s[...] = blocks[1][...].astype(F32)
    else:
        size = strip // 2
        for k in range(n):
            who = lax.bitwise_xor(meta[0], k)
            for kz in range(wt):
                lane = lax.bitwise_xor(meta[1], kz)
                block = blocks[k // 2][kz] if k % 2 == 0 else blocks[-1][k // 2, kz]
                block = block.astype(F32)
                at = lane * strip + lax.shift_right_logical(who, 2) * size
                grads[pl.ds(pl.multiple_of(at, size), size), block_lanes(who)] = block[:size]
                norm_s[lane, :, span(who, 128)] = block[size:, :128]
    gq[...] = grads[:, :width]
    go[...] = grads[:, width : 2 * width]
    both = grads[:, 2 * width :].T
    for g in range(KV_HEADS):
        gk[g * HEAD : (g + 1) * HEAD, :] = both[g * PAIR : g * PAIR + HEAD]
        gv[g * HEAD : (g + 1) * HEAD, :] = both[g * PAIR + HEAD : (g + 1) * PAIR]
    attn = jnp.concatenate([norm_s[lane, 0:1, :strip] for lane in range(wt)], axis=1)
    norm_attn[...] = (attn / row_of(gain)).reshape(width)
    norm_mlp[...] = norm_s[0, 1:2, :width].reshape(width)


def hop(x, axis, size, k):
    return lax.ppermute(x, axis, [(i, i ^ k) for i in range(size)])


def gather_blocks(x, axis, size):
    evens = [x] + [hop(x, axis, size, k) for k in range(2, size, 2)]
    odds = hop(jnp.stack(evens), axis, size, 1)
    return evens, odds


def pair_terms(even, odd, axis, size):
    got = hop(odd, axis, size, 1).astype(F32)
    pairs = [even[i].astype(F32) + got[i] for i in range(size // 2)]
    return pairs[:1] + [pair.astype(BF) for pair in pairs[1:]]


def scatter_terms(pairs, axis, size):
    return pairs[:1] + [hop(pairs[i], axis, size, 2 * i) for i in range(1, size // 2)]


def summed(terms):
    total = terms[0].astype(F32)
    for term in terms[1:]:
        total = total + term.astype(F32)
    return total


def after(dep, *arrays):
    held = lax.optimization_barrier((dep,) + arrays)
    return list(held[1:]) if len(arrays) > 1 else held[1]


def local(
    n,
    wt,
    tokens,
    w_query,
    w_key,
    w_value,
    w_out,
    norm_attn,
    norm_mlp,
    w_gate,
    w_up,
    w_down,
    stretch_order,
    cotangent,
):
    rows, width = tokens.shape
    stretch = rows // 2
    wide = GROUP * stretch
    kv_width = KV_HEADS * PAIR
    hidden_width = w_gate.shape[1]
    piece = rows // wt
    size = width // n
    strip = width // wt
    small = n <= 8
    padded = -(-width // 128) * 128
    turned, first, inner = (jnp.asarray(t) for t in angle_tables(n, stretch))
    tok, cot, wk, wv, w_down = tokens.T, cotangent.T, w_key.T, w_value.T, w_down.T

    normed, kv, angle, normed_q = call(
        key_body,
        [None, stretch_order, norm_attn, tok, wk, wv, turned],
        "mscccch",
        [shape((width, rows), BF), shape((rows, kv_width), BF), shape((HEAD, rows), F32)]
        + [shape((strip, rows), BF)],
        "vvvv",
        scratch=[
            pltpu.VMEM((width, rows), F32),
            pltpu.VMEM((2, HEAD, stretch), F32),
            pltpu.SemaphoreType.DMA((2,)),
        ],
        early=key_early,
    )
    (q,) = call(
        query_body,
        [normed, w_query, angle],
        "vcv",
        [shape((KV_HEADS, 2 * wide, PAIR), BF)],
        "c",
    )
    evens = [kv] + [hop(kv, "ctx", n, k) for k in range(2, n, 2)]
    strips = [normed_q] + [hop(normed_q, "ctx", n, k) for k in range(2, n, 2)]
    odds = hop(jnp.stack(after(q, *evens)), "ctx", n, 1)

    mlp_columns = 3 * hidden_width
    if small:
        block_shapes = [shape((n // 2, size, mlp_columns), BF)] * 2
    else:
        block_shapes = [shape((width, mlp_columns), BF), shape((8, 128), BF)]
    results = call(
        functools.partial(forward_body, n, wt),
        [*evens, odds, None, stretch_order, q, tok, w_out, norm_mlp, w_gate, w_up, cot, w_down],
        "h" * (n // 2 + 1) + "msccc" + "c" + "cccc",
        [
            shape((width, rows), F32),
            shape((2 * KV_HEADS, 1, wide), F32),
            shape((rows, padded), F32),
        ]
        + block_shapes
        + [shape((piece, padded), F32)]
        + [shape((piece, padded), BF)] * (2 * wt),
        "ccc" + "ccc" + "c" * (2 * wt),
        scratch=[
            pltpu.VMEM((n * rows, kv_width), BF),
            pltpu.VMEM((2 * KV_HEADS, 1, wide), F32),
            pltpu.VMEM((2 * KV_HEADS, 1, wide), F32),
            pltpu.VMEM((2 * KV_HEADS, PAIR, wide), F32),
            pltpu.VMEM((rows, padded), F32),
            pltpu.VMEM((width, mlp_columns), F32),
            pltpu.SemaphoreType.DMA((2 * n,)),
        ],
        early=functools.partial(forward_early, n),
        micros=14,
    )
    att_t, lse, mixed, even, odd, mixed_q, *pieces = after(strips, *results)
    part_in, out_parts = pieces[:wt], pieces[wt:]
    strip_odds = hop(jnp.stack(strips), "ctx", n, 1)

    terms = [part_in[0]] + [hop(part_in[k], "wt", wt, k) for k in range(1, wt)]
    quarter = summed(terms).astype(BF)
    quarters = [quarter] + [hop(quarter, "wt", wt, k) for k in range(1, wt)]

    if small:
        pairs = pair_terms(even, odd, "ctx", n)
        quarters = after(pairs[0], *quarters)
        mlp_own = summed(scatter_terms(pairs, "ctx", n)).astype(BF)
    else:
        mlp_blocks = [lax.psum(even, "ctx")]

    columns = 2 * width + kv_width
    if small:
        out_blocks = [shape((n // 2, piece + strip // 2 + 8, kv_width), BF)] * 2
    else:
        out_blocks = [
            shape((strip, columns), BF),
            shape((8, 128 * n), BF),
            shape((n, piece, kv_width), BF),
        ]
    gm_q, dq_q, *message = call(
        functools.partial(backward_body, n, wt),
        [*quarters, None, stretch_order, norm_mlp, mixed, cot, w_out, att_t, lse, q, angle]
        + [first, inner, normed_q, w_query, wk, wv, *evens, odds, *strips, strip_odds],
        "c" * wt + "msc" + "c" * 7 + "c" * 6 + "h" * (n + 2),
        [shape((piece, padded), F32), shape((piece, padded), BF)] + out_blocks,
        "cc" + "v" * len(out_blocks),
        scratch=[
            pltpu.VMEM((rows, padded), F32),
            pltpu.VMEM((KV_HEADS, 2 * wide, PAIR), BF),
            pltpu.VMEM((2 * KV_HEADS, 1, wide), F32),
            pltpu.VMEM((n * rows, PAIR), F32),
            pltpu.VMEM((2, PAIR, wide), F32),
            pltpu.VMEM((width, rows), F32),
            pltpu.VMEM((strip, columns), F32),
            pltpu.VMEM((8, max(128 * n, 640)), F32),
            pltpu.VMEM((strip, n * rows), BF),
            pltpu.VMEM((width, kv_width), F32),
            pltpu.VMEM((n * rows, kv_width), BF),
            pltpu.SemaphoreType.DMA((2 * n,)),
            pltpu.SemaphoreType.DMA((2 * n,)),
        ],
        early=functools.partial(backward_early, n, wt),
        early_at=wt + 10,
        micros=17,
    )
    out_terms = [out_parts[0]] + [hop(out_parts[k], "wt", wt, k) for k in range(1, wt)]
    out_q = (mixed_q + summed(out_terms)).astype(BF)
    out_qs = [out_q] + [hop(out_q, "wt", wt, k) for k in range(1, wt)]
    if small:
        mlp_evens, mlp_odds = gather_blocks(mlp_own, "ctx", n)
        mlp_blocks = [*mlp_evens, mlp_odds]
        message[1] = after((mlp_evens, out_terms), message[1])
        parts = scatter_terms(pair_terms(message[0], message[1], "ctx", n), "ctx", n)
        parts = after(out_qs, *parts)
        own = summed([part[piece:] for part in parts]).astype(BF)
        owns = [own] + [hop(own, "wt", wt, k) for k in range(1, wt)]
    else:
        parts = [lax.psum_scatter(message[2].astype(F32), "ctx", scatter_dimension=0)]
        last_blocks = list(lax.psum((message[0], message[1]), "ctx"))
        last_blocks = [lax.all_gather(b, "wt", axis=0, tiled=i == 0) for i, b in enumerate(last_blocks)]
    (gt,) = call(
        functools.partial(finish_body, len(parts)),
        [*parts, None, norm_attn, tok, gm_q, dq_q, w_query, wk, wv],
        "v" * len(parts) + "mvcvvccc",
        [shape((piece, padded), BF)],
        "v",
        scratch=[pltpu.VMEM((rows, width), F32)],
        vmem=16,
        micros=2,
    )
    gts = [gt] + [hop(gt, "wt", wt, k) for k in range(1, wt)]
    grad_gate, grad_up, grad_down = call(
        functools.partial(mlp_join_body, n),
        [None, *mlp_blocks],
        "m" + "v" * len(mlp_blocks),
        [shape((width, hidden_width), F32)] * 3,
        "vvv",
        scratch=[pltpu.VMEM((width, mlp_columns), F32)],
        vmem=24,
        micros=2,
    )
    grad_tokens, output = call(
        functools.partial(token_join_body, wt),
        [None, *gts, *out_qs],
        "m" + "v" * (2 * wt),
        [shape((width, rows), F32), shape((width, rows), BF)],
        "vv",
        scratch=[pltpu.VMEM((rows, width), F32)],
        vmem=24,
        micros=2,
    )
    if small:
        last = jnp.stack(after(gt, *owns))
        last_evens = [last] + [hop(last, "ctx", n, k) for k in range(2, n, 2)]
        last = hop(after((grad_gate, gts), jnp.stack(last_evens)), "ctx", n, 1)
        last_blocks = [*last_evens, after(grad_tokens, last)]
    grad_query, grad_out, grad_key, grad_value, grad_norm_attn, grad_norm_mlp = call(
        functools.partial(join_body, n, wt),
        [None, norm_attn, *last_blocks],
        "mv" + "v" * len(last_blocks),
        [shape((width, width), F32)] * 2
        + [shape((kv_width // 2, width), F32)] * 2
        + [shape((width,), F32)] * 2,
        "vvvvvv",
        scratch=[
            pltpu.VMEM((width, columns), F32),
            pltpu.VMEM((wt, 8, max(128 * n, 640)), F32),
        ],
        vmem=24,
    )
    return (
        output.T,
        grad_tokens.T,
        grad_query,
        grad_key.T,
        grad_value.T,
        grad_out,
        grad_norm_attn,
        grad_norm_mlp,
        grad_gate,
        grad_up,
        grad_down.T,
    )


def solution(mesh):
    return jax.shard_map(
        functools.partial(local, mesh.shape["ctx"], mesh.shape["wt"]),
        mesh=mesh,
        in_specs=(
            P("ctx", None),
            P(),
            P(),
            P(),
            P(),
            P(),
            P(),
            P(None, "wt"),
            P(None, "wt"),
            P("wt", None),
            P(),
            P("ctx", None),
        ),
        out_specs=(
            P("ctx", None),
            P("ctx", None),
            P(),
            P(),
            P(),
            P(),
            P(),
            P(),
            P(None, "wt"),
            P(None, "wt"),
            P("wt", None),
        ),
        check_vma=False,
    )
```

```python
import functools

import jax
import jax.numpy as jnp
import numpy as np
from jax import lax
from jax.experimental import pallas as pl
from jax.experimental.pallas import tpu as pltpu
from jax.sharding import PartitionSpec as P

Q_HEADS = 9
KV_HEADS = 3
GROUP = 3
HEAD = 64
HALF = 32
PAIR = 2 * HEAD
EPSILON = 1e-05
THETA = 100000.0
NEGATIVE = -1e30
BF = jnp.bfloat16
F32 = jnp.float32
MIB = 1 << 20


def dot(left, right):
    return jnp.dot(left, right, preferred_element_type=F32)


def dot_nt(left, right):
    return lax.dot_general(left, right, (((1,), (1,)), ((), ())), preferred_element_type=F32)


def dot_tn(left, right):
    return lax.dot_general(left, right, (((0,), (0,)), ((), ())), preferred_element_type=F32)


def shape(dims, dtype):
    return jax.ShapeDtypeStruct(dims, dtype)


SPEC = {
    "v": pl.BlockSpec(memory_space=pltpu.VMEM),
    "s": pl.BlockSpec(memory_space=pltpu.SMEM),
    "h": pl.BlockSpec(memory_space=pltpu.HBM),
    "c": pl.BlockSpec(memory_space=pltpu.HBM),
}


class Fetched:
    def __init__(self, copy, ref):
        self.copy, self.ref, self.waited = copy, ref, False

    def get(self):
        if not self.waited:
            self.copy.wait()
            self.waited = True
        return self.ref


class Stored:
    def __init__(self, copy, ref):
        self.copy, self.ref, self.sent = copy, ref, False

    def send(self):
        self.copy.start()
        self.sent = True


def call(body, ins, in_kinds, outs, out_kinds, scratch=(), vmem=60, early=None, early_at=0, micros=3):
    real = [(a, kind) for a, kind in zip(ins, in_kinds) if kind != "m"]
    staged = [a for a, kind in real if kind == "c"]
    staged_out = [o for o, kind in zip(outs, out_kinds) if kind == "c"]
    count = len(staged) + len(staged_out)
    buffers = [pltpu.VMEM(a.shape, a.dtype) for a in staged + staged_out]
    if count:
        buffers.append(pltpu.SemaphoreType.DMA((count,)))

    def kernel(*refs):
        in_refs = iter(refs[: len(real)])
        out_refs = refs[len(real) : len(real) + len(outs)]
        own = refs[len(real) + len(outs) : len(refs) - len(buffers)]
        extra = refs[len(refs) - len(buffers) :]
        at = 0
        given, results = [], []
        for kind in in_kinds:
            place = (lax.axis_index("ctx"), lax.axis_index("wt")) if kind == "m" else next(in_refs)
            given.append(place)
        state = ()
        for i, kind in enumerate(in_kinds):
            if early is not None and i == early_at:
                state = (early(given, own),)
            if kind == "c":
                ref = given[i]
                copy = pltpu.make_async_copy(ref, extra[at], extra[-1].at[at])
                copy.start()
                given[i] = Fetched(copy, extra[at])
                at += 1
        for ref, kind in zip(out_refs, out_kinds):
            if kind == "c":
                ref = Stored(pltpu.make_async_copy(extra[at], ref, extra[-1].at[at]), extra[at])
                at += 1
            results.append(ref)
        body(given, results, own, *state)
        for item in given:
            if isinstance(item, Fetched):
                item.get()
        stored = [item for item in results if isinstance(item, Stored)]
        for item in stored:
            if not item.sent:
                item.send()
        for item in stored:
            item.copy.wait()

    return pl.pallas_call(
        kernel,
        out_shape=tuple(outs),
        in_specs=[SPEC[k] for _, k in real],
        out_specs=tuple(SPEC[k] for k in out_kinds),
        scratch_shapes=list(scratch) + buffers,
        compiler_params=pltpu.CompilerParams(vmem_limit_bytes=vmem * MIB),
        cost_estimate=pl.CostEstimate(flops=micros * 1_150_000_000, bytes_accessed=MIB, transcendentals=0),
    )(*[a for a, _ in real])


def angle_tables(n, stretch):
    rates = THETA ** (-np.arange(HALF, dtype=np.float64) / HALF)
    places = np.arange(2 * n * stretch, dtype=np.float64).reshape(2 * n, 1, stretch)
    angle = places * rates[None, :, None]
    turned = np.concatenate([np.cos(angle), np.sin(angle)], axis=1).astype(np.float32)
    sign = np.concatenate([np.ones(HALF), -np.ones(HALF)])
    lanes = np.concatenate([rates, rates])
    start = np.arange(2 * n)[:, None] * stretch * lanes[None, :]
    offset = np.arange(stretch)[:, None] * lanes[None, :]

    def widen(table, fill):
        return np.concatenate([table, np.full(table.shape, fill)], axis=1).astype(np.float32)

    first = np.stack([widen(np.cos(start), 1.0), widen(np.sin(start) * sign, 0.0)], axis=1)
    inner = np.stack([widen(np.cos(offset), 1.0), widen(np.sin(offset) * sign, 0.0)])
    return turned, first, inner


def row_of(ref):
    return ref[...].astype(F32).reshape(1, ref.shape[0])


def norm_scale(x, axis):
    return lax.rsqrt(jnp.mean(x * x, axis=axis, keepdims=True) + EPSILON)


def key_early(ins, scratch):
    meta, order, turned = ins[0], ins[1], ins[-1]
    copies = []
    for half in range(2):
        src = turned.at[order[0, 2 * meta[0] + half]]
        copies.append(pltpu.make_async_copy(src, scratch[1].at[half], scratch[2].at[half]))
        copies[-1].start()
    return copies


def key_body(ins, outs, scratch, copies):
    meta, order, gain, tok, wk, wv, turned = ins
    normed_out, kv_out, angle_out, normed_q = outs
    normed_s, angle_s, sems = scratch
    x = tok.get()[...].astype(F32)
    gain = jnp.broadcast_to(row_of(gain.get()), (8, x.shape[0])).T[:, 0:1]
    normed = (x * norm_scale(x, 0) * gain).astype(BF)
    normed_out[...] = normed
    normed_s[...] = normed.astype(F32)
    normed_q[...] = normed_s[span(meta[1], normed_q.shape[0]), :].astype(BF)
    for copy in copies:
        copy.wait()
    angle = jnp.concatenate([angle_s[0], angle_s[1]], axis=1)
    angle_out[...] = angle
    cos, sin = angle[:HALF], angle[HALF:]
    k = dot(wk.get()[...], normed)
    v = dot(wv.get()[...], normed)
    parts = []
    for g in range(KV_HEADS):
        a, b = k[g * HEAD : g * HEAD + HALF], k[g * HEAD + HALF : (g + 1) * HEAD]
        parts += [a * cos - b * sin, b * cos + a * sin, v[g * HEAD : (g + 1) * HEAD]]
    kv_out[...] = jnp.concatenate(parts, axis=0).T.astype(BF)


def query_body(ins, outs, scratch):
    normed, wq, angle = ins
    q_out = outs[0].ref
    rows = normed.shape[1]
    stretch = rows // 2
    q = dot(normed[...].astype(F32).T.astype(BF), wq.get()[...])
    table = angle[...].T
    cos = jnp.concatenate([table[:, :HALF]] * 2, axis=1)
    sin = jnp.concatenate([-table[:, HALF:], table[:, HALF:]], axis=1)
    zero = jnp.zeros((rows, HEAD), F32)
    for h in range(Q_HEADS):
        qh = q[:, h * HEAD : (h + 1) * HEAD]
        swapped = jnp.concatenate([qh[:, HALF:], qh[:, :HALF]], axis=1)
        qr = (qh * cos + swapped * sin) * HEAD**-0.5
        wide = jnp.concatenate([qr, zero], axis=1).astype(BF)
        g, hh = h // GROUP, h % GROUP
        for sel in range(2):
            at = (sel * GROUP + hh) * stretch
            q_out[g, at : at + stretch, :] = wide[sel * stretch : (sel + 1) * stretch]


def parts_of(n):
    low_group = min(n, 8)
    unit_group = max(d for d in range(1, 14) if (n + 1) % d == 0)
    return low_group, n // low_group, unit_group, (n + 1) // unit_group


def loop(count, body):
    if count == 1:
        body(0)
    else:
        lax.fori_loop(0, count, lambda i, c: (body(i), c)[1], 0)


def unit(u, c, n):
    is_low = u <= c
    sel = jnp.where(is_low, 0, 1)
    stretch_id = jnp.where(is_low, u, n - 1 + u - c)
    diagonal = jnp.logical_or(u == c, u == n)
    return is_low, sel, stretch_id, diagonal


def seen_mask(stretch, diagonal):
    keys = lax.broadcasted_iota(jnp.int32, (stretch, GROUP * stretch), 0)
    cols = lax.broadcasted_iota(jnp.int32, (stretch, GROUP * stretch), 1)
    queries = lax.bitwise_and(cols, stretch - 1)
    return jnp.logical_or(keys <= queries, jnp.logical_not(diagonal))


def span(index, size):
    return pl.ds(pl.multiple_of(index * size, size), size)


def natural_copies(n, me, order, evens, odds, to, sems, stretch, lanes=False):
    copies = []
    for k in range(n):
        low = order[0, 2 * lax.bitwise_xor(me, k)]
        src = evens[k // 2] if k % 2 == 0 else odds.at[k // 2]
        for half in range(2):
            at = span(low if half == 0 else 2 * n - 1 - low, stretch)
            cut = slice(half * stretch, (half + 1) * stretch)
            src_cut, to_cut = (src.at[:, cut], to.at[:, at]) if lanes else (src.at[cut], to.at[at])
            copies.append(pltpu.make_async_copy(src_cut, to_cut, sems.at[2 * k + half]))
    for copy in copies:
        copy.start()
    return copies


def forward_early(n, ins, scratch):
    evens, (odds, meta, order) = ins[: n // 2], ins[n // 2 : n // 2 + 3]
    return natural_copies(n, meta[0], order, evens, odds, scratch[0], scratch[-1], evens[0].shape[0] // 2)


def forward_body(n, wt, ins, outs, scratch, copies):
    odds, meta, order, q_in, tok, w_out, gain, w_gate, w_up, cot, w_down = ins[n // 2 :]
    att_t_out, lse_out, mixed_out, even, odd, mixed_q = outs[:6]
    pin_outs, out_parts = outs[6 : 6 + wt], outs[6 + wt :]
    kvn, m_s, l_s, o_s, part, grads, sems = scratch
    rows = tok.ref.shape[1]
    stretch = rows // 2
    wide = GROUP * stretch
    me = meta[0]
    for copy in copies:
        copy.wait()
    c = order[0, 2 * me]
    low_group, low_steps, unit_group, unit_steps = parts_of(n)
    q_ref = q_in.get()
    att_t = att_t_out.ref

    def one_head(g):
        lanes = span(g, PAIR)
        for sel in range(2):
            m_s[2 * g + sel] = jnp.full((1, wide), NEGATIVE, F32)
            l_s[2 * g + sel] = jnp.zeros((1, wide), F32)
            o_s[2 * g + sel] = jnp.zeros((PAIR, wide), F32)

        def low_step(i):
            keys = kvn[span(i, low_group * stretch), lanes]
            s = dot_nt(keys, q_ref[g, wide : 2 * wide, :])
            at = 2 * g + 1
            top = jnp.maximum(m_s[at], jnp.max(s, axis=0, keepdims=True))
            fade = jnp.exp(m_s[at] - top)
            p = jnp.exp(s - top)
            l_s[at] = l_s[at] * fade + jnp.sum(p, axis=0, keepdims=True)
            o_s[at] = o_s[at] * fade + dot_tn(keys, p.astype(BF))
            m_s[at] = top

        loop(low_steps, low_step)

        def unit_step(i):
            scores = []
            tops = [m_s[2 * g], m_s[2 * g + 1]]
            for j in range(unit_group):
                u = i * unit_group + j
                is_low, sel, st, diagonal = unit(u, c, n)
                keys = kvn[span(st, stretch), lanes]
                s = dot_nt(keys, q_ref[g, span(sel, wide), :])
                s = jnp.where(seen_mask(stretch, diagonal), s, NEGATIVE)
                peak = jnp.max(s, axis=0, keepdims=True)
                tops[0] = jnp.where(is_low, jnp.maximum(tops[0], peak), tops[0])
                tops[1] = jnp.where(is_low, tops[1], jnp.maximum(tops[1], peak))
                scores.append((s, keys, is_low, sel))
            sums = []
            for sel in range(2):
                at = 2 * g + sel
                fade = jnp.exp(m_s[at] - tops[sel])
                sums.append(l_s[at] * fade)
                o_s[at] = o_s[at] * fade
                m_s[at] = tops[sel]
            for s, keys, is_low, sel in scores:
                p = jnp.exp(s - jnp.where(is_low, tops[0], tops[1]))
                part = jnp.sum(p, axis=0, keepdims=True)
                sums[0] = sums[0] + jnp.where(is_low, part, 0.0)
                sums[1] = sums[1] + jnp.where(is_low, 0.0, part)
                o_s[2 * g + sel] += dot_tn(keys, p.astype(BF))
            for sel in range(2):
                l_s[2 * g + sel] = sums[sel]

        loop(unit_steps, unit_step)
        for sel in range(2):
            at = 2 * g + sel
            total = l_s[at]
            lse_out.ref[at] = m_s[at] + jnp.log(total)
            result = o_s[at][HEAD:, :] / total
            for hh in range(GROUP):
                att_t[span(g * GROUP + hh, HEAD), sel * stretch : (sel + 1) * stretch] = result[
                    :, hh * stretch : (hh + 1) * stretch
                ]

    loop(KV_HEADS, one_head)
    lse_out.send()
    att_t_out.send()
    att_low = att_t[...].T.astype(BF)
    mixed = tok.get()[...].astype(F32).T + dot(att_low, w_out.get()[...])
    width = mixed.shape[1]
    part[...] = jnp.zeros(part.shape, F32)
    part[:, :width] = mixed
    mixed_out.ref[...] = part[...]
    mixed_out.send()
    n2 = (mixed * norm_scale(mixed, -1) * row_of(gain.get())).astype(BF)
    gate = dot(n2, w_gate.get()[...])
    up = dot(n2, w_up.get()[...])
    sig = 1.0 / (1.0 + jnp.exp(-gate))
    silu = gate * sig
    hidden = (silu * up).astype(BF)
    grad_hidden = dot_tn(cot.get()[...], w_down.get()[...])
    gl = (grad_hidden * up * (sig * (1.0 + gate * (1.0 - sig)))).astype(BF)
    ul = (grad_hidden * silu).astype(BF)
    piece = rows // wt
    mixed_q.ref[...] = part[span(meta[1], piece), :]
    mixed_q.send()
    part[:, :width] = dot_nt(gl, w_gate.get()[...]) + dot_nt(ul, w_up.get()[...])
    for k in range(wt):
        pin_outs[k].ref[...] = part[span(lax.bitwise_xor(meta[1], k), piece), :].astype(BF)
        pin_outs[k].send()
    part[:, :width] = dot_nt(hidden, w_down.get()[...])
    for k in range(wt):
        out_parts[k].ref[...] = part[span(lax.bitwise_xor(meta[1], k), piece), :].astype(BF)
        out_parts[k].send()
    units = gl.shape[1]
    grads[:, :units] = dot_tn(n2, gl)
    grads[:, units : 2 * units] = dot_tn(n2, ul)
    grads[:, 2 * units :] = dot(cot.get()[...], hidden)
    if n > 8:
        even.ref[...] = grads[...].astype(BF)
        odd.ref[...] = jnp.zeros(odd.ref.shape, BF)
    else:
        size = grads.shape[0] // n
        for k in range(n):
            to = even.ref if k % 2 == 0 else odd.ref
            to[k // 2] = grads[span(lax.bitwise_xor(me, k), size), :].astype(BF)


def backward_early(n, wt, ins, scratch):
    meta, order = ins[wt], ins[wt + 1]
    blocks = ins[wt + 16 :]
    count = n // 2 + 1
    evens, odds = blocks[: count - 1], blocks[count - 1]
    strips, strip_odds = blocks[count : 2 * count - 1], blocks[2 * count - 1]
    stretch = evens[0].shape[0] // 2
    all_s, kv, sems, strip_sems = scratch[8], scratch[10], scratch[11], scratch[12]
    kv_copies = natural_copies(n, meta[0], order, evens, odds, kv, sems, stretch)
    return kv_copies, natural_copies(
        n, meta[0], order, strips, strip_odds, all_s, strip_sems, stretch, True
    )


def backward_body(n, wt, ins, outs, scratch, copies):
    kv_copies, strip_copies = copies
    quarters = ins[:wt]
    (meta, order, gain, mixed, cot, w_out, att_t, lse, q_in, angle) = ins[wt : wt + 10]
    (first, inner, normed, wq, wk, wv) = ins[wt + 10 : wt + 16]
    gm_out, dq_out, even, odd = outs[:4]
    gn_s, do_s, dl_s, dkv, dq_s, dq_t, grads, norm_s, all_s, w_s, kv = scratch[:11]
    rows = mixed.ref.shape[0]
    width = gain.ref.shape[0]
    stretch = rows // 2
    wide = GROUP * stretch
    me = meta[0]
    c = order[0, 2 * me]
    low_group, low_steps, unit_group, unit_steps = parts_of(n)
    piece = rows // wt
    for k in range(wt):
        gn_s[span(lax.bitwise_xor(meta[1], k), piece), :] = quarters[k].get()[...].astype(F32)
    x = mixed.get()[:, :width]
    gn = gn_s[:, :width]
    r = norm_scale(x, -1)
    xn = x * r
    e = gn * row_of(gain.get())
    gm = cot.get()[...].astype(F32).T + r * (e - xn * jnp.mean(e * xn, axis=-1, keepdims=True))
    gn_s[:, :width] = gm
    gm_out.ref[...] = gn_s[span(meta[1], piece), :]
    gm_out.send()
    norm_s[...] = jnp.zeros(norm_s.shape, F32)
    norm_s[1:2, :width] = jnp.sum(gn * xn, axis=0, keepdims=True)
    branch = gm.astype(BF)
    ga = dot_nt(branch, w_out.get()[...]).astype(BF).astype(F32)
    prod = ga.T * att_t.get()[...]
    zero = jnp.zeros((rows, HEAD), F32)
    for h in range(Q_HEADS):
        g, hh = h // GROUP, h % GROUP
        delta = jnp.sum(prod[h * HEAD : (h + 1) * HEAD, :], axis=0, keepdims=True)
        do = jnp.concatenate([zero, ga[:, h * HEAD : (h + 1) * HEAD]], axis=1).astype(BF)
        for sel in range(2):
            at = (sel * 2 * GROUP + GROUP + hh) * stretch
            half = slice(sel * stretch, (sel + 1) * stretch)
            dl_s[2 * g + sel, :, hh * stretch : (hh + 1) * stretch] = delta[:, half]
            do_s[g, at : at + stretch, :] = do[half]
    strip = grads.shape[0]
    mine = span(meta[1], strip)
    grads[:, width : 2 * width] = dot(att_t.get()[mine, :].astype(BF), branch)
    lse, q_ref, angle = lse.get(), q_in.get(), angle.get()
    for g in range(KV_HEADS):
        for sel in range(2):
            do_s[g, 2 * sel * wide : (2 * sel + 1) * wide, :] = q_ref[g, sel * wide : (sel + 1) * wide, :]
    for copy in kv_copies:
        copy.wait()
    first, inner = first.get(), inner.get()
    chunk = 4
    low_chunks = lax.shift_right_logical(c, 2)
    key_ids = lax.broadcasted_iota(jnp.int32, (chunk * stretch, wide), 0)
    query_ids = lax.broadcasted_iota(jnp.int32, (chunk * stretch, wide), 1)
    query_ids = lax.bitwise_and(query_ids, stretch - 1)
    pre = kv
    lane_ids = lax.broadcasted_iota(jnp.int32, (stretch, PAIR), 1)

    def one_head(g):
        lanes = span(g, PAIR)
        dkv[n * stretch :, :] = jnp.zeros((n * stretch, PAIR), F32)
        dq_s[...] = jnp.zeros(dq_s.shape, F32)

        def low_step(i):
            at = span(i, low_group * stretch)
            keys = kv[at, lanes]
            both = do_s[g, 2 * wide :, :]
            s = dot_nt(keys, both)
            p = jnp.exp(s[:, :wide] - lse[2 * g + 1])
            ds = (p * (s[:, wide:] - dl_s[2 * g + 1])).astype(BF)
            dkv[at, :] = dot(jnp.concatenate([ds, p.astype(BF)], axis=1), both)
            dq_s[1] += dot_tn(keys, ds)

        loop(low_steps, low_step)

        def unit_step(u):
            is_low = u <= low_chunks
            sel = jnp.where(is_low, 0, 1)
            low_key = jnp.where(is_low, u, u - low_chunks - 1 + n // chunk) * (chunk * stretch)
            at = pl.ds(pl.multiple_of(low_key, chunk * stretch), chunk * stretch)
            keys = kv[at, lanes]
            both = do_s[g, span(sel, 2 * wide), :]
            s = dot_nt(keys, both)
            p = jnp.exp(s[:, :wide] - lse[2 * g + sel])
            ahead = low_key - jnp.where(is_low, c, 2 * n - 1 - c) * stretch
            p = jnp.where(key_ids + ahead <= query_ids, p, 0.0)
            ds = (p * (s[:, wide:] - dl_s[2 * g + sel])).astype(BF)
            dkv[at, :] += dot(jnp.concatenate([ds, p.astype(BF)], axis=1), both)
            dq_s[sel] += dot_tn(keys, ds)

        if n <= 8:
            for u in range(n // chunk + 1):
                unit_step(u)
        else:
            loop(n // chunk + 1, unit_step)

        def turn(i):
            ct, st = inner[0], inner[1]
            cs, ss = first[i, 0:1, :], first[i, 1:2, :]
            part = dkv[span(i, stretch), :]
            back = pltpu.roll(part, PAIR - HALF, 1)
            ahead = pltpu.roll(part, HALF, 1)
            swapped = jnp.where(lane_ids < HALF, back, ahead)
            result = part * (ct * cs - st * ss) + swapped * (st * cs + ct * ss)
            pre[span(i, stretch), lanes] = result.astype(BF)

        if n <= 8:
            for i in range(2 * n):
                turn(i)
        else:
            loop(2 * n, turn)
        for sel in range(2):
            half = slice(sel * stretch, (sel + 1) * stretch)
            cos, sin = angle[:HALF, half], angle[HALF:, half]
            for hh in range(GROUP):
                dq = dq_s[sel, :HEAD, hh * stretch : (hh + 1) * stretch] * HEAD**-0.5
                a, b = dq[:HALF], dq[HALF:]
                turned = jnp.concatenate([a * cos + b * sin, b * cos - a * sin], axis=0)
                dq_t[span(g * GROUP + hh, HEAD), half] = turned

    loop(KV_HEADS, one_head)
    dq = dq_t[...].T.astype(BF)
    gn_s[:, :width] = dq.astype(F32)
    dq_out.ref[...] = gn_s[span(meta[1], piece), :].astype(BF)
    dq_out.send()
    grads[:, :width] = dot(normed.get()[...], dq)
    for copy in strip_copies:
        copy.wait()
    grads[:, 2 * width :] = dot(all_s[...], pre[...])
    wk, wv = wk.get()[...].astype(F32), wv.get()[...].astype(F32)
    chunks = []
    for g in range(KV_HEADS):
        chunks += [wk[g * HEAD : (g + 1) * HEAD], wv[g * HEAD : (g + 1) * HEAD]]
    w_s[...] = jnp.concatenate(chunks, axis=0).T
    sums = jnp.sum(grads[:, :width] * wq.get()[mine, :].astype(F32), axis=1, keepdims=True)
    sums = sums + jnp.sum(grads[:, 2 * width :] * w_s[mine, :], axis=1, keepdims=True)
    norm_s[0:1, :strip] = jnp.broadcast_to(sums, (strip, 128)).T[0:1, :]
    quarter = meta[1] * piece
    upper = quarter >= stretch
    inside = jnp.where(upper, quarter - stretch, quarter)

    def rows_for(who):
        low = order[0, 2 * who]
        st = jnp.where(upper, 2 * n - 1 - low, low)
        return pre[pl.ds(pl.multiple_of(st * stretch + inside, piece), piece), :]

    if n > 8:
        even[...] = grads[...].astype(BF)
        odd[...] = norm_s[...].astype(BF)
        for k in range(n):
            outs[4][k] = rows_for(k)
        return
    for k in range(n):
        who = lax.bitwise_xor(me, k)
        to = even if k % 2 == 0 else odd
        to[k // 2, :piece, :] = rows_for(who)
        block = grads[block_rows(strip, who), block_lanes(who)]
        cut = norm_s[:, span(who, 128)]
        tail = jnp.concatenate([cut, jnp.zeros((8, block.shape[1] - 128), F32)], axis=1)
        to[k // 2, piece:, :] = jnp.concatenate([block, tail], axis=0).astype(BF)


def block_rows(strip, who):
    size = strip // 2
    return pl.ds(pl.multiple_of(lax.shift_right_logical(who, 2) * size, size), size)


def block_lanes(who):
    return span(lax.bitwise_and(who, 3), KV_HEADS * PAIR)


def finish_body(count, ins, outs, scratch):
    terms = ins[:count]
    meta, gain, tok, gm, dq, wq, wk, wv = ins[count:]
    (gt_out,) = outs
    (x_s,) = scratch
    piece = gt_out.shape[0]
    total = terms[0][:piece, :].astype(F32)
    for term in terms[1:]:
        total = total + term[:piece, :].astype(F32)
    mine = span(meta[1], piece)
    x_s[...] = tok.get()[...].astype(F32).T
    x = x_s[mine, :]
    dk, dv = [], []
    for g in range(KV_HEADS):
        dk.append(total[:, g * PAIR : g * PAIR + HEAD])
        dv.append(total[:, g * PAIR + HEAD : (g + 1) * PAIR])
    dk = jnp.concatenate(dk, axis=1).astype(BF)
    dv = jnp.concatenate(dv, axis=1).astype(BF)
    width = gain.shape[0]
    gn = dot_nt(dq[:, :width], wq.get()[...])
    gn = gn + dot(dk, wk.get()[...]) + dot(dv, wv.get()[...])
    r = norm_scale(x, -1)
    xn = x * r
    e = gn * row_of(gain)
    result = gm[:, :width] + r * (e - xn * jnp.mean(e * xn, axis=-1, keepdims=True))
    gt_out[:, :width] = result.astype(BF)
    gt_out[:, width:] = jnp.zeros((piece, gt_out.shape[1] - width), BF)


def token_join_body(wt, ins, outs, scratch):
    meta = ins[0]
    (rows_s,) = scratch
    for i in range(2):
        quarters = ins[1 + i * wt : 1 + (i + 1) * wt]
        for k in range(wt):
            at = span(lax.bitwise_xor(meta[1], k), quarters[0].shape[0])
            rows_s[at, :] = quarters[k][:, : rows_s.shape[1]].astype(F32)
        outs[i][...] = rows_s[...].T.astype(outs[i].dtype)


def mlp_join_body(n, ins, outs, scratch):
    meta, blocks = ins[0], ins[1:]
    (grads,) = scratch
    if n > 8:
        grads[...] = blocks[0][...].astype(F32)
    else:
        size = grads.shape[0] // n
        for k in range(n):
            block = blocks[k // 2][...] if k % 2 == 0 else blocks[-1][k // 2]
            grads[span(lax.bitwise_xor(meta[0], k), size), :] = block.astype(F32)
    width = outs[0].shape[1]
    for i in range(3):
        outs[i][...] = grads[:, i * width : (i + 1) * width]


def join_body(n, wt, ins, outs, scratch):
    meta, gain = ins[:2]
    blocks = ins[2:]
    gq, go, gk, gv, norm_attn, norm_mlp = outs
    grads, norm_s = scratch
    width = gq.shape[0]
    strip = width // wt
    norm_s[...] = jnp.zeros(norm_s.shape, F32)
    if n > 8:
        grads[...] = blocks[0][...].astype(F32)
        norm_s[...] = blocks[1][...].astype(F32)
    else:
        size = strip // 2
        for k in range(n):
            who = lax.bitwise_xor(meta[0], k)
            for kz in range(wt):
                lane = lax.bitwise_xor(meta[1], kz)
                block = blocks[k // 2][kz] if k % 2 == 0 else blocks[-1][k // 2, kz]
                block = block.astype(F32)
                at = lane * strip + lax.shift_right_logical(who, 2) * size
                grads[pl.ds(pl.multiple_of(at, size), size), block_lanes(who)] = block[:size]
                norm_s[lane, :, span(who, 128)] = block[size:, :128]
    gq[...] = grads[:, :width]
    go[...] = grads[:, width : 2 * width]
    both = grads[:, 2 * width :].T
    for g in range(KV_HEADS):
        gk[g * HEAD : (g + 1) * HEAD, :] = both[g * PAIR : g * PAIR + HEAD]
        gv[g * HEAD : (g + 1) * HEAD, :] = both[g * PAIR + HEAD : (g + 1) * PAIR]
    attn = jnp.concatenate([norm_s[lane, 0:1, :strip] for lane in range(wt)], axis=1)
    norm_attn[...] = (attn / row_of(gain)).reshape(width)
    norm_mlp[...] = norm_s[0, 1:2, :width].reshape(width)


def hop(x, axis, size, k):
    return lax.ppermute(x, axis, [(i, i ^ k) for i in range(size)])


def gather_blocks(x, axis, size):
    evens = [x] + [hop(x, axis, size, k) for k in range(2, size, 2)]
    odds = hop(jnp.stack(evens), axis, size, 1)
    return evens, odds


def pair_terms(even, odd, axis, size):
    got = hop(odd, axis, size, 1).astype(F32)
    pairs = [even[i].astype(F32) + got[i] for i in range(size // 2)]
    return pairs[:1] + [pair.astype(BF) for pair in pairs[1:]]


def scatter_terms(pairs, axis, size):
    return pairs[:1] + [hop(pairs[i], axis, size, 2 * i) for i in range(1, size // 2)]


def summed(terms):
    total = terms[0].astype(F32)
    for term in terms[1:]:
        total = total + term.astype(F32)
    return total


def after(dep, *arrays):
    held = lax.optimization_barrier((dep,) + arrays)
    return list(held[1:]) if len(arrays) > 1 else held[1]


def local(
    n,
    wt,
    tokens,
    w_query,
    w_key,
    w_value,
    w_out,
    norm_attn,
    norm_mlp,
    w_gate,
    w_up,
    w_down,
    stretch_order,
    cotangent,
):
    rows, width = tokens.shape
    stretch = rows // 2
    wide = GROUP * stretch
    kv_width = KV_HEADS * PAIR
    hidden_width = w_gate.shape[1]
    piece = rows // wt
    size = width // n
    strip = width // wt
    small = n <= 8
    padded = -(-width // 128) * 128
    turned, first, inner = (jnp.asarray(t) for t in angle_tables(n, stretch))
    tok, cot, wk, wv, w_down = tokens.T, cotangent.T, w_key.T, w_value.T, w_down.T

    normed, kv, angle, normed_q = call(
        key_body,
        [None, stretch_order, norm_attn, tok, wk, wv, turned],
        "mscccch",
        [shape((width, rows), BF), shape((rows, kv_width), BF), shape((HEAD, rows), F32)]
        + [shape((strip, rows), BF)],
        "vvvv",
        scratch=[
            pltpu.VMEM((width, rows), F32),
            pltpu.VMEM((2, HEAD, stretch), F32),
            pltpu.SemaphoreType.DMA((2,)),
        ],
        early=key_early,
    )
    (q,) = call(
        query_body,
        [normed, w_query, angle],
        "vcv",
        [shape((KV_HEADS, 2 * wide, PAIR), BF)],
        "c",
    )
    evens = [kv] + [hop(kv, "ctx", n, k) for k in range(2, n, 2)]
    strips = [normed_q] + [hop(normed_q, "ctx", n, k) for k in range(2, n, 2)]
    odds = hop(jnp.stack(after(q, *evens)), "ctx", n, 1)

    mlp_columns = 3 * hidden_width
    if small:
        block_shapes = [shape((n // 2, size, mlp_columns), BF)] * 2
    else:
        block_shapes = [shape((width, mlp_columns), BF), shape((8, 128), BF)]
    results = call(
        functools.partial(forward_body, n, wt),
        [*evens, odds, None, stretch_order, q, tok, w_out, norm_mlp, w_gate, w_up, cot, w_down],
        "h" * (n // 2 + 1) + "msccc" + "c" + "cccc",
        [
            shape((width, rows), F32),
            shape((2 * KV_HEADS, 1, wide), F32),
            shape((rows, padded), F32),
        ]
        + block_shapes
        + [shape((piece, padded), F32)]
        + [shape((piece, padded), BF)] * (2 * wt),
        "ccc" + "ccc" + "c" * (2 * wt),
        scratch=[
            pltpu.VMEM((n * rows, kv_width), BF),
            pltpu.VMEM((2 * KV_HEADS, 1, wide), F32),
            pltpu.VMEM((2 * KV_HEADS, 1, wide), F32),
            pltpu.VMEM((2 * KV_HEADS, PAIR, wide), F32),
            pltpu.VMEM((rows, padded), F32),
            pltpu.VMEM((width, mlp_columns), F32),
            pltpu.SemaphoreType.DMA((2 * n,)),
        ],
        early=functools.partial(forward_early, n),
        micros=14,
    )
    att_t, lse, mixed, even, odd, mixed_q, *pieces = after(strips, *results)
    part_in, out_parts = pieces[:wt], pieces[wt:]
    strip_odds = hop(jnp.stack(strips), "ctx", n, 1)

    terms = [part_in[0]] + [hop(part_in[k], "wt", wt, k) for k in range(1, wt)]
    quarter = summed(terms).astype(BF)
    quarters = [quarter] + [hop(quarter, "wt", wt, k) for k in range(1, wt)]

    if small:
        pairs = pair_terms(even, odd, "ctx", n)
        quarters = after(pairs[0], *quarters)
        mlp_own = summed(scatter_terms(pairs, "ctx", n)).astype(BF)
    else:
        mlp_blocks = [lax.psum(even, "ctx")]

    columns = 2 * width + kv_width
    if small:
        out_blocks = [shape((n // 2, piece + strip // 2 + 8, kv_width), BF)] * 2
    else:
        out_blocks = [
            shape((strip, columns), BF),
            shape((8, 128 * n), BF),
            shape((n, piece, kv_width), BF),
        ]
    gm_q, dq_q, *message = call(
        functools.partial(backward_body, n, wt),
        [*quarters, None, stretch_order, norm_mlp, mixed, cot, w_out, att_t, lse, q, angle]
        + [first, inner, normed_q, w_query, wk, wv, *evens, odds, *strips, strip_odds],
        "c" * wt + "msc" + "c" * 7 + "c" * 6 + "h" * (n + 2),
        [shape((piece, padded), F32), shape((piece, padded), BF)] + out_blocks,
        "cc" + "v" * len(out_blocks),
        scratch=[
            pltpu.VMEM((rows, padded), F32),
            pltpu.VMEM((KV_HEADS, 4 * wide, PAIR), BF),
            pltpu.VMEM((2 * KV_HEADS, 1, wide), F32),
            pltpu.VMEM((n * rows, PAIR), F32),
            pltpu.VMEM((2, PAIR, wide), F32),
            pltpu.VMEM((width, rows), F32),
            pltpu.VMEM((strip, columns), F32),
            pltpu.VMEM((8, max(128 * n, 640)), F32),
            pltpu.VMEM((strip, n * rows), BF),
            pltpu.VMEM((width, kv_width), F32),
            pltpu.VMEM((n * rows, kv_width), BF),
            pltpu.SemaphoreType.DMA((2 * n,)),
            pltpu.SemaphoreType.DMA((2 * n,)),
        ],
        early=functools.partial(backward_early, n, wt),
        early_at=wt + 10,
        micros=17,
    )
    out_parts = after(mlp_own, *out_parts) if small else out_parts
    out_terms = [out_parts[0]] + [hop(out_parts[k], "wt", wt, k) for k in range(1, wt)]
    out_q = (mixed_q + summed(out_terms)).astype(BF)
    out_qs = [out_q] + [hop(out_q, "wt", wt, k) for k in range(1, wt)]
    if small:
        mlp_evens, mlp_odds = gather_blocks(mlp_own, "ctx", n)
        mlp_blocks = [*mlp_evens, mlp_odds]
        message[1] = after((mlp_evens, out_terms), message[1])
        parts = scatter_terms(pair_terms(message[0], message[1], "ctx", n), "ctx", n)
        parts = after(out_qs, *parts)
        own = summed([part[piece:] for part in parts]).astype(BF)
        owns = [own] + [hop(own, "wt", wt, k) for k in range(1, wt)]
    else:
        parts = [lax.psum_scatter(message[2].astype(F32), "ctx", scatter_dimension=0)]
        last_blocks = list(lax.psum((message[0], message[1]), "ctx"))
        last_blocks = [lax.all_gather(b, "wt", axis=0, tiled=i == 0) for i, b in enumerate(last_blocks)]
    (gt,) = call(
        functools.partial(finish_body, len(parts)),
        [*parts, None, norm_attn, tok, gm_q, dq_q, w_query, wk, wv],
        "v" * len(parts) + "mvcvvccc",
        [shape((piece, padded), BF)],
        "v",
        scratch=[pltpu.VMEM((rows, width), F32)],
        vmem=16,
        micros=2,
    )
    gts = [gt] + [hop(gt, "wt", wt, k) for k in range(1, wt)]
    grad_gate, grad_up, grad_down = call(
        functools.partial(mlp_join_body, n),
        [None, *mlp_blocks],
        "m" + "v" * len(mlp_blocks),
        [shape((width, hidden_width), F32)] * 3,
        "vvv",
        scratch=[pltpu.VMEM((width, mlp_columns), F32)],
        vmem=24,
        micros=2,
    )
    grad_tokens, output = call(
        functools.partial(token_join_body, wt),
        [None, *gts, *out_qs],
        "m" + "v" * (2 * wt),
        [shape((width, rows), F32), shape((width, rows), BF)],
        "vv",
        scratch=[pltpu.VMEM((rows, width), F32)],
        vmem=24,
        micros=2,
    )
    if small:
        last = jnp.stack(after(gt, *owns))
        last_evens = [last] + [hop(last, "ctx", n, k) for k in range(2, n, 2)]
        last = hop(after((grad_gate, gts), jnp.stack(last_evens)), "ctx", n, 1)
        last_blocks = [*last_evens, after(grad_tokens, last)]
    grad_query, grad_out, grad_key, grad_value, grad_norm_attn, grad_norm_mlp = call(
        functools.partial(join_body, n, wt),
        [None, norm_attn, *last_blocks],
        "mv" + "v" * len(last_blocks),
        [shape((width, width), F32)] * 2
        + [shape((kv_width // 2, width), F32)] * 2
        + [shape((width,), F32)] * 2,
        "vvvvvv",
        scratch=[
            pltpu.VMEM((width, columns), F32),
            pltpu.VMEM((wt, 8, max(128 * n, 640)), F32),
        ],
        vmem=24,
    )
    return (
        output.T,
        grad_tokens.T,
        grad_query,
        grad_key.T,
        grad_value.T,
        grad_out,
        grad_norm_attn,
        grad_norm_mlp,
        grad_gate,
        grad_up,
        grad_down.T,
    )


def solution(mesh):
    return jax.shard_map(
        functools.partial(local, mesh.shape["ctx"], mesh.shape["wt"]),
        mesh=mesh,
        in_specs=(
            P("ctx", None),
            P(),
            P(),
            P(),
            P(),
            P(),
            P(),
            P(None, "wt"),
            P(None, "wt"),
            P("wt", None),
            P(),
            P("ctx", None),
        ),
        out_specs=(
            P("ctx", None),
            P("ctx", None),
            P(),
            P(),
            P(),
            P(),
            P(),
            P(),
            P(None, "wt"),
            P(None, "wt"),
            P("wt", None),
        ),
        check_vma=False,
    )
```

```python
import functools

import jax
import jax.numpy as jnp
import numpy as np
from jax import lax
from jax.experimental import pallas as pl
from jax.experimental.pallas import tpu as pltpu
from jax.sharding import PartitionSpec as P

Q_HEADS = 9
KV_HEADS = 3
GROUP = 3
HEAD = 64
HALF = 32
PAIR = 2 * HEAD
EPSILON = 1e-05
THETA = 100000.0
NEGATIVE = -1e30
BF = jnp.bfloat16
F32 = jnp.float32
MIB = 1 << 20


def dot(left, right):
    return jnp.dot(left, right, preferred_element_type=F32)


def dot_nt(left, right):
    return lax.dot_general(left, right, (((1,), (1,)), ((), ())), preferred_element_type=F32)


def dot_tn(left, right):
    return lax.dot_general(left, right, (((0,), (0,)), ((), ())), preferred_element_type=F32)


def shape(dims, dtype):
    return jax.ShapeDtypeStruct(dims, dtype)


SPEC = {
    "v": pl.BlockSpec(memory_space=pltpu.VMEM),
    "s": pl.BlockSpec(memory_space=pltpu.SMEM),
    "h": pl.BlockSpec(memory_space=pltpu.HBM),
    "c": pl.BlockSpec(memory_space=pltpu.HBM),
}


class Fetched:
    def __init__(self, copy, ref):
        self.copy, self.ref, self.waited = copy, ref, False

    def get(self):
        if not self.waited:
            self.copy.wait()
            self.waited = True
        return self.ref


class Stored:
    def __init__(self, copy, ref):
        self.copy, self.ref, self.sent = copy, ref, False

    def send(self):
        self.copy.start()
        self.sent = True


def call(body, ins, in_kinds, outs, out_kinds, scratch=(), vmem=60, early=None, early_at=0, micros=3):
    real = [(a, kind) for a, kind in zip(ins, in_kinds) if kind != "m"]
    staged = [a for a, kind in real if kind == "c"]
    staged_out = [o for o, kind in zip(outs, out_kinds) if kind == "c"]
    count = len(staged) + len(staged_out)
    buffers = [pltpu.VMEM(a.shape, a.dtype) for a in staged + staged_out]
    if count:
        buffers.append(pltpu.SemaphoreType.DMA((count,)))

    def kernel(*refs):
        in_refs = iter(refs[: len(real)])
        out_refs = refs[len(real) : len(real) + len(outs)]
        own = refs[len(real) + len(outs) : len(refs) - len(buffers)]
        extra = refs[len(refs) - len(buffers) :]
        at = 0
        given, results = [], []
        for kind in in_kinds:
            place = (lax.axis_index("ctx"), lax.axis_index("wt")) if kind == "m" else next(in_refs)
            given.append(place)
        state = ()
        for i, kind in enumerate(in_kinds):
            if early is not None and i == early_at:
                state = (early(given, own),)
            if kind == "c":
                ref = given[i]
                copy = pltpu.make_async_copy(ref, extra[at], extra[-1].at[at])
                copy.start()
                given[i] = Fetched(copy, extra[at])
                at += 1
        for ref, kind in zip(out_refs, out_kinds):
            if kind == "c":
                ref = Stored(pltpu.make_async_copy(extra[at], ref, extra[-1].at[at]), extra[at])
                at += 1
            results.append(ref)
        body(given, results, own, *state)
        for item in given:
            if isinstance(item, Fetched):
                item.get()
        stored = [item for item in results if isinstance(item, Stored)]
        for item in stored:
            if not item.sent:
                item.send()
        for item in stored:
            item.copy.wait()

    return pl.pallas_call(
        kernel,
        out_shape=tuple(outs),
        in_specs=[SPEC[k] for _, k in real],
        out_specs=tuple(SPEC[k] for k in out_kinds),
        scratch_shapes=list(scratch) + buffers,
        compiler_params=pltpu.CompilerParams(vmem_limit_bytes=vmem * MIB),
        cost_estimate=pl.CostEstimate(flops=micros * 1_150_000_000, bytes_accessed=MIB, transcendentals=0),
    )(*[a for a, _ in real])


def angle_tables(n, stretch):
    rates = THETA ** (-np.arange(HALF, dtype=np.float64) / HALF)
    places = np.arange(2 * n * stretch, dtype=np.float64).reshape(2 * n, 1, stretch)
    angle = places * rates[None, :, None]
    turned = np.concatenate([np.cos(angle), np.sin(angle)], axis=1).astype(np.float32)
    sign = np.concatenate([np.ones(HALF), -np.ones(HALF)])
    lanes = np.concatenate([rates, rates])
    start = np.arange(2 * n)[:, None] * stretch * lanes[None, :]
    offset = np.arange(stretch)[:, None] * lanes[None, :]

    def widen(table, fill):
        return np.concatenate([table, np.full(table.shape, fill)], axis=1).astype(np.float32)

    first = np.stack([widen(np.cos(start), 1.0), widen(np.sin(start) * sign, 0.0)], axis=1)
    inner = np.stack([widen(np.cos(offset), 1.0), widen(np.sin(offset) * sign, 0.0)])
    return turned, first, inner


def row_of(ref):
    return ref[...].astype(F32).reshape(1, ref.shape[0])


def norm_scale(x, axis):
    return lax.rsqrt(jnp.mean(x * x, axis=axis, keepdims=True) + EPSILON)


def key_early(ins, scratch):
    meta, order, turned = ins[0], ins[1], ins[-1]
    copies = []
    for half in range(2):
        src = turned.at[order[0, 2 * meta[0] + half]]
        copies.append(pltpu.make_async_copy(src, scratch[0].at[half], scratch[1].at[half]))
        copies[-1].start()
    return copies


def key_body(ins, outs, scratch, copies):
    meta, order, gain, tok, wk, wv, turned = ins
    normed_out, kv_out, angle_out = outs
    angle_s, sems = scratch
    x = tok.get()[...].astype(F32)
    gain = jnp.broadcast_to(row_of(gain.get()), (8, x.shape[0])).T[:, 0:1]
    normed = (x * norm_scale(x, 0) * gain).astype(BF)
    normed_out[...] = normed
    for copy in copies:
        copy.wait()
    angle = jnp.concatenate([angle_s[0], angle_s[1]], axis=1)
    angle_out[...] = angle
    cos, sin = angle[:HALF], angle[HALF:]
    k = dot(wk.get()[...], normed)
    v = dot(wv.get()[...], normed)
    parts = []
    for g in range(KV_HEADS):
        a, b = k[g * HEAD : g * HEAD + HALF], k[g * HEAD + HALF : (g + 1) * HEAD]
        parts += [a * cos - b * sin, b * cos + a * sin, v[g * HEAD : (g + 1) * HEAD]]
    kv_out[...] = jnp.concatenate(parts, axis=0).T.astype(BF)


def query_body(ins, outs, scratch):
    meta, normed, wq, angle = ins
    q_out, normed_q = outs[0].ref, outs[1]
    (normed_s,) = scratch
    normed_s[...] = normed[...].astype(F32)
    normed_q[...] = normed_s[span(meta[1], normed_q.shape[0]), :].astype(BF)
    rows = normed.shape[1]
    stretch = rows // 2
    q = dot(normed[...].astype(F32).T.astype(BF), wq.get()[...])
    table = angle[...].T
    cos = jnp.concatenate([table[:, :HALF]] * 2, axis=1)
    sin = jnp.concatenate([-table[:, HALF:], table[:, HALF:]], axis=1)
    zero = jnp.zeros((rows, HEAD), F32)
    for h in range(Q_HEADS):
        qh = q[:, h * HEAD : (h + 1) * HEAD]
        swapped = jnp.concatenate([qh[:, HALF:], qh[:, :HALF]], axis=1)
        qr = (qh * cos + swapped * sin) * HEAD**-0.5
        wide = jnp.concatenate([qr, zero], axis=1).astype(BF)
        g, hh = h // GROUP, h % GROUP
        for sel in range(2):
            at = (sel * GROUP + hh) * stretch
            q_out[g, at : at + stretch, :] = wide[sel * stretch : (sel + 1) * stretch]


def parts_of(n):
    low_group = min(n, 8)
    unit_group = max(d for d in range(1, 14) if (n + 1) % d == 0)
    return low_group, n // low_group, unit_group, (n + 1) // unit_group


def loop(count, body):
    if count == 1:
        body(0)
    else:
        lax.fori_loop(0, count, lambda i, c: (body(i), c)[1], 0)


def unit(u, c, n):
    is_low = u <= c
    sel = jnp.where(is_low, 0, 1)
    stretch_id = jnp.where(is_low, u, n - 1 + u - c)
    diagonal = jnp.logical_or(u == c, u == n)
    return is_low, sel, stretch_id, diagonal


def seen_mask(stretch, diagonal):
    keys = lax.broadcasted_iota(jnp.int32, (stretch, GROUP * stretch), 0)
    cols = lax.broadcasted_iota(jnp.int32, (stretch, GROUP * stretch), 1)
    queries = lax.bitwise_and(cols, stretch - 1)
    return jnp.logical_or(keys <= queries, jnp.logical_not(diagonal))


def span(index, size):
    return pl.ds(pl.multiple_of(index * size, size), size)


def natural_copies(n, me, order, evens, odds, to, sems, stretch, lanes=False):
    copies = []
    for k in range(n):
        low = order[0, 2 * lax.bitwise_xor(me, k)]
        src = evens[k // 2] if k % 2 == 0 else odds.at[k // 2]
        for half in range(2):
            at = span(low if half == 0 else 2 * n - 1 - low, stretch)
            cut = slice(half * stretch, (half + 1) * stretch)
            src_cut, to_cut = (src.at[:, cut], to.at[:, at]) if lanes else (src.at[cut], to.at[at])
            copies.append(pltpu.make_async_copy(src_cut, to_cut, sems.at[2 * k + half]))
    for copy in copies:
        copy.start()
    return copies


def forward_early(n, ins, scratch):
    evens, (odds, meta, order) = ins[: n // 2], ins[n // 2 : n // 2 + 3]
    return natural_copies(n, meta[0], order, evens, odds, scratch[0], scratch[-1], evens[0].shape[0] // 2)


def forward_body(n, wt, ins, outs, scratch, copies):
    odds, meta, order, q_in, tok, w_out, gain, w_gate, w_up, cot, w_down = ins[n // 2 :]
    att_t_out, lse_out, mixed_out, even, odd, mixed_q = outs[:6]
    pin_outs, out_parts = outs[6 : 6 + wt], outs[6 + wt :]
    kvn, m_s, l_s, o_s, part, grads, sems = scratch
    rows = tok.ref.shape[1]
    stretch = rows // 2
    wide = GROUP * stretch
    me = meta[0]
    for copy in copies:
        copy.wait()
    c = order[0, 2 * me]
    low_group, low_steps, unit_group, unit_steps = parts_of(n)
    q_ref = q_in.get()
    att_t = att_t_out.ref

    def one_head(g):
        lanes = span(g, PAIR)
        for sel in range(2):
            m_s[2 * g + sel] = jnp.full((1, wide), NEGATIVE, F32)
            l_s[2 * g + sel] = jnp.zeros((1, wide), F32)
            o_s[2 * g + sel] = jnp.zeros((PAIR, wide), F32)

        def low_step(i):
            keys = kvn[span(i, low_group * stretch), lanes]
            s = dot_nt(keys, q_ref[g, wide : 2 * wide, :])
            at = 2 * g + 1
            top = jnp.maximum(m_s[at], jnp.max(s, axis=0, keepdims=True))
            fade = jnp.exp(m_s[at] - top)
            p = jnp.exp(s - top)
            l_s[at] = l_s[at] * fade + jnp.sum(p, axis=0, keepdims=True)
            o_s[at] = o_s[at] * fade + dot_tn(keys, p.astype(BF))
            m_s[at] = top

        loop(low_steps, low_step)

        def unit_step(i):
            scores = []
            tops = [m_s[2 * g], m_s[2 * g + 1]]
            for j in range(unit_group):
                u = i * unit_group + j
                is_low, sel, st, diagonal = unit(u, c, n)
                keys = kvn[span(st, stretch), lanes]
                s = dot_nt(keys, q_ref[g, span(sel, wide), :])
                s = jnp.where(seen_mask(stretch, diagonal), s, NEGATIVE)
                peak = jnp.max(s, axis=0, keepdims=True)
                tops[0] = jnp.where(is_low, jnp.maximum(tops[0], peak), tops[0])
                tops[1] = jnp.where(is_low, tops[1], jnp.maximum(tops[1], peak))
                scores.append((s, keys, is_low, sel))
            sums = []
            for sel in range(2):
                at = 2 * g + sel
                fade = jnp.exp(m_s[at] - tops[sel])
                sums.append(l_s[at] * fade)
                o_s[at] = o_s[at] * fade
                m_s[at] = tops[sel]
            for s, keys, is_low, sel in scores:
                p = jnp.exp(s - jnp.where(is_low, tops[0], tops[1]))
                part = jnp.sum(p, axis=0, keepdims=True)
                sums[0] = sums[0] + jnp.where(is_low, part, 0.0)
                sums[1] = sums[1] + jnp.where(is_low, 0.0, part)
                o_s[2 * g + sel] += dot_tn(keys, p.astype(BF))
            for sel in range(2):
                l_s[2 * g + sel] = sums[sel]

        loop(unit_steps, unit_step)
        for sel in range(2):
            at = 2 * g + sel
            total = l_s[at]
            lse_out.ref[at] = m_s[at] + jnp.log(total)
            result = o_s[at][HEAD:, :] / total
            for hh in range(GROUP):
                att_t[span(g * GROUP + hh, HEAD), sel * stretch : (sel + 1) * stretch] = result[
                    :, hh * stretch : (hh + 1) * stretch
                ]

    loop(KV_HEADS, one_head)
    lse_out.send()
    att_t_out.send()
    att_low = att_t[...].T.astype(BF)
    mixed = tok.get()[...].astype(F32).T + dot(att_low, w_out.get()[...])
    width = mixed.shape[1]
    part[...] = jnp.zeros(part.shape, F32)
    part[:, :width] = mixed
    mixed_out.ref[...] = part[...]
    mixed_out.send()
    n2 = (mixed * norm_scale(mixed, -1) * row_of(gain.get())).astype(BF)
    gate = dot(n2, w_gate.get()[...])
    up = dot(n2, w_up.get()[...])
    sig = 1.0 / (1.0 + jnp.exp(-gate))
    silu = gate * sig
    hidden = (silu * up).astype(BF)
    grad_hidden = dot_tn(cot.get()[...], w_down.get()[...])
    gl = (grad_hidden * up * (sig * (1.0 + gate * (1.0 - sig)))).astype(BF)
    ul = (grad_hidden * silu).astype(BF)
    piece = rows // wt
    mixed_q.ref[...] = part[span(meta[1], piece), :]
    mixed_q.send()
    part[:, :width] = dot_nt(gl, w_gate.get()[...]) + dot_nt(ul, w_up.get()[...])
    for k in range(wt):
        pin_outs[k].ref[...] = part[span(lax.bitwise_xor(meta[1], k), piece), :].astype(BF)
        pin_outs[k].send()
    part[:, :width] = dot_nt(hidden, w_down.get()[...])
    for k in range(wt):
        out_parts[k].ref[...] = part[span(lax.bitwise_xor(meta[1], k), piece), :].astype(BF)
        out_parts[k].send()
    units = gl.shape[1]
    grads[:, :units] = dot_tn(n2, gl)
    grads[:, units : 2 * units] = dot_tn(n2, ul)
    grads[:, 2 * units :] = dot(cot.get()[...], hidden)
    if n > 8:
        even.ref[...] = grads[...].astype(BF)
        odd.ref[...] = jnp.zeros(odd.ref.shape, BF)
    else:
        size = grads.shape[0] // n
        for k in range(n):
            to = even.ref if k % 2 == 0 else odd.ref
            to[k // 2] = grads[span(lax.bitwise_xor(me, k), size), :].astype(BF)


def backward_early(n, wt, ins, scratch):
    meta, order = ins[wt], ins[wt + 1]
    blocks = ins[wt + 16 :]
    count = n // 2 + 1
    evens, odds = blocks[: count - 1], blocks[count - 1]
    strips, strip_odds = blocks[count : 2 * count - 1], blocks[2 * count - 1]
    stretch = evens[0].shape[0] // 2
    all_s, kv, sems, strip_sems = scratch[8], scratch[10], scratch[11], scratch[12]
    kv_copies = natural_copies(n, meta[0], order, evens, odds, kv, sems, stretch)
    return kv_copies, natural_copies(
        n, meta[0], order, strips, strip_odds, all_s, strip_sems, stretch, True
    )


def backward_body(n, wt, ins, outs, scratch, copies):
    kv_copies, strip_copies = copies
    quarters = ins[:wt]
    (meta, order, gain, mixed, cot, w_out, att_t, lse, q_in, angle) = ins[wt : wt + 10]
    (first, inner, normed, wq, wk, wv) = ins[wt + 10 : wt + 16]
    gm_out, dq_out, even, odd = outs[:4]
    gn_s, do_s, dl_s, dkv, dq_s, dq_t, grads, norm_s, all_s, w_s, kv = scratch[:11]
    rows = mixed.ref.shape[0]
    width = gain.ref.shape[0]
    stretch = rows // 2
    wide = GROUP * stretch
    me = meta[0]
    c = order[0, 2 * me]
    low_group, low_steps, unit_group, unit_steps = parts_of(n)
    piece = rows // wt
    for k in range(wt):
        gn_s[span(lax.bitwise_xor(meta[1], k), piece), :] = quarters[k].get()[...].astype(F32)
    x = mixed.get()[:, :width]
    gn = gn_s[:, :width]
    r = norm_scale(x, -1)
    xn = x * r
    e = gn * row_of(gain.get())
    gm = cot.get()[...].astype(F32).T + r * (e - xn * jnp.mean(e * xn, axis=-1, keepdims=True))
    gn_s[:, :width] = gm
    gm_out.ref[...] = gn_s[span(meta[1], piece), :]
    gm_out.send()
    norm_s[...] = jnp.zeros(norm_s.shape, F32)
    norm_s[1:2, :width] = jnp.sum(gn * xn, axis=0, keepdims=True)
    branch = gm.astype(BF)
    ga = dot_nt(branch, w_out.get()[...]).astype(BF).astype(F32)
    prod = ga.T * att_t.get()[...]
    zero = jnp.zeros((rows, HEAD), F32)
    for h in range(Q_HEADS):
        g, hh = h // GROUP, h % GROUP
        delta = jnp.sum(prod[h * HEAD : (h + 1) * HEAD, :], axis=0, keepdims=True)
        do = jnp.concatenate([zero, ga[:, h * HEAD : (h + 1) * HEAD]], axis=1).astype(BF)
        for sel in range(2):
            at = (sel * 2 * GROUP + GROUP + hh) * stretch
            half = slice(sel * stretch, (sel + 1) * stretch)
            dl_s[2 * g + sel, :, hh * stretch : (hh + 1) * stretch] = delta[:, half]
            do_s[g, at : at + stretch, :] = do[half]
    strip = grads.shape[0]
    mine = span(meta[1], strip)
    grads[:, width : 2 * width] = dot(att_t.get()[mine, :].astype(BF), branch)
    lse, q_ref, angle = lse.get(), q_in.get(), angle.get()
    for g in range(KV_HEADS):
        for sel in range(2):
            do_s[g, 2 * sel * wide : (2 * sel + 1) * wide, :] = q_ref[g, sel * wide : (sel + 1) * wide, :]
    for copy in kv_copies:
        copy.wait()
    first, inner = first.get(), inner.get()
    chunk = 4
    low_chunks = lax.shift_right_logical(c, 2)
    key_ids = lax.broadcasted_iota(jnp.int32, (chunk * stretch, wide), 0)
    query_ids = lax.broadcasted_iota(jnp.int32, (chunk * stretch, wide), 1)
    query_ids = lax.bitwise_and(query_ids, stretch - 1)
    pre = kv
    lane_ids = lax.broadcasted_iota(jnp.int32, (stretch, PAIR), 1)

    def one_head(g):
        lanes = span(g, PAIR)
        dkv[n * stretch :, :] = jnp.zeros((n * stretch, PAIR), F32)
        dq_s[...] = jnp.zeros(dq_s.shape, F32)

        def low_step(i):
            at = span(i, low_group * stretch)
            keys = kv[at, lanes]
            both = do_s[g, 2 * wide :, :]
            s = dot_nt(keys, both)
            p = jnp.exp(s[:, :wide] - lse[2 * g + 1])
            ds = (p * (s[:, wide:] - dl_s[2 * g + 1])).astype(BF)
            dkv[at, :] = dot(jnp.concatenate([ds, p.astype(BF)], axis=1), both)
            dq_s[1] += dot_tn(keys, ds)

        loop(low_steps, low_step)

        def unit_step(u):
            is_low = u <= low_chunks
            sel = jnp.where(is_low, 0, 1)
            low_key = jnp.where(is_low, u, u - low_chunks - 1 + n // chunk) * (chunk * stretch)
            at = pl.ds(pl.multiple_of(low_key, chunk * stretch), chunk * stretch)
            keys = kv[at, lanes]
            both = do_s[g, span(sel, 2 * wide), :]
            s = dot_nt(keys, both)
            p = jnp.exp(s[:, :wide] - lse[2 * g + sel])
            ahead = low_key - jnp.where(is_low, c, 2 * n - 1 - c) * stretch
            p = jnp.where(key_ids + ahead <= query_ids, p, 0.0)
            ds = (p * (s[:, wide:] - dl_s[2 * g + sel])).astype(BF)
            dkv[at, :] += dot(jnp.concatenate([ds, p.astype(BF)], axis=1), both)
            dq_s[sel] += dot_tn(keys, ds)

        if n <= 8:
            for u in range(n // chunk + 1):
                unit_step(u)
        else:
            loop(n // chunk + 1, unit_step)

        def turn(i):
            ct, st = inner[0], inner[1]
            cs, ss = first[i, 0:1, :], first[i, 1:2, :]
            part = dkv[span(i, stretch), :]
            back = pltpu.roll(part, PAIR - HALF, 1)
            ahead = pltpu.roll(part, HALF, 1)
            swapped = jnp.where(lane_ids < HALF, back, ahead)
            result = part * (ct * cs - st * ss) + swapped * (st * cs + ct * ss)
            pre[span(i, stretch), lanes] = result.astype(BF)

        if n <= 8:
            for i in range(2 * n):
                turn(i)
        else:
            loop(2 * n, turn)
        for sel in range(2):
            half = slice(sel * stretch, (sel + 1) * stretch)
            cos, sin = angle[:HALF, half], angle[HALF:, half]
            for hh in range(GROUP):
                dq = dq_s[sel, :HEAD, hh * stretch : (hh + 1) * stretch] * HEAD**-0.5
                a, b = dq[:HALF], dq[HALF:]
                turned = jnp.concatenate([a * cos + b * sin, b * cos - a * sin], axis=0)
                dq_t[span(g * GROUP + hh, HEAD), half] = turned

    loop(KV_HEADS, one_head)
    dq = dq_t[...].T.astype(BF)
    gn_s[:, :width] = dq.astype(F32)
    dq_out.ref[...] = gn_s[span(meta[1], piece), :].astype(BF)
    dq_out.send()
    grads[:, :width] = dot(normed.get()[...], dq)
    for copy in strip_copies:
        copy.wait()
    grads[:, 2 * width :] = dot(all_s[...], pre[...])
    wk, wv = wk.get()[...].astype(F32), wv.get()[...].astype(F32)
    chunks = []
    for g in range(KV_HEADS):
        chunks += [wk[g * HEAD : (g + 1) * HEAD], wv[g * HEAD : (g + 1) * HEAD]]
    w_s[...] = jnp.concatenate(chunks, axis=0).T
    sums = jnp.sum(grads[:, :width] * wq.get()[mine, :].astype(F32), axis=1, keepdims=True)
    sums = sums + jnp.sum(grads[:, 2 * width :] * w_s[mine, :], axis=1, keepdims=True)
    norm_s[0:1, :strip] = jnp.broadcast_to(sums, (strip, 128)).T[0:1, :]
    quarter = meta[1] * piece
    upper = quarter >= stretch
    inside = jnp.where(upper, quarter - stretch, quarter)

    def rows_for(who):
        low = order[0, 2 * who]
        st = jnp.where(upper, 2 * n - 1 - low, low)
        return pre[pl.ds(pl.multiple_of(st * stretch + inside, piece), piece), :]

    if n > 8:
        even[...] = grads[...].astype(BF)
        odd[...] = norm_s[...].astype(BF)
        for k in range(n):
            outs[4][k] = rows_for(k)
        return
    for k in range(n):
        who = lax.bitwise_xor(me, k)
        to = even if k % 2 == 0 else odd
        to[k // 2, :piece, :] = rows_for(who)
        block = grads[block_rows(strip, who), block_lanes(who)]
        cut = norm_s[:, span(who, 128)]
        tail = jnp.concatenate([cut, jnp.zeros((8, block.shape[1] - 128), F32)], axis=1)
        to[k // 2, piece:, :] = jnp.concatenate([block, tail], axis=0).astype(BF)


def block_rows(strip, who):
    size = strip // 2
    return pl.ds(pl.multiple_of(lax.shift_right_logical(who, 2) * size, size), size)


def block_lanes(who):
    return span(lax.bitwise_and(who, 3), KV_HEADS * PAIR)


def finish_body(count, ins, outs, scratch):
    terms = ins[:count]
    meta, gain, tok, gm, dq, wq, wk, wv = ins[count:]
    (gt_out,) = outs
    (x_s,) = scratch
    piece = gt_out.shape[0]
    total = terms[0][:piece, :].astype(F32)
    for term in terms[1:]:
        total = total + term[:piece, :].astype(F32)
    mine = span(meta[1], piece)
    x_s[...] = tok.get()[...].astype(F32).T
    x = x_s[mine, :]
    dk, dv = [], []
    for g in range(KV_HEADS):
        dk.append(total[:, g * PAIR : g * PAIR + HEAD])
        dv.append(total[:, g * PAIR + HEAD : (g + 1) * PAIR])
    dk = jnp.concatenate(dk, axis=1).astype(BF)
    dv = jnp.concatenate(dv, axis=1).astype(BF)
    width = gain.shape[0]
    gn = dot_nt(dq[:, :width], wq.get()[...])
    gn = gn + dot(dk, wk.get()[...]) + dot(dv, wv.get()[...])
    r = norm_scale(x, -1)
    xn = x * r
    e = gn * row_of(gain)
    result = gm[:, :width] + r * (e - xn * jnp.mean(e * xn, axis=-1, keepdims=True))
    gt_out[:, :width] = result.astype(BF)
    gt_out[:, width:] = jnp.zeros((piece, gt_out.shape[1] - width), BF)


def token_join_body(wt, ins, outs, scratch):
    meta = ins[0]
    (rows_s,) = scratch
    for i in range(2):
        quarters = ins[1 + i * wt : 1 + (i + 1) * wt]
        for k in range(wt):
            at = span(lax.bitwise_xor(meta[1], k), quarters[0].shape[0])
            rows_s[at, :] = quarters[k][:, : rows_s.shape[1]].astype(F32)
        outs[i][...] = rows_s[...].T.astype(outs[i].dtype)


def mlp_join_body(n, ins, outs, scratch):
    meta, blocks = ins[0], ins[1:]
    (grads,) = scratch
    if n > 8:
        grads[...] = blocks[0][...].astype(F32)
    else:
        size = grads.shape[0] // n
        for k in range(n):
            block = blocks[k // 2][...] if k % 2 == 0 else blocks[-1][k // 2]
            grads[span(lax.bitwise_xor(meta[0], k), size), :] = block.astype(F32)
    width = outs[0].shape[1]
    for i in range(3):
        outs[i][...] = grads[:, i * width : (i + 1) * width]


def join_body(n, wt, ins, outs, scratch):
    meta, gain = ins[:2]
    blocks = ins[2:]
    gq, go, gk, gv, norm_attn, norm_mlp = outs
    grads, norm_s = scratch
    width = gq.shape[0]
    strip = width // wt
    norm_s[...] = jnp.zeros(norm_s.shape, F32)
    if n > 8:
        grads[...] = blocks[0][...].astype(F32)
        norm_s[...] = blocks[1][...].astype(F32)
    else:
        size = strip // 2
        for k in range(n):
            who = lax.bitwise_xor(meta[0], k)
            for kz in range(wt):
                lane = lax.bitwise_xor(meta[1], kz)
                block = blocks[k // 2][kz] if k % 2 == 0 else blocks[-1][k // 2, kz]
                block = block.astype(F32)
                at = lane * strip + lax.shift_right_logical(who, 2) * size
                grads[pl.ds(pl.multiple_of(at, size), size), block_lanes(who)] = block[:size]
                norm_s[lane, :, span(who, 128)] = block[size:, :128]
    gq[...] = grads[:, :width]
    go[...] = grads[:, width : 2 * width]
    both = grads[:, 2 * width :].T
    for g in range(KV_HEADS):
        gk[g * HEAD : (g + 1) * HEAD, :] = both[g * PAIR : g * PAIR + HEAD]
        gv[g * HEAD : (g + 1) * HEAD, :] = both[g * PAIR + HEAD : (g + 1) * PAIR]
    attn = jnp.concatenate([norm_s[lane, 0:1, :strip] for lane in range(wt)], axis=1)
    norm_attn[...] = (attn / row_of(gain)).reshape(width)
    norm_mlp[...] = norm_s[0, 1:2, :width].reshape(width)


def hop(x, axis, size, k):
    return lax.ppermute(x, axis, [(i, i ^ k) for i in range(size)])


def gather_blocks(x, axis, size):
    evens = [x] + [hop(x, axis, size, k) for k in range(2, size, 2)]
    odds = hop(jnp.stack(evens), axis, size, 1)
    return evens, odds


def pair_terms(even, odd, axis, size):
    got = hop(odd, axis, size, 1).astype(F32)
    pairs = [even[i].astype(F32) + got[i] for i in range(size // 2)]
    return pairs[:1] + [pair.astype(BF) for pair in pairs[1:]]


def scatter_terms(pairs, axis, size):
    return pairs[:1] + [hop(pairs[i], axis, size, 2 * i) for i in range(1, size // 2)]


def summed(terms):
    total = terms[0].astype(F32)
    for term in terms[1:]:
        total = total + term.astype(F32)
    return total


def after(dep, *arrays):
    held = lax.optimization_barrier((dep,) + arrays)
    return list(held[1:]) if len(arrays) > 1 else held[1]


def local(
    n,
    wt,
    tokens,
    w_query,
    w_key,
    w_value,
    w_out,
    norm_attn,
    norm_mlp,
    w_gate,
    w_up,
    w_down,
    stretch_order,
    cotangent,
):
    rows, width = tokens.shape
    stretch = rows // 2
    wide = GROUP * stretch
    kv_width = KV_HEADS * PAIR
    hidden_width = w_gate.shape[1]
    piece = rows // wt
    size = width // n
    strip = width // wt
    small = n <= 8
    padded = -(-width // 128) * 128
    turned, first, inner = (jnp.asarray(t) for t in angle_tables(n, stretch))
    tok, cot, wk, wv, w_down = tokens.T, cotangent.T, w_key.T, w_value.T, w_down.T

    normed, kv, angle = call(
        key_body,
        [None, stretch_order, norm_attn, tok, wk, wv, turned],
        "mscccch",
        [shape((width, rows), BF), shape((rows, kv_width), BF), shape((HEAD, rows), F32)],
        "vvv",
        scratch=[
            pltpu.VMEM((2, HEAD, stretch), F32),
            pltpu.SemaphoreType.DMA((2,)),
        ],
        early=key_early,
    )
    q, normed_q = call(
        query_body,
        [None, normed, w_query, angle],
        "mvcv",
        [shape((KV_HEADS, 2 * wide, PAIR), BF), shape((strip, rows), BF)],
        "cv",
        scratch=[pltpu.VMEM((width, rows), F32)],
    )
    evens = [kv] + [hop(kv, "ctx", n, k) for k in range(2, n, 2)]
    strips = [normed_q] + [hop(normed_q, "ctx", n, k) for k in range(2, n, 2)]
    odds = hop(jnp.stack(after(q, *evens)), "ctx", n, 1)

    mlp_columns = 3 * hidden_width
    if small:
        block_shapes = [shape((n // 2, size, mlp_columns), BF)] * 2
    else:
        block_shapes = [shape((width, mlp_columns), BF), shape((8, 128), BF)]
    results = call(
        functools.partial(forward_body, n, wt),
        [*evens, odds, None, stretch_order, q, tok, w_out, norm_mlp, w_gate, w_up, cot, w_down],
        "h" * (n // 2 + 1) + "msccc" + "c" + "cccc",
        [
            shape((width, rows), F32),
            shape((2 * KV_HEADS, 1, wide), F32),
            shape((rows, padded), F32),
        ]
        + block_shapes
        + [shape((piece, padded), F32)]
        + [shape((piece, padded), BF)] * (2 * wt),
        "ccc" + "ccc" + "c" * (2 * wt),
        scratch=[
            pltpu.VMEM((n * rows, kv_width), BF),
            pltpu.VMEM((2 * KV_HEADS, 1, wide), F32),
            pltpu.VMEM((2 * KV_HEADS, 1, wide), F32),
            pltpu.VMEM((2 * KV_HEADS, PAIR, wide), F32),
            pltpu.VMEM((rows, padded), F32),
            pltpu.VMEM((width, mlp_columns), F32),
            pltpu.SemaphoreType.DMA((2 * n,)),
        ],
        early=functools.partial(forward_early, n),
        micros=14,
    )
    att_t, lse, mixed, even, odd, mixed_q, *pieces = after(strips, *results)
    part_in, out_parts = pieces[:wt], pieces[wt:]
    strip_odds = hop(jnp.stack(strips), "ctx", n, 1)

    terms = [part_in[0]] + [hop(part_in[k], "wt", wt, k) for k in range(1, wt)]
    quarter = summed(terms).astype(BF)
    quarters = [quarter] + [hop(quarter, "wt", wt, k) for k in range(1, wt)]

    if small:
        pairs = pair_terms(even, odd, "ctx", n)
        quarters = after(pairs[0], *quarters)
        mlp_own = summed(scatter_terms(pairs, "ctx", n)).astype(BF)
    else:
        mlp_blocks = [lax.psum(even, "ctx")]

    columns = 2 * width + kv_width
    if small:
        out_blocks = [shape((n // 2, piece + strip // 2 + 8, kv_width), BF)] * 2
    else:
        out_blocks = [
            shape((strip, columns), BF),
            shape((8, 128 * n), BF),
            shape((n, piece, kv_width), BF),
        ]
    gm_q, dq_q, *message = call(
        functools.partial(backward_body, n, wt),
        [*quarters, None, stretch_order, norm_mlp, mixed, cot, w_out, att_t, lse, q, angle]
        + [first, inner, normed_q, w_query, wk, wv, *evens, odds, *strips, strip_odds],
        "c" * wt + "msc" + "c" * 7 + "c" * 6 + "h" * (n + 2),
        [shape((piece, padded), F32), shape((piece, padded), BF)] + out_blocks,
        "cc" + "v" * len(out_blocks),
        scratch=[
            pltpu.VMEM((rows, padded), F32),
            pltpu.VMEM((KV_HEADS, 4 * wide, PAIR), BF),
            pltpu.VMEM((2 * KV_HEADS, 1, wide), F32),
            pltpu.VMEM((n * rows, PAIR), F32),
            pltpu.VMEM((2, PAIR, wide), F32),
            pltpu.VMEM((width, rows), F32),
            pltpu.VMEM((strip, columns), F32),
            pltpu.VMEM((8, max(128 * n, 640)), F32),
            pltpu.VMEM((strip, n * rows), BF),
            pltpu.VMEM((width, kv_width), F32),
            pltpu.VMEM((n * rows, kv_width), BF),
            pltpu.SemaphoreType.DMA((2 * n,)),
            pltpu.SemaphoreType.DMA((2 * n,)),
        ],
        early=functools.partial(backward_early, n, wt),
        early_at=wt + 10,
        micros=17,
    )
    out_parts = after(mlp_own, *out_parts) if small else out_parts
    out_terms = [out_parts[0]] + [hop(out_parts[k], "wt", wt, k) for k in range(1, wt)]
    out_q = (mixed_q + summed(out_terms)).astype(BF)
    out_qs = [out_q] + [hop(out_q, "wt", wt, k) for k in range(1, wt)]
    if small:
        mlp_evens, mlp_odds = gather_blocks(mlp_own, "ctx", n)
        mlp_blocks = [*mlp_evens, mlp_odds]
        message[1] = after((mlp_evens, out_terms), message[1])
        parts = scatter_terms(pair_terms(message[0], message[1], "ctx", n), "ctx", n)
        parts = after(out_qs, *parts)
        own = summed([part[piece:] for part in parts]).astype(BF)
        owns = [own] + [hop(own, "wt", wt, k) for k in range(1, wt)]
    else:
        parts = [lax.psum_scatter(message[2].astype(F32), "ctx", scatter_dimension=0)]
        last_blocks = list(lax.psum((message[0], message[1]), "ctx"))
        last_blocks = [lax.all_gather(b, "wt", axis=0, tiled=i == 0) for i, b in enumerate(last_blocks)]
    (gt,) = call(
        functools.partial(finish_body, len(parts)),
        [*parts, None, norm_attn, tok, gm_q, dq_q, w_query, wk, wv],
        "v" * len(parts) + "mvcvvccc",
        [shape((piece, padded), BF)],
        "v",
        scratch=[pltpu.VMEM((rows, width), F32)],
        vmem=16,
        micros=2,
    )
    gts = [gt] + [hop(gt, "wt", wt, k) for k in range(1, wt)]
    grad_gate, grad_up, grad_down = call(
        functools.partial(mlp_join_body, n),
        [None, *mlp_blocks],
        "m" + "v" * len(mlp_blocks),
        [shape((width, hidden_width), F32)] * 3,
        "vvv",
        scratch=[pltpu.VMEM((width, mlp_columns), F32)],
        vmem=24,
        micros=2,
    )
    grad_tokens, output = call(
        functools.partial(token_join_body, wt),
        [None, *gts, *out_qs],
        "m" + "v" * (2 * wt),
        [shape((width, rows), F32), shape((width, rows), BF)],
        "vv",
        scratch=[pltpu.VMEM((rows, width), F32)],
        vmem=24,
        micros=2,
    )
    if small:
        last = jnp.stack(after(gt, *owns))
        last_evens = [last] + [hop(last, "ctx", n, k) for k in range(2, n, 2)]
        last = hop(after((grad_gate, gts), jnp.stack(last_evens)), "ctx", n, 1)
        last_blocks = [*last_evens, after(grad_tokens, last)]
    grad_query, grad_out, grad_key, grad_value, grad_norm_attn, grad_norm_mlp = call(
        functools.partial(join_body, n, wt),
        [None, norm_attn, *last_blocks],
        "mv" + "v" * len(last_blocks),
        [shape((width, width), F32)] * 2
        + [shape((kv_width // 2, width), F32)] * 2
        + [shape((width,), F32)] * 2,
        "vvvvvv",
        scratch=[
            pltpu.VMEM((width, columns), F32),
            pltpu.VMEM((wt, 8, max(128 * n, 640)), F32),
        ],
        vmem=24,
    )
    return (
        output.T,
        grad_tokens.T,
        grad_query,
        grad_key.T,
        grad_value.T,
        grad_out,
        grad_norm_attn,
        grad_norm_mlp,
        grad_gate,
        grad_up,
        grad_down.T,
    )


def solution(mesh):
    return jax.shard_map(
        functools.partial(local, mesh.shape["ctx"], mesh.shape["wt"]),
        mesh=mesh,
        in_specs=(
            P("ctx", None),
            P(),
            P(),
            P(),
            P(),
            P(),
            P(),
            P(None, "wt"),
            P(None, "wt"),
            P("wt", None),
            P(),
            P("ctx", None),
        ),
        out_specs=(
            P("ctx", None),
            P("ctx", None),
            P(),
            P(),
            P(),
            P(),
            P(),
            P(),
            P(None, "wt"),
            P(None, "wt"),
            P("wt", None),
        ),
        check_vma=False,
    )
```
